32 devices in a mesh: ctx: 8 (over z, x), fsdp: 4 (over y, core).
Axes of the slice: x: 2, y: 2, z: 4, core: 2. Of those that a mesh axis runs over, the one named last changes fastest.
Arguments:
- inputs: bfloat16 [4, 2048, 2048], P('fsdp', 'ctx'), may hold values from -6 to 6
- norm_gain: float32 [2048], replicated, may hold values from 0.1 to 1.9
- norm_shift: float32 [2048], replicated, may hold values from -2 to 2
- qkv_weight: bfloat16 [2048, 6144], P('fsdp'), may hold values from -0.125 to 0.125
- qkv_bias: float32 [6144], replicated, may hold values from -2 to 2
- out_weight: bfloat16 [2048, 2048], P('fsdp'), may hold values from -0.25 to 0.25
- out_bias: float32 [2048], replicated, may hold values from -2 to 2
- up_weight: bfloat16 [2048, 8192], P('fsdp'), may hold values from -0.125 to 0.125
- up_bias: float32 [8192], replicated, may hold values from -2 to 2
- down_weight: bfloat16 [8192, 2048], P('fsdp'), may hold values from -0.0625 to 0.0625
- down_bias: float32 [2048], replicated, may hold values from -2 to 2
- cotangent: bfloat16 [4, 2048, 2048], P('fsdp', 'ctx'), may hold values from -6 to 6
Outputs:
- output: bfloat16 [4, 2048, 2048], P('fsdp', 'ctx')
- input_grad: bfloat16 [4, 2048, 2048], P('fsdp', 'ctx')
- gain_grad: float32 [2048], replicated
- shift_grad: float32 [2048], replicated
- qkv_weight_grad: float32 [2048, 6144], P(('fsdp', 'ctx'))
- qkv_bias_grad: float32 [6144], replicated
- out_weight_grad: float32 [2048, 2048], P(('fsdp', 'ctx'))
- out_bias_grad: float32 [2048], replicated
- up_weight_grad: float32 [2048, 8192], P(('fsdp', 'ctx'))
- up_bias_grad: float32 [8192], replicated
- down_weight_grad: float32 [8192, 2048], P(('fsdp', 'ctx'))
- down_bias_grad: float32 [2048], replicated
The draws below stay inside these ranges and needn't reach their ends.
All inputs are finite; a program needn't handle non-finite values.
Results may differ from the reference program's by a relative error of at most 0.012.
Values may be sent and summed in bfloat16 or wider, within the bound.
A program may use at most 704 MiB of HBM per device.

```python
import math
import jax
import jax.numpy as jnp
from jax import lax

D = 2048
NH = 32
HD = 64
FF = 8192
ROT = 32
TOK_DEV = 256
SEQ = 2048
SEQS = 4
N_CTX = 8


def steps_of(stream_key, extent, cuts, least, high):
    level, own = 1.0, jax.random.fold_in(stream_key, 6)
    for axis_at, blocks in cuts:
        draws = jnp.exp(jax.random.uniform(jax.random.fold_in(own, axis_at), (blocks,), jnp.float32, least / len(cuts), high / len(cuts)))
        level = level * jnp.repeat(draws, extent[axis_at] // blocks).reshape([-1 if axis == axis_at else 1 for axis in range(len(extent))])
    return level


def normal_values(own_key, dims, deviation, most, pieces=(), held_as=jnp.bfloat16):
    array = jax.random.normal(own_key, dims, jnp.float32) * deviation
    if len(pieces) > 0:
        array = steps_of(own_key, dims, pieces, -0.22, 0.18) * array
    return jnp.clip(array, min=-most, max=most).astype(held_as)


def setup_inputs(seed: int = 0) -> dict:
    key_list = jax.random.split(jax.random.key(seed), 13)
    return {
        "inputs": normal_values(key_list[0], (SEQS, SEQ, D), 1.0, 6.0, ((0, 4), (1, 8))),
        "norm_gain": jnp.clip(1.0 + 0.18 * jax.random.normal(key_list[1], (D,), jnp.float32), 0.1, 1.9),
        "norm_shift": normal_values(key_list[2], (D,), 0.3, 2.0, (), jnp.float32),
        "qkv_weight": normal_values(key_list[3], (D, 3 * D), D ** -0.5, 0.125, ((0, 4),)),
        "qkv_bias": normal_values(key_list[4], (3 * D,), 0.3, 2.0, (), jnp.float32),
        "out_weight": normal_values(key_list[5], (D, D), (D // 4) ** -0.5, 0.25, ((0, 4),)),
        "out_bias": normal_values(key_list[6], (D,), 0.3, 2.0, (), jnp.float32),
        "up_weight": normal_values(key_list[7], (D, FF), D ** -0.5, 0.125, ((0, 4),)),
        "up_bias": normal_values(key_list[8], (FF,), 0.3, 2.0, (), jnp.float32),
        "down_weight": normal_values(key_list[9], (FF, D), FF ** -0.5, 0.0625, ((0, 4),)),
        "down_bias": normal_values(key_list[10], (D,), 0.3, 2.0, (), jnp.float32),
        "cotangent": normal_values(key_list[11], (SEQS, SEQ, D), 1.0, 6.0, ((0, 4), (1, 8))),
    }


@jax.custom_vjp
def low(v):
    return lax.optimization_barrier(v.astype(jnp.bfloat16)).astype(jnp.float32)

@jax.custom_vjp
def low_back(v):
    return v

def low_keep(v):
    return (low(v), None)

def low_pass(kept, grad):
    return (grad,)

def back_keep(v):
    return (v, None)

def back_low(kept, grad):
    return (low(grad),)
low.defvjp(low_keep, low_pass)
low_back.defvjp(back_keep, back_low)
EPS = 1e-05
HIGH = lax.Precision.HIGHEST
ROOT = 0.7978845608028654
CUBIC = 0.044715

def matmul(left, right):
    return jnp.dot(left, right, precision=HIGH, preferred_element_type=jnp.float32)

def row_positions(length):
    rows = jnp.arange(length, dtype=jnp.int32)
    half = TOK_DEV // 2
    shard = rows // TOK_DEV
    within = rows % TOK_DEV
    block = jnp.where(within < half, shard, 2 * N_CTX - 1 - shard)
    return (block * half + within % half).astype(jnp.int32)

def rotate(heads, positions):
    quarter = ROT // 2
    inverse = 10000.0 ** (-jnp.arange(quarter, dtype=jnp.float32) * 2.0 / ROT)
    angle = positions.astype(jnp.float32)[:, None] * inverse[None, :]
    cosine = jnp.cos(angle)[:, None, :]
    sine = jnp.sin(angle)[:, None, :]
    first = heads[..., :quarter]
    second = heads[..., quarter:ROT]
    return jnp.concatenate([first * cosine - second * sine, second * cosine + first * sine, heads[..., ROT:]], axis=-1)

def gelu(value):
    return 0.5 * value * (1.0 + jnp.tanh(ROOT * (value + CUBIC * value * value * value)))

def forward(inputs, norm_gain, norm_shift, qkv_weight, qkv_bias, out_weight, out_bias, up_weight, up_bias, down_weight, down_bias):
    seqs, length, width = inputs.shape
    mean = lax.optimization_barrier(jnp.mean(inputs, axis=-1, keepdims=True))
    centred = inputs - mean
    variance = lax.optimization_barrier(jnp.mean(centred * centred, axis=-1, keepdims=True))
    normed = centred * lax.rsqrt(variance + EPS) * norm_gain + norm_shift
    flat = low(normed.reshape(seqs * length, width))
    qkv = low_back(matmul(flat, qkv_weight) + qkv_bias)
    positions = row_positions(length)
    split = qkv.reshape(seqs, length, 3, NH, HD)
    queries = low(rotate(split[:, :, 0], positions))
    keys = low(rotate(split[:, :, 1], positions))
    values = low(split[:, :, 2])
    block = math.gcd(512, length)
    count = length // block
    query_blocks = queries.reshape(seqs * count, block, NH, HD)
    position_blocks = jnp.tile(positions.reshape(count, block), (seqs, 1))
    owners = jnp.repeat(jnp.arange(seqs, dtype=jnp.int32), count)
    scale = 1.0 / math.sqrt(HD)

    def one_block(items):
        query, query_pos, owner = items
        key_seq = lax.dynamic_index_in_dim(keys, owner, 0, keepdims=False)
        value_seq = lax.dynamic_index_in_dim(values, owner, 0, keepdims=False)
        scores = low_back(jnp.einsum('qhd,khd->hqk', query, key_seq, precision=HIGH) * scale)
        allowed = positions[None, :] <= query_pos[:, None]
        scores = jnp.where(allowed[None], scores, -1e+30)
        top = lax.optimization_barrier(jnp.max(scores, axis=-1, keepdims=True))
        weights = jnp.exp(scores - top)
        probs = low(weights / lax.optimization_barrier(jnp.sum(weights, axis=-1, keepdims=True)))
        return jnp.einsum('hqk,khd->qhd', probs, value_seq, precision=HIGH)
    mixed = lax.map(jax.checkpoint(one_block), (query_blocks, position_blocks, owners))
    attended = low(low_back(mixed.reshape(seqs * length, width)))
    branch = matmul(attended, out_weight) + out_bias
    up = low_back(matmul(flat, up_weight) + up_bias)
    hidden = low(gelu(up))
    result = inputs.reshape(seqs * length, width) + branch + matmul(hidden, down_weight) + down_bias
    return result.reshape(seqs, length, width)

def reference(inputs, norm_gain, norm_shift, qkv_weight, qkv_bias, out_weight, out_bias, up_weight, up_bias, down_weight, down_bias, cotangent):
    params = tuple((item.astype(jnp.float32) for item in (inputs, norm_gain, norm_shift, qkv_weight, qkv_bias, out_weight, out_bias, up_weight, up_bias, down_weight, down_bias)))
    result, pullback = jax.vjp(forward, *params)
    grads = pullback(cotangent.astype(jnp.float32))
    return (result.astype(jnp.bfloat16), grads[0].astype(jnp.bfloat16), grads[1], grads[2], grads[3], grads[4], grads[5], grads[6], grads[7], grads[8], grads[9], grads[10])
```

```python
from functools import partial

import jax
import jax.numpy as jnp
from jax import lax
from jax.experimental import pallas as pl
from jax.experimental.pallas import tpu as pltpu
from jax.sharding import PartitionSpec as P

HD = 64
ROT = 32
LANES = 128

EPS = 1e-05
ROOT = 0.7978845608028654
CUBIC = 0.044715
F32 = jnp.float32
BF16 = jnp.bfloat16


def gelu_value(value):
    return 0.5 * value * (1.0 + jnp.tanh(ROOT * (value + CUBIC * value * value * value)))


def gelu_slope(value):
    tangent = jnp.tanh(ROOT * (value + CUBIC * value * value * value))
    return 0.5 * (1.0 + tangent) + 0.5 * value * (1.0 - tangent * tangent) * ROOT * (
        1.0 + 3.0 * CUBIC * value * value
    )


def contract_rows(left, right):
    return lax.dot_general(left, right, (((0,), (0,)), ((), ())), preferred_element_type=F32)


def contract_cols(left, right):
    return lax.dot_general(left, right, (((1,), (1,)), ((), ())), preferred_element_type=F32)


def matmul(left, right):
    return jnp.dot(left, right, preferred_element_type=F32)


def swap(value, axis, bit):
    size = lax.axis_size(axis)
    return lax.ppermute(value, axis, [(i, i ^ bit) for i in range(size)])


def rotary(positions):
    quarter = ROT // 2
    inverse = 10000.0 ** (-jnp.arange(quarter, dtype=F32) * 2.0 / ROT)
    angle = positions.astype(F32)[:, None] * inverse[None, :]
    cosine, sine = jnp.cos(angle), jnp.sin(angle)
    rest = positions.shape[0], HD - ROT
    one = jnp.concatenate([cosine, cosine, jnp.ones(rest, F32)], axis=1)
    two = jnp.concatenate([-sine, sine, jnp.zeros(rest, F32)], axis=1)
    return jnp.tile(one, (1, LANES // HD)), jnp.tile(two, (1, LANES // HD))


def turn(rows, cosine, sine):
    lane = lax.broadcasted_iota(jnp.int32, rows.shape, 1) % HD
    quarter = ROT // 2
    other = jnp.where(
        lane < quarter,
        pltpu.roll(rows, LANES - quarter, 1),
        pltpu.roll(rows, quarter, 1),
    )
    return rows * cosine + other * sine


def qkv_kernel(pieces, rows_ref, *refs):
    weights = refs[:pieces]
    bias_ref, cos_ref, sin_ref, out_ref = refs[pieces:]
    part = pl.program_id(0)
    depth = weights[0].shape[0]
    acc = bias_ref[0]
    for j in range(pieces):
        acc = acc + jnp.dot(
            rows_ref[:, j * depth : (j + 1) * depth],
            weights[j][...],
            preferred_element_type=F32,
        )
    cosine, sine = cos_ref[...], sin_ref[...]
    for h in range(out_ref.shape[0]):
        cols = acc[:, h * LANES : (h + 1) * LANES]
        turned = turn(cols, cosine, sine)
        out_ref[h, 0, 0, 0] = jnp.where(part < 2, turned, cols).astype(out_ref.dtype)


def project(rows, weights, bias, cosine, sine, groups, per_group):
    tokens = cosine.shape[0]
    slots = rows.shape[0] // tokens
    width = rows.shape[1]
    part_cols = bias.shape[1]
    pairs = part_cols // LANES
    pieces = len(weights)
    depth = width // pieces
    return pl.pallas_call(
        partial(qkv_kernel, pieces),
        grid=(3, slots),
        out_shape=jax.ShapeDtypeStruct((pairs, groups, per_group, 3, tokens, LANES), BF16),
        in_specs=[pl.BlockSpec((tokens, width), lambda p, s: (s, 0))]
        + [pl.BlockSpec((depth, part_cols), lambda p, s: (0, p))] * pieces
        + [
            pl.BlockSpec((1, 1, part_cols), lambda p, s: (p, 0, 0)),
            pl.BlockSpec((tokens, LANES), lambda p, s: (0, 0)),
            pl.BlockSpec((tokens, LANES), lambda p, s: (0, 0)),
        ],
        out_specs=pl.BlockSpec(
            (pairs, 1, 1, 1, tokens, LANES),
            lambda p, s: (0, s // per_group, s % per_group, p, 0, 0),
        ),
        compiler_params=pltpu.CompilerParams(vmem_limit_bytes=40 * 2**20),
        cost_estimate=pl.CostEstimate(
            flops=2 * rows.shape[0] * width * part_cols * 3,
            bytes_accessed=30 * 2**20,
            transcendentals=0,
        ),
    )(rows, *weights, bias.reshape(3, 1, part_cols), cosine, sine)


def attend_kernel(
    shards, heads, dup, qkv_ref, do_ref, cos_ref, sin_ref, out_ref, s_buf, dp_buf, dk_buf, dv_buf
):
    half = qkv_ref.shape[-2]
    block = 2 * half
    count = shards
    base = lax.axis_index("ctx") % dup
    lane = lax.broadcasted_iota(jnp.int32, (block, LANES), 1) // HD
    own = [lane == (base + h) for h in range(heads)]
    scale = HD**-0.5

    def where_is(item):
        low = item < count // 2
        first = jnp.where(low, 2 * item, 2 * count - 1 - 2 * item)
        second = jnp.where(low, 2 * item + 1, 2 * count - 2 - 2 * item)
        return first, second, jnp.where(low, 0, 1)

    def load(part, item):
        first, second, side = where_is(item)
        return jnp.concatenate(
            [qkv_ref[first, 0, part, side], qkv_ref[second, 0, part, side]], axis=0
        )

    def load_do(item):
        first, second, side = where_is(item)
        return jnp.concatenate([do_ref[first, 0, side], do_ref[second, 0, side]], axis=0)

    def store(part, item, value):
        first, second, side = where_is(item)
        out_ref[first, 0, part, side] = value[:half].astype(out_ref.dtype)
        out_ref[second, 0, part, side] = value[half:].astype(out_ref.dtype)

    dk_buf[...] = jnp.zeros_like(dk_buf)
    dv_buf[...] = jnp.zeros_like(dv_buf)
    nothing = jnp.zeros((block, LANES), BF16)
    key_at = lax.broadcasted_iota(jnp.int32, (block, block), 0)
    query_at = lax.broadcasted_iota(jnp.int32, (block, block), 1)

    def per_query(item, _):
        query = load(0, item) * jnp.asarray(scale, BF16)
        grad = load_do(item)
        queries = [jnp.where(own[h], query, nothing) for h in range(heads)]
        grads = [jnp.where(own[h], grad, nothing) for h in range(heads)]

        def measure(key_item, state, diagonal):
            keys, values = load(1, key_item), load(2, key_item)
            new = []
            for h in range(heads):
                top, total, dot = state[h]
                s = contract_cols(keys, queries[h])
                if diagonal:
                    s = jnp.where(key_at <= query_at, s, -1e30)
                dp = contract_cols(values, grads[h])
                s_buf[h, key_item] = s
                dp_buf[h, key_item] = dp
                new_top = jnp.maximum(top, jnp.max(s, axis=0, keepdims=True))
                e = jnp.exp(s - new_top)
                fade = jnp.exp(top - new_top)
                new.append(
                    (
                        new_top,
                        total * fade + jnp.sum(e, axis=0, keepdims=True),
                        dot * fade + jnp.sum(e * dp, axis=0, keepdims=True),
                    )
                )
            return tuple(new)

        zero = jnp.zeros((1, block), F32)
        start = tuple((zero - 1e30, zero, zero) for _ in range(heads))
        state = lax.fori_loop(0, item, lambda k, st: measure(k, st, False), start)
        state = measure(item, state, True)
        logs = [top + jnp.log(total) for top, total, _ in state]
        deltas = [dot / total for _, total, dot in state]

        def apply(key_item, state):
            keys, values = load(1, key_item), load(2, key_item)
            out, dq = state
            dk, dv = dk_buf[key_item], dv_buf[key_item]
            for h in range(heads):
                p = jnp.exp(s_buf[h, key_item] - logs[h])
                ds = (p * (dp_buf[h, key_item] - deltas[h])).astype(BF16)
                p = p.astype(BF16)
                dv = dv + matmul(p, grads[h])
                dk = dk + matmul(ds, queries[h])
                out = out + jnp.where(own[h], contract_rows(p, values), 0.0)
                dq = dq + jnp.where(own[h], contract_rows(ds, keys), 0.0)
            dk_buf[key_item] = dk
            dv_buf[key_item] = dv
            return out, dq

        empty = jnp.zeros((block, LANES), F32)
        out, dq = lax.fori_loop(0, item + 1, apply, (empty, empty))
        store(0, item, out)
        rows = pl.ds(pl.multiple_of(item * block, block), block)
        store(1, item, turn(dq * scale, cos_ref[rows, :], -sin_ref[rows, :]))
        return 0

    lax.fori_loop(0, count, per_query, 0)

    def finish(item, _):
        rows = pl.ds(pl.multiple_of(item * block, block), block)
        store(2, item, turn(dk_buf[item], cos_ref[rows, :], -sin_ref[rows, :]))
        store(3, item, dv_buf[item])
        return 0

    lax.fori_loop(0, count, finish, 0)


def attend(qkv, grads, cosine, sine, heads, dup):
    shards, items = qkv.shape[:2]
    half = qkv.shape[-2]
    tokens = shards * 2 * half
    block = 2 * half
    once = pl.Buffered(1)
    pairs = shards * (shards + 1) // 2 * items * heads
    return pl.pallas_call(
        partial(attend_kernel, shards, heads, dup),
        grid=(items,),
        out_shape=jax.ShapeDtypeStruct((shards, items, 4, 2, half, LANES), BF16),
        in_specs=[
            pl.BlockSpec(
                (shards, 1, 3, 2, half, LANES), lambda i: (0, i, 0, 0, 0, 0), pipeline_mode=once
            ),
            pl.BlockSpec((shards, 1, 2, half, LANES), lambda i: (0, i, 0, 0, 0), pipeline_mode=once),
            pl.BlockSpec((tokens, LANES), lambda i: (0, 0), pipeline_mode=once),
            pl.BlockSpec((tokens, LANES), lambda i: (0, 0), pipeline_mode=once),
        ],
        out_specs=pl.BlockSpec(
            (shards, 1, 4, 2, half, LANES), lambda i: (0, i, 0, 0, 0, 0), pipeline_mode=once
        ),
        scratch_shapes=[
            pltpu.VMEM((heads, shards, block, block), F32),
            pltpu.VMEM((heads, shards, block, block), F32),
            pltpu.VMEM((shards, block, LANES), F32),
            pltpu.VMEM((shards, block, LANES), F32),
        ],
        compiler_params=pltpu.CompilerParams(vmem_limit_bytes=58 * 2**20),
        cost_estimate=pl.CostEstimate(
            flops=pairs * 5 * 2 * block * block * 256,
            bytes_accessed=16 * 2**20,
            transcendentals=2 * pairs * block * block,
        ),
    )(qkv, grads, cosine, sine)


def scatter_sum(parts, axis_at, place, bits):
    lead, tail = parts.shape[:axis_at], parts.shape[axis_at + 1 :]
    total = len(bits)
    left = list(range(total - 1, -1, -1))
    value = parts.reshape(lead + (2,) * total + tail)
    for bit in bits:
        at = axis_at + left.index(bit)
        left.remove(bit)
        mine = (place >> bit) & 1
        send = lax.dynamic_index_in_dim(value, 1 - mine, at, keepdims=False)
        keep = lax.dynamic_index_in_dim(value, mine, at, keepdims=False)
        got = swap(send.astype(BF16), "ctx", 1 << bit)
        value = keep.astype(F32) + got.astype(F32)
    return value


def gather_rows(own):
    far = swap(own, "fsdp", 2)
    pair = swap(jnp.stack([own, far]), "fsdp", 1)
    return [own, pair[0], far, pair[1]]


def scatter_rows(parts):
    near = swap(jnp.stack([parts[1], parts[3]]).astype(BF16), "fsdp", 1).astype(F32)
    mine = parts[0] + near[0]
    far = swap((parts[2] + near[1]).astype(BF16), "fsdp", 2)
    return mine + far.astype(F32)


def total_sum(value):
    for axis in ("fsdp", "ctx"):
        bit = 1
        while bit < lax.axis_size(axis):
            value = value + swap(value, axis, bit)
            bit *= 2
    return value


def on_device(
    inputs,
    norm_gain,
    norm_shift,
    qkv_weight,
    qkv_bias,
    out_weight,
    out_bias,
    up_weight,
    up_bias,
    down_weight,
    down_bias,
    cotangent,
):
    rows = inputs.shape[1]
    width = inputs.shape[2]
    hidden_width = up_weight.shape[1]
    half = rows // 2
    shards = lax.axis_size("ctx")
    groups = lax.axis_size("fsdp")
    place = lax.axis_index("ctx")
    member = lax.axis_index("fsdp")
    wide = width // groups
    deep = hidden_width // groups
    bits = shards.bit_length() - 1

    tokens = inputs[0].astype(F32)
    mean = jnp.mean(tokens, axis=-1, keepdims=True)
    centred = tokens - mean
    inv_scale = lax.rsqrt(jnp.mean(centred * centred, axis=-1, keepdims=True) + EPS)
    normal = centred * inv_scale
    flat = (normal * norm_gain + norm_shift).astype(BF16)

    def relative(value, axis):
        return [
            lax.dynamic_index_in_dim(value, member ^ j, axis, keepdims=False) for j in range(groups)
        ]

    flat_rel = jnp.stack(relative(flat.reshape(rows, groups, wide), 1))
    got = gather_rows(flat_rel)
    normed = jnp.concatenate(
        [
            jnp.concatenate([got[j][i ^ j] for i in range(groups)], axis=1)
            for j in range(groups)
        ],
        axis=0,
    )
    grad_low = cotangent[0]
    grads = jnp.concatenate(gather_rows(grad_low), axis=0)

    qkv_cols = qkv_weight.reshape(wide, 3, groups, wide)
    up_cols = up_weight.reshape(wide, groups, deep)
    qkv_pieces, up_pieces = [], []
    for j in range(groups):
        piece = lax.dynamic_index_in_dim(qkv_cols, member ^ j, 2, keepdims=False).reshape(
            wide, 3 * wide
        )
        qkv_pieces.append(swap(piece, "fsdp", j) if j else piece)
    for j in range(groups):
        piece = lax.dynamic_index_in_dim(up_cols, member ^ j, 1, keepdims=False)
        up_pieces.append(swap(piece, "fsdp", j) if j else piece)
    qkv_bias_own = lax.dynamic_index_in_dim(
        qkv_bias.reshape(3, groups, wide), member, 1, keepdims=False
    )
    up_bias_own = lax.dynamic_index_in_dim(up_bias.reshape(groups, deep), member, 0, keepdims=False)

    pairs = wide // LANES
    heads_in_pair = LANES // HD
    units = pairs * groups
    dup = max(1, shards // units)
    slot_groups = shards // (pairs * dup)
    per_group = groups // slot_groups
    heads = heads_in_pair // dup

    def spread(value):
        shape = value.shape
        if dup > 1:
            value = jnp.broadcast_to(
                value[:, :, None], shape[:2] + (dup,) + shape[2:]
            )
        return value.reshape((shards,) + shape[2:])

    local = jnp.arange(rows, dtype=jnp.int32)
    blocks = jnp.where(local < half, place, 2 * shards - 1 - place)
    cosine, sine = rotary(blocks * half + local % half)
    qkv_out = project(normed, qkv_pieces, qkv_bias_own, cosine, sine, slot_groups, per_group)
    qkv_in = lax.all_to_all(spread(qkv_out), "ctx", 0, 0)

    grad_att = contract_cols(grads, out_weight).astype(BF16)
    grad_att = grad_att.reshape(slot_groups, per_group, rows, pairs, LANES).transpose(3, 0, 1, 2, 4)
    grad_in = lax.all_to_all(spread(grad_att), "ctx", 0, 0)

    up_own = jnp.concatenate(up_pieces, axis=0)
    up_rows = matmul(normed, up_own) + up_bias_own
    hidden = gelu_value(up_rows).astype(BF16)
    grad_hidden = contract_cols(grads, down_weight)
    grad_up = (grad_hidden * gelu_slope(up_rows)).astype(BF16)
    down_grad = contract_rows(hidden, grads).astype(BF16)
    up_grad = contract_rows(normed, grad_up).astype(BF16)
    hw = deep // shards
    down_weight_grad = scatter_sum(
        down_grad.reshape(shards, hw, width), 0, place, list(range(bits))
    )
    up_part = scatter_sum(
        up_grad.reshape(groups, shards, wide // shards, deep), 1, place, list(range(bits))
    )

    full = jnp.arange(shards * rows, dtype=jnp.int32)
    cos_full, sin_full = rotary(full)
    back = attend(
        qkv_in.reshape(shards, per_group, 3, 2, half, LANES),
        grad_in.reshape(shards, per_group, 2, half, LANES),
        cos_full,
        sin_full,
        heads,
        dup,
    )
    back = lax.all_to_all(back, "ctx", 0, 0)
    back = back.reshape(pairs, slot_groups, dup, per_group, 4, rows, LANES)
    back = jnp.sum(back, axis=2) if dup > 1 else back[:, :, 0]
    back = back.transpose(3, 1, 2, 4, 0, 5).reshape(4, groups * rows, wide)
    attended = back[0]
    grad_qkv = jnp.concatenate([back[1], back[2], back[3]], axis=1)

    share = matmul(hidden, down_weight) + matmul(attended, out_weight)
    result = tokens + scatter_rows(list(share.reshape(groups, rows, width))) + out_bias + down_bias

    qkv_own = jnp.concatenate(qkv_pieces, axis=0)
    grad_share = contract_cols(grad_up, up_own) + contract_cols(grad_qkv, qkv_own)
    grad_share = grad_share.reshape(groups, rows, groups, wide)
    grad_share = [
        jnp.stack([grad_share[j, :, i ^ j] for i in range(groups)]) for j in range(groups)
    ]
    grad_normed = scatter_rows(grad_share)
    grad_normed = jnp.concatenate(relative(grad_normed, 0), axis=1)
    grad_full = grad_low.astype(F32)
    grad_normal = grad_normed * norm_gain
    grad_tokens = inv_scale * (
        grad_normal
        - jnp.mean(grad_normal, axis=-1, keepdims=True)
        - normal * jnp.mean(grad_normal * normal, axis=-1, keepdims=True)
    )
    input_grad = (grad_full + grad_tokens).astype(BF16)

    qkv_grad = contract_rows(normed, grad_qkv).astype(BF16)
    out_grad = contract_rows(attended, grads).astype(BF16)
    ow = wide // shards
    out_weight_grad = scatter_sum(out_grad.reshape(shards, ow, width), 0, place, list(range(bits)))
    qkv_part = scatter_sum(
        qkv_grad.reshape(groups, shards, ow, 3 * wide), 1, place, list(range(bits))
    )

    def exchange(part):
        part = part.astype(BF16)
        got = [part[0]] + [swap(part[j], "fsdp", j) for j in range(1, groups)]
        return relative(jnp.stack(got), 0)

    up_weight_grad = jnp.concatenate(exchange(up_part), axis=1).astype(F32)
    qkv_weight_grad = jnp.concatenate(
        [item.reshape(ow, 3, 1, wide) for item in exchange(qkv_part)], axis=2
    ).reshape(ow, 3 * width).astype(F32)

    qkv_bias_cols = jnp.sum(grad_qkv.astype(F32), axis=0).reshape(3, 1, wide)
    up_bias_cols = jnp.sum(grad_up.astype(F32), axis=0).reshape(1, deep)
    qkv_bias_all = lax.dynamic_update_slice(
        jnp.zeros((3, groups, wide), F32), qkv_bias_cols, (0, member, 0)
    ).reshape(-1)
    up_bias_all = lax.dynamic_update_slice(
        jnp.zeros((groups, deep), F32), up_bias_cols, (member, 0)
    ).reshape(-1)
    sums = total_sum(
        jnp.concatenate(
            [
                jnp.sum(grad_normed * normal, axis=0),
                jnp.sum(grad_normed, axis=0),
                jnp.sum(grad_full, axis=0),
                qkv_bias_all,
                up_bias_all,
            ]
        )
    )
    gain_grad = sums[:width]
    shift_grad = sums[width : 2 * width]
    out_bias_grad = sums[2 * width : 3 * width]
    qkv_bias_grad = sums[3 * width : 6 * width]
    up_bias_grad = sums[6 * width :]
    return (
        result.astype(BF16)[None],
        input_grad[None],
        gain_grad,
        shift_grad,
        qkv_weight_grad,
        qkv_bias_grad,
        out_weight_grad,
        out_bias_grad,
        up_weight_grad,
        up_bias_grad,
        down_weight_grad,
        out_bias_grad,
    )


def solution(mesh):
    in_specs = (
        P("fsdp", "ctx", None),
        P(),
        P(),
        P("fsdp", None),
        P(),
        P("fsdp", None),
        P(),
        P("fsdp", None),
        P(),
        P("fsdp", None),
        P(),
        P("fsdp", "ctx", None),
    )
    out_specs = (
        P("fsdp", "ctx", None),
        P("fsdp", "ctx", None),
        P(),
        P(),
        P(("fsdp", "ctx"), None),
        P(),
        P(("fsdp", "ctx"), None),
        P(),
        P(("fsdp", "ctx"), None),
        P(),
        P(("fsdp", "ctx"), None),
        P(),
    )
    return jax.shard_map(
        on_device, mesh=mesh, in_specs=in_specs, out_specs=out_specs, check_vma=False
    )
```

```python
from functools import partial

import jax
import jax.numpy as jnp
import numpy as np
from jax import lax
from jax.experimental import pallas as pl
from jax.experimental.pallas import tpu as pltpu
from jax.sharding import PartitionSpec as P

HD = 64
ROT = 32
LANES = 128

EPS = 1e-05
ROOT = 0.7978845608028654
CUBIC = 0.044715
F32 = jnp.float32
BF16 = jnp.bfloat16


def gelu_value(value):
    return 0.5 * value * (1.0 + jnp.tanh(ROOT * (value + CUBIC * value * value * value)))


def gelu_slope(value):
    tangent = jnp.tanh(ROOT * (value + CUBIC * value * value * value))
    return 0.5 * (1.0 + tangent) + 0.5 * value * (1.0 - tangent * tangent) * ROOT * (
        1.0 + 3.0 * CUBIC * value * value
    )


def contract_rows(left, right):
    return lax.dot_general(left, right, (((0,), (0,)), ((), ())), preferred_element_type=F32)


def contract_cols(left, right):
    return lax.dot_general(left, right, (((1,), (1,)), ((), ())), preferred_element_type=F32)


def matmul(left, right):
    return jnp.dot(left, right, preferred_element_type=F32)


def swap(value, axis, bit):
    size = lax.axis_size(axis)
    return lax.ppermute(value, axis, [(i, i ^ bit) for i in range(size)])


def after(value, *events):
    return lax.optimization_barrier((value,) + events)[0]


def rotary(length):
    quarter = ROT // 2
    inverse = np.float32(10000.0) ** (-np.arange(quarter, dtype=np.float32) * 2.0 / ROT)
    angle = np.arange(length, dtype=np.float32)[:, None] * inverse.astype(np.float32)[None, :]
    cosine, sine = np.cos(angle), np.sin(angle)
    one = np.concatenate([cosine, cosine, np.ones((length, HD - ROT))], axis=1)
    two = np.concatenate([-sine, sine, np.zeros((length, HD - ROT))], axis=1)
    copies = (1, LANES // HD)
    return (
        jnp.asarray(np.tile(one, copies), F32),
        jnp.asarray(np.tile(two, copies), F32),
    )


def turn(rows, cosine, sine):
    lane = lax.broadcasted_iota(jnp.int32, rows.shape, 1) % HD
    quarter = ROT // 2
    other = jnp.where(
        lane < quarter,
        pltpu.roll(rows, LANES - quarter, 1),
        pltpu.roll(rows, quarter, 1),
    )
    return rows * cosine + other * sine


def remote(src, dst, sends, recvs, at, target):
    return pltpu.make_async_remote_copy(
        src_ref=src,
        dst_ref=dst,
        send_sem=sends.at[at],
        recv_sem=recvs.at[at],
        device_id=target,
        device_id_type=pl.DeviceIdType.MESH,
    )


def start_kernel(
    shards,
    groups,
    pairs,
    slot_groups,
    items,
    dup,
    x_ref,
    gain_ref,
    shift_ref,
    cot_ref,
    qkv_ref,
    qkv_bias_ref,
    up_ref,
    up_bias_ref,
    out_ref,
    down_ref,
    cos_ref,
    sin_ref,
    normed_out,
    grads_out,
    wqkv_out,
    wup_out,
    hidden_out,
    du_out,
    qkv_in,
    do_in,
    normed,
    grads,
    wqkv,
    wup,
    down,
    outw,
    cosine,
    sine,
    stage,
    dstage,
    dh,
    hidden,
    du,
    local_sem,
    store_sem,
    qs,
    qr,
    us,
    ur,
    rs,
    rr,
    as_,
    ar,
    ds_,
    dr,
):
    place = lax.axis_index("ctx")
    member = lax.axis_index("fsdp")
    side = place % 2
    rows, width = x_ref.shape
    half = rows // 2
    wide = width // groups
    deep = up_ref.shape[1] // groups
    part = wide // 2

    barrier = pltpu.get_barrier_semaphore()
    for j in range(1, groups):
        pl.semaphore_signal(
            barrier, inc=1, device_id={"fsdp": member ^ j}, device_id_type=pl.DeviceIdType.MESH
        )
    for k in range(1, shards):
        pl.semaphore_signal(
            barrier, inc=1, device_id={"ctx": place ^ k}, device_id_type=pl.DeviceIdType.MESH
        )

    def local(src, dst, at):
        copy = pltpu.make_async_copy(src, dst, local_sem.at[at])
        copy.start()
        return copy

    def block(at, size):
        return pl.ds(pl.multiple_of(at, size), size)

    own_rows = block(member * wide, wide)
    loads = [
        local(
            qkv_ref.at[:, block(p * width + member * wide, wide)],
            wqkv.at[own_rows, pl.ds(p * wide, wide)],
            p,
        )
        for p in range(3)
    ]
    loads.append(local(up_ref.at[:, block(member * deep, deep)], wup.at[own_rows, :], 3))
    loads.append(local(cot_ref, grads.at[pl.ds(0, rows)], 4))
    loads.append(local(out_ref, outw, 5))
    loads.append(local(down_ref, down, 6))
    upper = 2 * shards - 1 - place
    for at, (table, held) in enumerate(((cos_ref, cosine), (sin_ref, sine))):
        loads.append(
            local(table.at[block(place * half, half)], held.at[pl.ds(0, half)], 7 + 2 * at)
        )
        loads.append(
            local(table.at[block(upper * half, half)], held.at[pl.ds(half, half)], 8 + 2 * at)
        )
    pl.semaphore_wait(barrier, groups - 1 + shards - 1)

    half_rows = block(member * wide + side * part, part)
    started = []

    def begin(copy):
        copy.start()
        started.append(copy)
        return copy

    q_far = {}
    for j in (2, 3):
        for p in range(3):
            q_far[j, p] = begin(
                remote(
                    qkv_ref.at[block(side * part, part), block(p * width + (member ^ j) * wide, wide)],
                    wqkv.at[half_rows, pl.ds(p * wide, wide)],
                    qs,
                    qr,
                    (j - 2) * 3 + p,
                    {"fsdp": member ^ j},
                )
            )

    tokens = x_ref[...].astype(F32)
    centred = tokens - jnp.mean(tokens, axis=-1, keepdims=True)
    spread = lax.rsqrt(jnp.mean(centred * centred, axis=-1, keepdims=True) + EPS)
    normed[0:rows, :] = (centred * spread * gain_ref[...] + shift_ref[...]).astype(BF16)
    n_far = begin(
        remote(
            normed.at[pl.ds(0, rows)], normed.at[pl.ds(2 * rows, rows)], rs, rr, 0, {"fsdp": member ^ 2}
        )
    )
    n_near = begin(
        remote(normed.at[pl.ds(0, rows)], normed.at[pl.ds(rows, rows)], rs, rr, 1, {"fsdp": member ^ 1})
    )
    q_near = [
        begin(
            remote(
                qkv_ref.at[:, block(p * width + (member ^ 1) * wide, wide)],
                wqkv.at[own_rows, pl.ds(p * wide, wide)],
                qs,
                qr,
                6 + p,
                {"fsdp": member ^ 1},
            )
        )
        for p in range(3)
    ]

    q_side = []
    for j in (2, 3):
        for p in range(3):
            q_far[j, p].wait_recv()
            spot = wqkv.at[block((member ^ j) * wide + side * part, part), pl.ds(p * wide, wide)]
            q_side.append(
                begin(remote(spot, spot, qs, qr, 9 + (j - 2) * 3 + p, {"ctx": place ^ 1}))
            )
    n_far.wait_recv()
    n_last = begin(
        remote(
            normed.at[pl.ds(2 * rows, rows)],
            normed.at[pl.ds(3 * rows, rows)],
            rs,
            rr,
            2,
            {"fsdp": member ^ 1},
        )
    )

    loads[4].wait()
    g_far = begin(
        remote(
            grads.at[pl.ds(0, rows)], grads.at[pl.ds(2 * rows, rows)], rs, rr, 3, {"fsdp": member ^ 2}
        )
    )
    g_near = begin(
        remote(grads.at[pl.ds(0, rows)], grads.at[pl.ds(rows, rows)], rs, rr, 4, {"fsdp": member ^ 1})
    )
    u_far = [
        begin(
            remote(
                up_ref.at[block(side * part, part), block((member ^ j) * deep, deep)],
                wup.at[half_rows, :],
                us,
                ur,
                j - 2,
                {"fsdp": member ^ j},
            )
        )
        for j in (2, 3)
    ]
    u_near = begin(
        remote(
            up_ref.at[:, block((member ^ 1) * deep, deep)],
            wup.at[own_rows, :],
            us,
            ur,
            2,
            {"fsdp": member ^ 1},
        )
    )

    for at in (0, 1, 2, 7, 8, 9, 10):
        loads[at].wait()
    for copy in q_near + q_side:
        copy.wait_recv()
    n_near.wait_recv()
    arrivals = []
    stores = []

    def keep(src, dst):
        copy = pltpu.make_async_copy(src, dst, store_sem.at[len(stores)])
        copy.start()
        stores.append(copy)

    def owner(target):
        return target // (slot_groups * dup), (target // dup) % slot_groups

    for item in range(items):
        if item == items - 1:
            n_last.wait_recv()

        def project(p, _, item=item):
            for g in range(slot_groups):
                slot = item * slot_groups + g
                acc = qkv_bias_ref[p * groups + member] + jnp.dot(
                    normed[slot * rows : (slot + 1) * rows, :],
                    wqkv[:, block(p * wide, wide)],
                    preferred_element_type=F32,
                )
                for h in range(pairs):
                    cols = acc[:, h * LANES : (h + 1) * LANES]
                    turned = turn(cols, cosine[...], sine[...])
                    stage[item, h, g, p] = jnp.where(p < 2, turned, cols).astype(BF16)
            return 0

        lax.fori_loop(0, 3, project, 0)
        for k in range(1, shards):
            pair, group = owner(place ^ k)
            arrivals.append(
                begin(
                    remote(
                        stage.at[item, pair, group],
                        qkv_in.at[item, place],
                        as_,
                        ar,
                        item * shards + k,
                        {"ctx": place ^ k},
                    )
                )
            )
        pair, group = owner(place)
        keep(stage.at[item, pair, group], qkv_in.at[item, place])

    g_far.wait_recv()
    g_last = begin(
        remote(
            grads.at[pl.ds(2 * rows, rows)],
            grads.at[pl.ds(3 * rows, rows)],
            rs,
            rr,
            5,
            {"fsdp": member ^ 1},
        )
    )
    g_near.wait_recv()
    loads[5].wait()
    g_last.wait_recv()
    for slot in range(groups):
        item, g = slot // slot_groups, slot % slot_groups
        att = contract_cols(grads[slot * rows : (slot + 1) * rows, :], outw[...]).astype(BF16)
        for h in range(pairs):
            dstage[h, g, item] = att[:, h * LANES : (h + 1) * LANES]
    for k in range(1, shards):
        pair, group = owner(place ^ k)
        arrivals.append(
            begin(
                remote(
                    dstage.at[pair, group],
                    do_in.at[place],
                    ds_,
                    dr,
                    k,
                    {"ctx": place ^ k},
                )
            )
        )
    pair, group = owner(place)
    keep(dstage.at[pair, group], do_in.at[place])
    keep(normed, normed_out)
    keep(grads, grads_out)
    keep(wqkv, wqkv_out)

    u_side = []
    for j in (2, 3):
        u_far[j - 2].wait_recv()
        spot = wup.at[block((member ^ j) * wide + side * part, part), :]
        u_side.append(begin(remote(spot, spot, us, ur, 3 + j - 2, {"ctx": place ^ 1})))

    loads[6].wait()
    tile = 512
    high = 2 * rows

    def spot_of(at):
        return block((at % 2) * high, high), block((at // 2) * tile, tile)

    def back(at, _):
        r, c = spot_of(at)
        dh[r, c] = contract_cols(grads[r, :], down[c, :])
        return 0

    lax.fori_loop(0, 2 * (deep // tile), back, 0)
    loads[3].wait()
    u_near.wait_recv()
    for copy in u_side:
        copy.wait_recv()
    keep(wup, wup_out)

    def forward(at, _):
        r, c = spot_of(at)
        value = matmul(normed[r, :], wup[:, c]) + up_bias_ref[member, :, c]
        hidden[r, c] = gelu_value(value).astype(BF16)
        du[r, c] = (dh[r, c] * gelu_slope(value)).astype(BF16)
        return 0

    lax.fori_loop(0, 2 * (deep // tile), forward, 0)
    keep(hidden, hidden_out)
    keep(du, du_out)
    for copy in arrivals:
        copy.wait_recv()
    for copy in started:
        copy.wait_send()
    for copy in stores:
        copy.wait()


def begin_layer(
    x, gain, shift, cot, qkv_w, qkv_b, up_w, up_b, out_w, down_w, cosine, sine,
    shards, groups, pairs, slot_groups, items, dup,
):
    rows, width = x.shape
    wide = width // groups
    deep = up_w.shape[1] // groups
    total = rows * groups
    whole = pl.BlockSpec(memory_space=pltpu.VMEM)
    apart = pl.BlockSpec(memory_space=pl.ANY)
    dma = pltpu.SemaphoreType.DMA
    shape = jax.ShapeDtypeStruct
    stores = items + 1 + 6
    return pl.pallas_call(
        partial(start_kernel, shards, groups, pairs, slot_groups, items, dup),
        out_shape=[
            shape((total, width), BF16),
            shape((total, width), BF16),
            shape((width, 3 * wide), BF16),
            shape((width, deep), BF16),
            shape((total, deep), BF16),
            shape((total, deep), BF16),
            shape((items, shards, 3, rows, LANES), BF16),
            shape((shards, items, rows, LANES), BF16),
        ],
        in_specs=[whole, whole, whole, apart, apart, whole, apart, whole, apart, apart, apart, apart],
        out_specs=[apart] * 8,
        scratch_shapes=[
            pltpu.VMEM((total, width), BF16),
            pltpu.VMEM((total, width), BF16),
            pltpu.VMEM((width, 3 * wide), BF16),
            pltpu.VMEM((width, deep), BF16),
            pltpu.VMEM((deep, width), BF16),
            pltpu.VMEM((wide, width), BF16),
            pltpu.VMEM((rows, LANES), F32),
            pltpu.VMEM((rows, LANES), F32),
            pltpu.VMEM((items, pairs, slot_groups, 3, rows, LANES), BF16),
            pltpu.VMEM((pairs, slot_groups, items, rows, LANES), BF16),
            pltpu.VMEM((total, deep), F32),
            pltpu.VMEM((total, deep), BF16),
            pltpu.VMEM((total, deep), BF16),
            dma((11,)),
            dma((stores,)),
            dma((15,)),
            dma((15,)),
            dma((5,)),
            dma((5,)),
            dma((6,)),
            dma((6,)),
            dma((items * shards,)),
            dma((items * shards,)),
            dma((shards,)),
            dma((shards,)),
        ],
        compiler_params=pltpu.CompilerParams(
            collective_id=0, has_side_effects=True, vmem_limit_bytes=62 * 2**20
        ),
        cost_estimate=pl.CostEstimate(
            flops=2 * total * width * (3 * wide + wide + 2 * deep),
            bytes_accessed=60 * 2**20,
            transcendentals=total * deep,
        ),
    )(
        x,
        gain.reshape(1, width),
        shift.reshape(1, width),
        cot,
        qkv_w,
        qkv_b.reshape(3 * groups, 1, wide),
        up_w,
        up_b.reshape(groups, 1, deep),
        out_w,
        down_w,
        cosine,
        sine,
    )


def attend_kernel(
    shards, heads, dup, qkv_ref, do_ref, cos_ref, sin_ref, out_ref, s_buf, dp_buf, dk_buf, dv_buf
):
    half = qkv_ref.shape[-2]
    block = 2 * half
    count = shards
    base = lax.axis_index("ctx") % dup
    lane = lax.broadcasted_iota(jnp.int32, (block, LANES), 1) // HD
    own = [lane == (base + h) for h in range(heads)]
    scale = HD**-0.5

    def where_is(item):
        low = item < count // 2
        first = jnp.where(low, 2 * item, 2 * count - 1 - 2 * item)
        second = jnp.where(low, 2 * item + 1, 2 * count - 2 - 2 * item)
        return first, second, jnp.where(low, 0, 1)

    def load(part, item):
        first, second, side = where_is(item)
        return jnp.concatenate(
            [qkv_ref[0, first, part, side], qkv_ref[0, second, part, side]], axis=0
        )

    def load_do(item):
        first, second, side = where_is(item)
        return jnp.concatenate([do_ref[first, 0, side], do_ref[second, 0, side]], axis=0)

    def store(part, item, value):
        first, second, side = where_is(item)
        out_ref[first, 0, part, side] = value[:half].astype(out_ref.dtype)
        out_ref[second, 0, part, side] = value[half:].astype(out_ref.dtype)

    dk_buf[...] = jnp.zeros_like(dk_buf)
    dv_buf[...] = jnp.zeros_like(dv_buf)
    nothing = jnp.zeros((block, LANES), BF16)
    key_at = lax.broadcasted_iota(jnp.int32, (block, block), 0)
    query_at = lax.broadcasted_iota(jnp.int32, (block, block), 1)

    def per_query(item, _):
        query = load(0, item) * jnp.asarray(scale, BF16)
        grad = load_do(item)
        queries = [jnp.where(own[h], query, nothing) for h in range(heads)]
        grads = [jnp.where(own[h], grad, nothing) for h in range(heads)]

        def measure(key_item, state, diagonal):
            keys, values = load(1, key_item), load(2, key_item)
            new = []
            for h in range(heads):
                top, total, dot = state[h]
                s = contract_cols(keys, queries[h])
                if diagonal:
                    s = jnp.where(key_at <= query_at, s, -1e30)
                dp = contract_cols(values, grads[h])
                s_buf[h, key_item] = s
                dp_buf[h, key_item] = dp
                new_top = jnp.maximum(top, jnp.max(s, axis=0, keepdims=True))
                e = jnp.exp(s - new_top)
                fade = jnp.exp(top - new_top)
                new.append(
                    (
                        new_top,
                        total * fade + jnp.sum(e, axis=0, keepdims=True),
                        dot * fade + jnp.sum(e * dp, axis=0, keepdims=True),
                    )
                )
            return tuple(new)

        zero = jnp.zeros((1, block), F32)
        start = tuple((zero - 1e30, zero, zero) for _ in range(heads))
        state = lax.fori_loop(0, item, lambda k, st: measure(k, st, False), start)
        state = measure(item, state, True)
        logs = [top + jnp.log(total) for top, total, _ in state]
        deltas = [dot / total for _, total, dot in state]

        def apply(key_item, state):
            keys, values = load(1, key_item), load(2, key_item)
            out, dq = state
            dk, dv = dk_buf[key_item], dv_buf[key_item]
            for h in range(heads):
                p = jnp.exp(s_buf[h, key_item] - logs[h])
                ds = (p * (dp_buf[h, key_item] - deltas[h])).astype(BF16)
                p = p.astype(BF16)
                dv = dv + matmul(p, grads[h])
                dk = dk + matmul(ds, queries[h])
                out = out + jnp.where(own[h], contract_rows(p, values), 0.0)
                dq = dq + jnp.where(own[h], contract_rows(ds, keys), 0.0)
            dk_buf[key_item] = dk
            dv_buf[key_item] = dv
            return out, dq

        empty = jnp.zeros((block, LANES), F32)
        out, dq = lax.fori_loop(0, item + 1, apply, (empty, empty))
        store(0, item, out)
        rows = pl.ds(pl.multiple_of(item * block, block), block)
        store(1, item, turn(dq * scale, cos_ref[rows, :], -sin_ref[rows, :]))
        return 0

    lax.fori_loop(0, count, per_query, 0)

    def finish(item, _):
        rows = pl.ds(pl.multiple_of(item * block, block), block)
        store(2, item, turn(dk_buf[item], cos_ref[rows, :], -sin_ref[rows, :]))
        store(3, item, dv_buf[item])
        return 0

    lax.fori_loop(0, count, finish, 0)


def attend(qkv, grads, item, cosine, sine, heads, dup):
    shards, items = qkv.shape[1], 1
    half = qkv.shape[-2]
    tokens = shards * 2 * half
    block = 2 * half
    once = pl.Buffered(1)
    pairs = shards * (shards + 1) // 2 * items * heads
    return pl.pallas_call(
        partial(attend_kernel, shards, heads, dup),
        grid=(items,),
        out_shape=jax.ShapeDtypeStruct((shards, items, 4, 2, half, LANES), BF16),
        in_specs=[
            pl.BlockSpec(
                (1, shards, 3, 2, half, LANES), lambda i: (item, 0, 0, 0, 0, 0), pipeline_mode=once
            ),
            pl.BlockSpec(
                (shards, 1, 2, half, LANES), lambda i: (0, item, 0, 0, 0), pipeline_mode=once
            ),
            pl.BlockSpec((tokens, LANES), lambda i: (0, 0), pipeline_mode=once),
            pl.BlockSpec((tokens, LANES), lambda i: (0, 0), pipeline_mode=once),
        ],
        out_specs=pl.BlockSpec(
            (shards, 1, 4, 2, half, LANES), lambda i: (0, i, 0, 0, 0, 0), pipeline_mode=once
        ),
        scratch_shapes=[
            pltpu.VMEM((heads, shards, block, block), F32),
            pltpu.VMEM((heads, shards, block, block), F32),
            pltpu.VMEM((shards, block, LANES), F32),
            pltpu.VMEM((shards, block, LANES), F32),
        ],
        compiler_params=pltpu.CompilerParams(vmem_limit_bytes=58 * 2**20),
        cost_estimate=pl.CostEstimate(
            flops=pairs * 5 * 2 * block * block * 256,
            bytes_accessed=16 * 2**20,
            transcendentals=2 * pairs * block * block,
        ),
    )(qkv, grads, cosine, sine)


def scatter_sum(parts, axis_at, place, bits):
    lead, tail = parts.shape[:axis_at], parts.shape[axis_at + 1 :]
    total = len(bits)
    left = list(range(total - 1, -1, -1))
    value = parts.reshape(lead + (2,) * total + tail)
    for bit in bits:
        at = axis_at + left.index(bit)
        left.remove(bit)
        mine = (place >> bit) & 1
        send = lax.dynamic_index_in_dim(value, 1 - mine, at, keepdims=False)
        keep = lax.dynamic_index_in_dim(value, mine, at, keepdims=False)
        got = swap(send.astype(BF16), "ctx", 1 << bit)
        value = keep.astype(F32) + got.astype(F32)
    return value


def scatter_rows(parts):
    last = swap(parts[3].astype(BF16), "fsdp", 1).astype(F32)
    far = swap((parts[2] + last).astype(BF16), "fsdp", 2).astype(F32)
    near = swap(parts[1].astype(BF16), "fsdp", 1).astype(F32)
    return parts[0] + near + far


def total_sum(value):
    for axis in ("fsdp", "ctx"):
        bit = 1
        while bit < lax.axis_size(axis):
            value = value + swap(value, axis, bit)
            bit *= 2
    return value


def on_device(
    inputs,
    norm_gain,
    norm_shift,
    qkv_weight,
    qkv_bias,
    out_weight,
    out_bias,
    up_weight,
    up_bias,
    down_weight,
    down_bias,
    cotangent,
):
    rows = inputs.shape[1]
    width = inputs.shape[2]
    hidden_width = up_weight.shape[1]
    half = rows // 2
    shards = lax.axis_size("ctx")
    groups = lax.axis_size("fsdp")
    place = lax.axis_index("ctx")
    member = lax.axis_index("fsdp")
    wide = width // groups
    deep = hidden_width // groups
    x_first = list(range(shards.bit_length() - 1))
    z_first = x_first[1:2] + x_first[:1] + x_first[2:]

    tokens = inputs[0].astype(F32)
    mean = jnp.mean(tokens, axis=-1, keepdims=True)
    centred = tokens - mean
    inv_scale = lax.rsqrt(jnp.mean(centred * centred, axis=-1, keepdims=True) + EPS)
    normal = centred * inv_scale
    grad_low = cotangent[0]
    grad_full = grad_low.astype(F32)

    pairs = wide // LANES
    heads_in_pair = LANES // HD
    units = pairs * groups
    dup = max(1, shards // units)
    slot_groups = shards // (pairs * dup)
    per_group = groups // slot_groups
    heads = heads_in_pair // dup

    cos_full, sin_full = rotary(shards * rows)
    normed, grads, qkv_own, up_own, hidden, grad_up, qkv_in, grad_in = begin_layer(
        inputs[0],
        norm_gain,
        norm_shift,
        grad_low,
        qkv_weight,
        qkv_bias,
        up_weight,
        up_bias,
        out_weight,
        down_weight,
        cos_full,
        sin_full,
        shards,
        groups,
        pairs,
        slot_groups,
        per_group,
        dup,
    )

    down_grad = contract_rows(hidden, grads).astype(BF16)
    up_grad = contract_rows(normed, grad_up).astype(BF16)
    hw = deep // shards
    down_weight_grad = scatter_sum(
        down_grad.reshape(shards, hw, width), 0, place, x_first
    )
    up_part = scatter_sum(
        up_grad.reshape(groups, shards, wide // shards, deep), 1, place, z_first
    )

    backs = []
    for item in range(per_group):
        back = attend(
            qkv_in.reshape(per_group, shards, 3, 2, half, LANES),
            grad_in.reshape(shards, per_group, 2, half, LANES),
            item,
            cos_full,
            sin_full,
            heads,
            dup,
        )
        back = lax.all_to_all(back, "ctx", 0, 0)
        back = back.reshape(pairs, slot_groups, dup, 4, rows, LANES)
        back = jnp.sum(back, axis=2) if dup > 1 else back[:, :, 0]
        backs.append(back.transpose(2, 1, 3, 0, 4).reshape(4, slot_groups * rows, wide))
    back = jnp.concatenate(backs, axis=1)
    attended = back[0]
    grad_qkv = jnp.concatenate([back[1], back[2], back[3]], axis=1)

    share = matmul(hidden, down_weight) + matmul(attended, out_weight)
    result = tokens + scatter_rows(list(share.reshape(groups, rows, width))) + out_bias + down_bias

    grad_share = contract_cols(grad_up, up_own) + contract_cols(grad_qkv, qkv_own)
    grad_normed = scatter_rows(list(grad_share.reshape(groups, rows, width)))
    grad_full = grad_low.astype(F32)
    grad_normal = grad_normed * norm_gain
    grad_tokens = inv_scale * (
        grad_normal
        - jnp.mean(grad_normal, axis=-1, keepdims=True)
        - normal * jnp.mean(grad_normal * normal, axis=-1, keepdims=True)
    )
    input_grad = (grad_full + grad_tokens).astype(BF16)

    qkv_grad = contract_rows(normed, grad_qkv).astype(BF16)
    out_grad = contract_rows(attended, grads).astype(BF16)
    ow = wide // shards
    out_weight_grad = scatter_sum(out_grad.reshape(shards, ow, width), 0, place, z_first)
    qkv_part = scatter_sum(
        qkv_grad.reshape(groups, shards, ow, 3 * wide), 1, place, x_first
    )

    def relative(value):
        return [
            lax.dynamic_index_in_dim(value, member ^ j, 0, keepdims=False) for j in range(groups)
        ]

    def exchange(part):
        sent = relative(part.astype(BF16))
        got = [sent[0]] + [swap(sent[j], "fsdp", j) for j in range(1, groups)]
        return relative(jnp.stack(got))

    up_weight_grad = jnp.concatenate(exchange(up_part), axis=1).astype(F32)
    qkv_weight_grad = jnp.concatenate(
        [item.reshape(ow, 3, 1, wide) for item in exchange(qkv_part)], axis=2
    ).reshape(ow, 3 * width).astype(F32)

    qkv_bias_cols = jnp.sum(grad_qkv.astype(F32), axis=0).reshape(3, 1, wide)
    up_bias_cols = jnp.sum(grad_up.astype(F32), axis=0).reshape(1, deep)
    qkv_bias_all = lax.dynamic_update_slice(
        jnp.zeros((3, groups, wide), F32), qkv_bias_cols, (0, member, 0)
    ).reshape(-1)
    up_bias_all = lax.dynamic_update_slice(
        jnp.zeros((groups, deep), F32), up_bias_cols, (member, 0)
    ).reshape(-1)
    early = total_sum(jnp.concatenate([jnp.sum(grad_full, axis=0), up_bias_all]))
    late = total_sum(
        jnp.concatenate(
            [jnp.sum(grad_normed * normal, axis=0), jnp.sum(grad_normed, axis=0), qkv_bias_all]
        )
    )
    out_bias_grad, up_bias_grad = early[:width], early[width:]
    gain_grad, shift_grad, qkv_bias_grad = late[:width], late[width : 2 * width], late[2 * width :]
    return (
        result.astype(BF16)[None],
        input_grad[None],
        gain_grad,
        shift_grad,
        qkv_weight_grad,
        qkv_bias_grad,
        out_weight_grad,
        out_bias_grad,
        up_weight_grad,
        up_bias_grad,
        down_weight_grad,
        out_bias_grad,
    )


def solution(mesh):
    in_specs = (
        P("fsdp", "ctx", None),
        P(),
        P(),
        P("fsdp", None),
        P(),
        P("fsdp", None),
        P(),
        P("fsdp", None),
        P(),
        P("fsdp", None),
        P(),
        P("fsdp", "ctx", None),
    )
    out_specs = (
        P("fsdp", "ctx", None),
        P("fsdp", "ctx", None),
        P(),
        P(),
        P(("fsdp", "ctx"), None),
        P(),
        P(("fsdp", "ctx"), None),
        P(),
        P(("fsdp", "ctx"), None),
        P(),
        P(("fsdp", "ctx"), None),
        P(),
    )
    return jax.shard_map(
        on_device, mesh=mesh, in_specs=in_specs, out_specs=out_specs, check_vma=False
    )
```

```python
from functools import partial

import jax
import jax.numpy as jnp
import numpy as np
from jax import lax
from jax.experimental import pallas as pl
from jax.experimental.pallas import tpu as pltpu
from jax.sharding import PartitionSpec as P

HD = 64
ROT = 32
LANES = 128

EPS = 1e-05
ROOT = 0.7978845608028654
CUBIC = 0.044715
F32 = jnp.float32
BF16 = jnp.bfloat16


def gelu_value(value):
    return 0.5 * value * (1.0 + jnp.tanh(ROOT * (value + CUBIC * value * value * value)))


def gelu_slope(value):
    tangent = jnp.tanh(ROOT * (value + CUBIC * value * value * value))
    return 0.5 * (1.0 + tangent) + 0.5 * value * (1.0 - tangent * tangent) * ROOT * (
        1.0 + 3.0 * CUBIC * value * value
    )


def contract_rows(left, right):
    return lax.dot_general(left, right, (((0,), (0,)), ((), ())), preferred_element_type=F32)


def contract_cols(left, right):
    return lax.dot_general(left, right, (((1,), (1,)), ((), ())), preferred_element_type=F32)


def matmul(left, right):
    return jnp.dot(left, right, preferred_element_type=F32)


def swap(value, axis, bit):
    size = lax.axis_size(axis)
    return lax.ppermute(value, axis, [(i, i ^ bit) for i in range(size)])


def after(value, *events):
    return lax.optimization_barrier((value,) + events)[0]


def rotary(length):
    quarter = ROT // 2
    inverse = np.float32(10000.0) ** (-np.arange(quarter, dtype=np.float32) * 2.0 / ROT)
    angle = np.arange(length, dtype=np.float32)[:, None] * inverse.astype(np.float32)[None, :]
    cosine, sine = np.cos(angle), np.sin(angle)
    one = np.concatenate([cosine, cosine, np.ones((length, HD - ROT))], axis=1)
    two = np.concatenate([-sine, sine, np.zeros((length, HD - ROT))], axis=1)
    copies = (1, LANES // HD)
    return (
        jnp.asarray(np.tile(one, copies), F32),
        jnp.asarray(np.tile(two, copies), F32),
    )


def turn(rows, cosine, sine):
    lane = lax.broadcasted_iota(jnp.int32, rows.shape, 1) % HD
    quarter = ROT // 2
    other = jnp.where(
        lane < quarter,
        pltpu.roll(rows, LANES - quarter, 1),
        pltpu.roll(rows, quarter, 1),
    )
    return rows * cosine + other * sine


def remote(src, dst, sends, recvs, at, target):
    return pltpu.make_async_remote_copy(
        src_ref=src,
        dst_ref=dst,
        send_sem=sends.at[at],
        recv_sem=recvs.at[at],
        device_id=target,
        device_id_type=pl.DeviceIdType.MESH,
    )


def start_kernel(
    shards,
    groups,
    pairs,
    slot_groups,
    items,
    dup,
    x_ref,
    gain_ref,
    shift_ref,
    cot_ref,
    qkv_ref,
    qkv_bias_ref,
    up_ref,
    up_bias_ref,
    out_ref,
    down_ref,
    cos_ref,
    sin_ref,
    normed_out,
    grads_out,
    wqkv_out,
    wup_out,
    hidden_out,
    du_out,
    qkv_in,
    do_in,
    normed,
    grads,
    wqkv,
    wup,
    down,
    outw,
    cosine,
    sine,
    stage,
    dstage,
    dh,
    hidden,
    du,
    local_sem,
    store_sem,
    qs,
    qr,
    us,
    ur,
    rs,
    rr,
    as_,
    ar,
    ds_,
    dr,
):
    place = lax.axis_index("ctx")
    member = lax.axis_index("fsdp")
    side = place % 2
    rows, width = x_ref.shape
    half = rows // 2
    wide = width // groups
    deep = up_ref.shape[1] // groups
    part = wide // 2

    barrier = pltpu.get_barrier_semaphore()
    for j in range(1, groups):
        pl.semaphore_signal(
            barrier, inc=1, device_id={"fsdp": member ^ j}, device_id_type=pl.DeviceIdType.MESH
        )
    for k in range(1, shards):
        pl.semaphore_signal(
            barrier, inc=1, device_id={"ctx": place ^ k}, device_id_type=pl.DeviceIdType.MESH
        )

    def local(src, dst, at):
        copy = pltpu.make_async_copy(src, dst, local_sem.at[at])
        copy.start()
        return copy

    def block(at, size):
        return pl.ds(pl.multiple_of(at, size), size)

    own_rows = block(member * wide, wide)
    loads = [
        local(
            qkv_ref.at[:, block(p * width + member * wide, wide)],
            wqkv.at[own_rows, pl.ds(p * wide, wide)],
            p,
        )
        for p in range(3)
    ]
    loads.append(local(up_ref.at[:, block(member * deep, deep)], wup.at[own_rows, :], 3))
    loads.append(local(cot_ref, grads.at[pl.ds(0, rows)], 4))
    loads.append(local(out_ref, outw, 5))
    loads.append(local(down_ref, down, 6))
    upper = 2 * shards - 1 - place
    for at, (table, held) in enumerate(((cos_ref, cosine), (sin_ref, sine))):
        loads.append(
            local(table.at[block(place * half, half)], held.at[pl.ds(0, half)], 7 + 2 * at)
        )
        loads.append(
            local(table.at[block(upper * half, half)], held.at[pl.ds(half, half)], 8 + 2 * at)
        )
    pl.semaphore_wait(barrier, groups - 1 + shards - 1)

    half_rows = block(member * wide + side * part, part)
    started = []

    def begin(copy):
        copy.start()
        started.append(copy)
        return copy

    q_far = {}
    for j in (2, 3):
        for p in range(3):
            q_far[j, p] = begin(
                remote(
                    qkv_ref.at[block(side * part, part), block(p * width + (member ^ j) * wide, wide)],
                    wqkv.at[half_rows, pl.ds(p * wide, wide)],
                    qs,
                    qr,
                    (j - 2) * 3 + p,
                    {"fsdp": member ^ j},
                )
            )

    tokens = x_ref[...].astype(F32)
    centred = tokens - jnp.mean(tokens, axis=-1, keepdims=True)
    spread = lax.rsqrt(jnp.mean(centred * centred, axis=-1, keepdims=True) + EPS)
    normed[0:rows, :] = (centred * spread * gain_ref[...] + shift_ref[...]).astype(BF16)
    n_far = begin(
        remote(
            normed.at[pl.ds(0, rows)], normed.at[pl.ds(2 * rows, rows)], rs, rr, 0, {"fsdp": member ^ 2}
        )
    )
    n_near = begin(
        remote(normed.at[pl.ds(0, rows)], normed.at[pl.ds(rows, rows)], rs, rr, 1, {"fsdp": member ^ 1})
    )
    q_near = [
        begin(
            remote(
                qkv_ref.at[:, block(p * width + (member ^ 1) * wide, wide)],
                wqkv.at[own_rows, pl.ds(p * wide, wide)],
                qs,
                qr,
                6 + p,
                {"fsdp": member ^ 1},
            )
        )
        for p in range(3)
    ]

    q_side = []
    for j in (2, 3):
        for p in range(3):
            q_far[j, p].wait_recv()
            spot = wqkv.at[block((member ^ j) * wide + side * part, part), pl.ds(p * wide, wide)]
            q_side.append(
                begin(remote(spot, spot, qs, qr, 9 + (j - 2) * 3 + p, {"ctx": place ^ 1}))
            )
    n_far.wait_recv()
    n_last = begin(
        remote(
            normed.at[pl.ds(2 * rows, rows)],
            normed.at[pl.ds(3 * rows, rows)],
            rs,
            rr,
            2,
            {"fsdp": member ^ 1},
        )
    )

    loads[4].wait()
    g_far = begin(
        remote(
            grads.at[pl.ds(0, rows)], grads.at[pl.ds(2 * rows, rows)], rs, rr, 3, {"fsdp": member ^ 2}
        )
    )
    g_near = begin(
        remote(grads.at[pl.ds(0, rows)], grads.at[pl.ds(rows, rows)], rs, rr, 4, {"fsdp": member ^ 1})
    )
    u_far = [
        begin(
            remote(
                up_ref.at[block(side * part, part), block((member ^ j) * deep, deep)],
                wup.at[half_rows, :],
                us,
                ur,
                j - 2,
                {"fsdp": member ^ j},
            )
        )
        for j in (2, 3)
    ]
    u_near = begin(
        remote(
            up_ref.at[:, block((member ^ 1) * deep, deep)],
            wup.at[own_rows, :],
            us,
            ur,
            2,
            {"fsdp": member ^ 1},
        )
    )

    for at in (0, 1, 2, 7, 8, 9, 10):
        loads[at].wait()
    for copy in q_near + q_side:
        copy.wait_recv()
    n_near.wait_recv()
    arrivals = []
    stores = []

    def keep(src, dst):
        copy = pltpu.make_async_copy(src, dst, store_sem.at[len(stores)])
        copy.start()
        stores.append(copy)

    def owner(target):
        return target // (slot_groups * dup), (target // dup) % slot_groups

    for item in range(items):
        if item == items - 1:
            n_last.wait_recv()

        def project(p, _, item=item):
            for g in range(slot_groups):
                slot = item * slot_groups + g
                acc = qkv_bias_ref[p * groups + member] + jnp.dot(
                    normed[slot * rows : (slot + 1) * rows, :],
                    wqkv[:, block(p * wide, wide)],
                    preferred_element_type=F32,
                )
                for h in range(pairs):
                    cols = acc[:, h * LANES : (h + 1) * LANES]
                    turned = turn(cols, cosine[...], sine[...])
                    stage[item, h, g, p] = jnp.where(p < 2, turned, cols).astype(BF16)
            return 0

        lax.fori_loop(0, 3, project, 0)
        for k in range(1, shards):
            pair, group = owner(place ^ k)
            arrivals.append(
                begin(
                    remote(
                        stage.at[item, pair, group],
                        qkv_in.at[item, place],
                        as_,
                        ar,
                        item * shards + k,
                        {"ctx": place ^ k},
                    )
                )
            )
        pair, group = owner(place)
        keep(stage.at[item, pair, group], qkv_in.at[item, place])

    g_far.wait_recv()
    g_last = begin(
        remote(
            grads.at[pl.ds(2 * rows, rows)],
            grads.at[pl.ds(3 * rows, rows)],
            rs,
            rr,
            5,
            {"fsdp": member ^ 1},
        )
    )
    g_near.wait_recv()
    loads[5].wait()
    g_last.wait_recv()
    for slot in range(groups):
        item, g = slot // slot_groups, slot % slot_groups
        att = contract_cols(grads[slot * rows : (slot + 1) * rows, :], outw[...]).astype(BF16)
        for h in range(pairs):
            dstage[h, g, item] = att[:, h * LANES : (h + 1) * LANES]
    for k in range(1, shards):
        pair, group = owner(place ^ k)
        arrivals.append(
            begin(
                remote(
                    dstage.at[pair, group],
                    do_in.at[place],
                    ds_,
                    dr,
                    k,
                    {"ctx": place ^ k},
                )
            )
        )
    pair, group = owner(place)
    keep(dstage.at[pair, group], do_in.at[place])
    keep(normed, normed_out)
    keep(grads, grads_out)
    keep(wqkv, wqkv_out)

    u_side = []
    for j in (2, 3):
        u_far[j - 2].wait_recv()
        spot = wup.at[block((member ^ j) * wide + side * part, part), :]
        u_side.append(begin(remote(spot, spot, us, ur, 3 + j - 2, {"ctx": place ^ 1})))

    loads[6].wait()
    tile = 512
    high = 2 * rows

    def spot_of(at):
        return block((at % 2) * high, high), block((at // 2) * tile, tile)

    def back(at, _):
        r, c = spot_of(at)
        dh[r, c] = contract_cols(grads[r, :], down[c, :])
        return 0

    lax.fori_loop(0, 2 * (deep // tile), back, 0)
    loads[3].wait()
    u_near.wait_recv()
    for copy in u_side:
        copy.wait_recv()
    keep(wup, wup_out)

    def forward(at, _):
        r, c = spot_of(at)
        value = matmul(normed[r, :], wup[:, c]) + up_bias_ref[member, :, c]
        hidden[r, c] = gelu_value(value).astype(BF16)
        du[r, c] = (dh[r, c] * gelu_slope(value)).astype(BF16)
        return 0

    lax.fori_loop(0, 2 * (deep // tile), forward, 0)
    keep(hidden, hidden_out)
    keep(du, du_out)
    for copy in arrivals:
        copy.wait_recv()
    for copy in started:
        copy.wait_send()
    for copy in stores:
        copy.wait()


def begin_layer(
    x, gain, shift, cot, qkv_w, qkv_b, up_w, up_b, out_w, down_w, cosine, sine,
    shards, groups, pairs, slot_groups, items, dup,
):
    rows, width = x.shape
    wide = width // groups
    deep = up_w.shape[1] // groups
    total = rows * groups
    whole = pl.BlockSpec(memory_space=pltpu.VMEM)
    apart = pl.BlockSpec(memory_space=pl.ANY)
    dma = pltpu.SemaphoreType.DMA
    shape = jax.ShapeDtypeStruct
    stores = items + 1 + 6
    return pl.pallas_call(
        partial(start_kernel, shards, groups, pairs, slot_groups, items, dup),
        out_shape=[
            shape((total, width), BF16),
            shape((total, width), BF16),
            shape((width, 3 * wide), BF16),
            shape((width, deep), BF16),
            shape((total, deep), BF16),
            shape((total, deep), BF16),
            shape((items, shards, 3, rows, LANES), BF16),
            shape((shards, items, rows, LANES), BF16),
        ],
        in_specs=[whole, whole, whole, apart, apart, whole, apart, whole, apart, apart, apart, apart],
        out_specs=[apart] * 8,
        scratch_shapes=[
            pltpu.VMEM((total, width), BF16),
            pltpu.VMEM((total, width), BF16),
            pltpu.VMEM((width, 3 * wide), BF16),
            pltpu.VMEM((width, deep), BF16),
            pltpu.VMEM((deep, width), BF16),
            pltpu.VMEM((wide, width), BF16),
            pltpu.VMEM((rows, LANES), F32),
            pltpu.VMEM((rows, LANES), F32),
            pltpu.VMEM((items, pairs, slot_groups, 3, rows, LANES), BF16),
            pltpu.VMEM((pairs, slot_groups, items, rows, LANES), BF16),
            pltpu.VMEM((total, deep), F32),
            pltpu.VMEM((total, deep), BF16),
            pltpu.VMEM((total, deep), BF16),
            dma((11,)),
            dma((stores,)),
            dma((15,)),
            dma((15,)),
            dma((5,)),
            dma((5,)),
            dma((6,)),
            dma((6,)),
            dma((items * shards,)),
            dma((items * shards,)),
            dma((shards,)),
            dma((shards,)),
        ],
        compiler_params=pltpu.CompilerParams(
            collective_id=0, has_side_effects=True, vmem_limit_bytes=62 * 2**20
        ),
        cost_estimate=pl.CostEstimate(
            flops=2 * total * width * (3 * wide + wide + 2 * deep),
            bytes_accessed=60 * 2**20,
            transcendentals=total * deep,
        ),
    )(
        x,
        gain.reshape(1, width),
        shift.reshape(1, width),
        cot,
        qkv_w,
        qkv_b.reshape(3 * groups, 1, wide),
        up_w,
        up_b.reshape(groups, 1, deep),
        out_w,
        down_w,
        cosine,
        sine,
    )


def attend_kernel(
    shards, heads, dup, qkv_ref, do_ref, cos_ref, sin_ref, out_ref, s_buf, dp_buf, dk_buf, dv_buf
):
    half = qkv_ref.shape[-2]
    block = 2 * half
    count = shards
    base = lax.axis_index("ctx") % dup
    lane = lax.broadcasted_iota(jnp.int32, (block, LANES), 1) // HD
    own = [lane == (base + h) for h in range(heads)]
    scale = HD**-0.5

    def where_is(item):
        low = item < count // 2
        first = jnp.where(low, 2 * item, 2 * count - 1 - 2 * item)
        second = jnp.where(low, 2 * item + 1, 2 * count - 2 - 2 * item)
        return first, second, jnp.where(low, 0, 1)

    def load(part, item):
        first, second, side = where_is(item)
        return jnp.concatenate(
            [qkv_ref[0, first, part, side], qkv_ref[0, second, part, side]], axis=0
        )

    def load_do(item):
        first, second, side = where_is(item)
        return jnp.concatenate([do_ref[first, 0, side], do_ref[second, 0, side]], axis=0)

    def store(part, item, value):
        first, second, side = where_is(item)
        out_ref[first, 0, part, side] = value[:half].astype(out_ref.dtype)
        out_ref[second, 0, part, side] = value[half:].astype(out_ref.dtype)

    dk_buf[...] = jnp.zeros_like(dk_buf)
    dv_buf[...] = jnp.zeros_like(dv_buf)
    nothing = jnp.zeros((block, LANES), BF16)
    key_at = lax.broadcasted_iota(jnp.int32, (block, block), 0)
    query_at = lax.broadcasted_iota(jnp.int32, (block, block), 1)

    def per_query(item, _):
        query = load(0, item) * jnp.asarray(scale, BF16)
        grad = load_do(item)
        queries = [jnp.where(own[h], query, nothing) for h in range(heads)]
        grads = [jnp.where(own[h], grad, nothing) for h in range(heads)]

        def measure(key_item, state, diagonal):
            keys, values = load(1, key_item), load(2, key_item)
            new = []
            for h in range(heads):
                top, total, dot = state[h]
                s = contract_cols(keys, queries[h])
                if diagonal:
                    s = jnp.where(key_at <= query_at, s, -1e30)
                dp = contract_cols(values, grads[h])
                s_buf[h, key_item] = s
                dp_buf[h, key_item] = dp
                new_top = jnp.maximum(top, jnp.max(s, axis=0, keepdims=True))
                e = jnp.exp(s - new_top)
                fade = jnp.exp(top - new_top)
                new.append(
                    (
                        new_top,
                        total * fade + jnp.sum(e, axis=0, keepdims=True),
                        dot * fade + jnp.sum(e * dp, axis=0, keepdims=True),
                    )
                )
            return tuple(new)

        zero = jnp.zeros((1, block), F32)
        start = tuple((zero - 1e30, zero, zero) for _ in range(heads))
        state = lax.fori_loop(0, item, lambda k, st: measure(k, st, False), start)
        state = measure(item, state, True)
        logs = [top + jnp.log(total) for top, total, _ in state]
        deltas = [dot / total for _, total, dot in state]

        def apply(key_item, state):
            keys, values = load(1, key_item), load(2, key_item)
            out, dq = state
            dk, dv = dk_buf[key_item], dv_buf[key_item]
            for h in range(heads):
                p = jnp.exp(s_buf[h, key_item] - logs[h])
                ds = (p * (dp_buf[h, key_item] - deltas[h])).astype(BF16)
                p = p.astype(BF16)
                dv = dv + matmul(p, grads[h])
                dk = dk + matmul(ds, queries[h])
                out = out + jnp.where(own[h], contract_rows(p, values), 0.0)
                dq = dq + jnp.where(own[h], contract_rows(ds, keys), 0.0)
            dk_buf[key_item] = dk
            dv_buf[key_item] = dv
            return out, dq

        empty = jnp.zeros((block, LANES), F32)
        out, dq = lax.fori_loop(0, item + 1, apply, (empty, empty))
        store(0, item, out)
        rows = pl.ds(pl.multiple_of(item * block, block), block)
        store(1, item, turn(dq * scale, cos_ref[rows, :], -sin_ref[rows, :]))
        return 0

    lax.fori_loop(0, count, per_query, 0)

    def finish(item, _):
        rows = pl.ds(pl.multiple_of(item * block, block), block)
        store(2, item, turn(dk_buf[item], cos_ref[rows, :], -sin_ref[rows, :]))
        store(3, item, dv_buf[item])
        return 0

    lax.fori_loop(0, count, finish, 0)


def attend(qkv, grads, item, cosine, sine, heads, dup):
    shards, items = qkv.shape[1], 1
    half = qkv.shape[-2]
    tokens = shards * 2 * half
    block = 2 * half
    once = pl.Buffered(1)
    pairs = shards * (shards + 1) // 2 * items * heads
    return pl.pallas_call(
        partial(attend_kernel, shards, heads, dup),
        grid=(items,),
        out_shape=jax.ShapeDtypeStruct((shards, items, 4, 2, half, LANES), BF16),
        in_specs=[
            pl.BlockSpec(
                (1, shards, 3, 2, half, LANES), lambda i: (item, 0, 0, 0, 0, 0), pipeline_mode=once
            ),
            pl.BlockSpec(
                (shards, 1, 2, half, LANES), lambda i: (0, item, 0, 0, 0), pipeline_mode=once
            ),
            pl.BlockSpec((tokens, LANES), lambda i: (0, 0), pipeline_mode=once),
            pl.BlockSpec((tokens, LANES), lambda i: (0, 0), pipeline_mode=once),
        ],
        out_specs=pl.BlockSpec(
            (shards, 1, 4, 2, half, LANES), lambda i: (0, i, 0, 0, 0, 0), pipeline_mode=once
        ),
        scratch_shapes=[
            pltpu.VMEM((heads, shards, block, block), F32),
            pltpu.VMEM((heads, shards, block, block), F32),
            pltpu.VMEM((shards, block, LANES), F32),
            pltpu.VMEM((shards, block, LANES), F32),
        ],
        compiler_params=pltpu.CompilerParams(vmem_limit_bytes=58 * 2**20),
        cost_estimate=pl.CostEstimate(
            flops=pairs * 5 * 2 * block * block * 256,
            bytes_accessed=16 * 2**20,
            transcendentals=2 * pairs * block * block,
        ),
    )(qkv, grads, cosine, sine)


def middle_kernel(
    items,
    heads,
    qkv_in,
    do_in,
    hidden_in,
    normed_in,
    grads_in,
    du_in,
    cos_in,
    sin_in,
    back_in,
    down_out,
    up_out,
    d_send,
    d_keep,
    d_recv,
    d_last,
    u_send,
    u_keep,
    u_recv,
    u_last,
    out,
    local_sem,
    store_sem,
    own_sem,
    ds_,
    dr,
    us,
    ur,
    bs,
    br,
):
    place = lax.axis_index("ctx")
    shards = out.shape[1]
    x_at, z_at = place % 2, (place // 2) % 2
    near, over = {"ctx": place ^ 1}, {"ctx": place ^ 2}
    barrier = pltpu.get_barrier_semaphore()
    for k in range(1, shards):
        pl.semaphore_signal(
            barrier, inc=1, device_id={"ctx": place ^ k}, device_id_type=pl.DeviceIdType.MESH
        )

    def fetch(src, dst, at):
        copy = pltpu.make_async_copy(src, dst, local_sem.at[at])
        copy.start()
        return copy

    def block(at, size):
        return pl.ds(pl.multiple_of(at, size), size)

    members, tops, lanes, width = u_send.shape
    wide = lanes * 2 * tops
    units = d_send.shape[2]
    piece = lanes // 2

    def down_one(top):
        return remote(d_send.at[top], d_recv.at[top], ds_, dr, top, near)

    def down_two(top):
        return remote(d_send.at[top, 0], d_last.at[top], ds_, dr, tops + top, over)

    def up_one(member):
        return remote(u_send.at[member], u_recv.at[member], us, ur, member, over)

    def up_two(member):
        return remote(
            u_send.at[member, :, pl.ds(0, piece)], u_last.at[member], us, ur, members + member, near
        )

    def back_one(item, part, k):
        return remote(
            out.at[item, place ^ k, :, part],
            back_in.at[item, place, :, part],
            bs,
            br,
            (item * 2 + part) * shards + k,
            {"ctx": place ^ k},
        )

    def back_own(item, part):
        return pltpu.make_async_copy(
            out.at[item, place, :, part],
            back_in.at[item, place, :, part],
            own_sem.at[item * 2 + part],
        )

    def sums(hidden, normed, grads, du):
        loads = [
            fetch(src, dst, at)
            for at, (src, dst) in enumerate(
                ((hidden_in, hidden), (grads_in, grads), (normed_in, normed), (du_in, du))
            )
        ]
        loads[0].wait()
        loads[1].wait()
        pl.semaphore_wait(barrier, shards - 1)

        def down(which, into, top):
            def one(low, _):
                at = ((top * 2 + low) * 2 + which) * units
                into[top, low] = contract_rows(hidden[:, block(at, units)], grads[...]).astype(BF16)
                return 0

            lax.fori_loop(0, 2, one, 0)

        for top in range(tops):
            down(1 - x_at, d_send, top)
            down_one(top).start()
        loads[2].wait()
        loads[3].wait()

        def up(which, into, member):
            def one(top, _):
                at = member * wide + (top * 2 + which) * lanes
                into[member, top] = contract_rows(normed[:, block(at, lanes)], du[...]).astype(BF16)
                return 0

            lax.fori_loop(0, tops, one, 0)

        for member in range(members):
            up(1 - z_at, u_send, member)
            up_one(member).start()
        for top in range(tops):
            down(x_at, d_keep, top)
        for member in range(members):
            up(z_at, u_keep, member)

    tokens = hidden_in.shape[0]
    pl.run_scoped(
        sums,
        pltpu.VMEM(hidden_in.shape, BF16),
        pltpu.VMEM((tokens, width), BF16),
        pltpu.VMEM((tokens, width), BF16),
        pltpu.VMEM(du_in.shape, BF16),
    )

    half = out.shape[-2]
    size = 2 * half

    def attention(qkv, do, cosine, sine, s_buf, dp_buf, dk_buf, dv_buf):
        loads = []
        for item in range(items):
            loads.append(fetch(qkv_in.at[item], qkv.at[item], 2 * item))
            loads.append(fetch(do_in.at[:, item], do.at[item], 2 * item + 1))
        loads.append(fetch(cos_in, cosine, 2 * items))
        loads.append(fetch(sin_in, sine, 2 * items + 1))
        for load in loads:
            load.wait()
        lane = lax.broadcasted_iota(jnp.int32, (size, LANES), 1) // HD
        own = [lane == h for h in range(heads)]
        key_at = lax.broadcasted_iota(jnp.int32, (size, size), 0)
        query_at = lax.broadcasted_iota(jnp.int32, (size, size), 1)
        nothing = jnp.zeros((size, LANES), BF16)
        scale = HD**-0.5

        for item in range(items):
            dk_buf[...] = jnp.zeros_like(dk_buf)
            dv_buf[...] = jnp.zeros_like(dv_buf)
            for part in (1, 0):

                def where_is(at, part=part):
                    if part:
                        return 2 * shards - 1 - 2 * at, 2 * shards - 2 - 2 * at
                    return 2 * at, 2 * at + 1

                def shard_of(at):
                    low = at < shards // 2
                    first = jnp.where(low, 2 * at, 2 * shards - 1 - 2 * at)
                    second = jnp.where(low, 2 * at + 1, 2 * shards - 2 - 2 * at)
                    return first, second, jnp.where(low, 0, 1)

                def load(which, at, item=item):
                    first, second, side = shard_of(at)
                    return jnp.concatenate(
                        [qkv[item, first, which, side], qkv[item, second, which, side]], axis=0
                    )

                def store(which, at, value, item=item, part=part, where_is=where_is):
                    first, second = where_is(at)
                    out[item, first, which, part] = value[:half].astype(BF16)
                    out[item, second, which, part] = value[half:].astype(BF16)

                def per_query(at, _, item=item, load=load, store=store, shard_of=shard_of):
                    query = load(0, at) * jnp.asarray(scale, BF16)
                    first, second, where = shard_of(at)
                    grad = jnp.concatenate([do[item, first, where], do[item, second, where]], axis=0)
                    queries = [jnp.where(own[h], query, nothing) for h in range(heads)]
                    grads = [jnp.where(own[h], grad, nothing) for h in range(heads)]

                    def measure(key, state, diagonal):
                        keys, values = load(1, key), load(2, key)
                        new = []
                        for h in range(heads):
                            top, total, dot = state[h]
                            s = contract_cols(keys, queries[h])
                            if diagonal:
                                s = jnp.where(key_at <= query_at, s, -1e30)
                            dp = contract_cols(values, grads[h])
                            s_buf[h, key] = s
                            dp_buf[h, key] = dp
                            new_top = jnp.maximum(top, jnp.max(s, axis=0, keepdims=True))
                            e = jnp.exp(s - new_top)
                            fade = jnp.exp(top - new_top)
                            new.append(
                                (
                                    new_top,
                                    total * fade + jnp.sum(e, axis=0, keepdims=True),
                                    dot * fade + jnp.sum(e * dp, axis=0, keepdims=True),
                                )
                            )
                        return tuple(new)

                    zero = jnp.zeros((1, size), F32)
                    start = tuple((zero - 1e30, zero, zero) for _ in range(heads))
                    state = lax.fori_loop(0, at, lambda k, st: measure(k, st, False), start)
                    state = measure(at, state, True)
                    logs = [top + jnp.log(total) for top, total, _ in state]
                    deltas = [dot / total for _, total, dot in state]

                    def apply(key, state):
                        keys, values = load(1, key), load(2, key)
                        attended, dq = state
                        dk, dv = dk_buf[key], dv_buf[key]
                        for h in range(heads):
                            p = jnp.exp(s_buf[h, key] - logs[h])
                            ds = (p * (dp_buf[h, key] - deltas[h])).astype(BF16)
                            p = p.astype(BF16)
                            dv = dv + matmul(p, grads[h])
                            dk = dk + matmul(ds, queries[h])
                            attended = attended + jnp.where(own[h], contract_rows(p, values), 0.0)
                            dq = dq + jnp.where(own[h], contract_rows(ds, keys), 0.0)
                        dk_buf[key] = dk
                        dv_buf[key] = dv
                        return attended, dq

                    empty = jnp.zeros((size, LANES), F32)
                    attended, dq = lax.fori_loop(0, at + 1, apply, (empty, empty))
                    store(0, at, attended)
                    rows = block(at * size, size)
                    store(1, at, turn(dq * scale, cosine[rows, :], -sine[rows, :]))
                    return 0

                low = part * (shards // 2)
                lax.fori_loop(low, low + shards // 2, per_query, 0)

                def finish(at, _, store=store):
                    rows = block(at * size, size)
                    store(2, at, turn(dk_buf[at], cosine[rows, :], -sine[rows, :]))
                    store(3, at, dv_buf[at])
                    return 0

                lax.fori_loop(low, low + shards // 2, finish, 0)
                for k in range(1, shards):
                    back_one(item, part, k).start()
                back_own(item, part).start()

    pl.run_scoped(
        attention,
        pltpu.VMEM((items,) + qkv_in.shape[1:], BF16),
        pltpu.VMEM((items, shards) + do_in.shape[2:], BF16),
        pltpu.VMEM(cos_in.shape, F32),
        pltpu.VMEM(sin_in.shape, F32),
        pltpu.VMEM((heads, shards, size, size), F32),
        pltpu.VMEM((heads, shards, size, size), F32),
        pltpu.VMEM((shards, size, LANES), F32),
        pltpu.VMEM((shards, size, LANES), F32),
    )

    for top in range(tops):
        down_one(top).wait()
    for top in range(tops):
        d_send[top, 0] = (
            d_keep[top, 1 - z_at].astype(F32) + d_recv[top, 1 - z_at].astype(F32)
        ).astype(BF16)
        down_two(top).start()
    theirs = block((1 - x_at) * piece, piece)
    mine = block(x_at * piece, piece)
    for member in range(members):
        up_one(member).wait()
    for member in range(members):
        for top in range(tops):
            u_send[member, top, pl.ds(0, piece)] = (
                u_keep[member, top, theirs].astype(F32) + u_recv[member, top, theirs].astype(F32)
            ).astype(BF16)
        up_two(member).start()
    stores = []
    for top in range(tops):
        d_keep[top, z_at] = (
            d_keep[top, z_at].astype(F32) + d_recv[top, z_at].astype(F32)
        ).astype(BF16)
    for member in range(members):
        for top in range(tops):
            u_keep[member, top, mine] = (
                u_keep[member, top, mine].astype(F32) + u_recv[member, top, mine].astype(F32)
            ).astype(BF16)
    for top in range(tops):
        down_two(top).wait_recv()
        d_last[top] = (d_keep[top, z_at].astype(F32) + d_last[top].astype(F32)).astype(BF16)
        stores.append(pltpu.make_async_copy(d_last.at[top], down_out.at[top], store_sem.at[top]))
        stores[-1].start()
    for member in range(members):
        up_two(member).wait_recv()
        for top in range(tops):
            u_last[member, top] = (
                u_keep[member, top, mine].astype(F32) + u_last[member, top].astype(F32)
            ).astype(BF16)
        stores.append(
            pltpu.make_async_copy(u_last.at[member], up_out.at[member], store_sem.at[tops + member])
        )
        stores[-1].start()
    for item in range(items):
        for part in (1, 0):
            for k in range(1, shards):
                back_one(item, part, k).wait()
            back_own(item, part).wait()
    for top in range(tops):
        down_two(top).wait_send()
    for member in range(members):
        up_two(member).wait_send()
    for copy in stores:
        copy.wait()


def middle(qkv_in, do_in, hidden, normed, grads, du, cosine, sine, heads, groups):
    items, shards = qkv_in.shape[:2]
    half = qkv_in.shape[-2]
    width = normed.shape[1]
    deep = hidden.shape[1]
    units = deep // shards
    tops = shards // 4
    lanes = width // groups // tops // 2
    apart = pl.BlockSpec(memory_space=pl.ANY)
    dma = pltpu.SemaphoreType.DMA
    shape = jax.ShapeDtypeStruct
    pairs = shards * (shards + 1) // 2 * items * heads
    return pl.pallas_call(
        partial(middle_kernel, items, heads),
        out_shape=[
            shape((items, shards, 4, 2, half, LANES), BF16),
            shape((tops, units, width), BF16),
            shape((groups, tops, lanes // 2, deep), BF16),
        ],
        in_specs=[apart] * 8,
        out_specs=[apart] * 3,
        scratch_shapes=[
            pltpu.VMEM((tops, 2, units, width), BF16),
            pltpu.VMEM((tops, 2, units, width), BF16),
            pltpu.VMEM((tops, 2, units, width), BF16),
            pltpu.VMEM((tops, units, width), BF16),
            pltpu.VMEM((groups, tops, lanes, deep), BF16),
            pltpu.VMEM((groups, tops, lanes, deep), BF16),
            pltpu.VMEM((groups, tops, lanes, deep), BF16),
            pltpu.VMEM((groups, tops, lanes // 2, deep), BF16),
            pltpu.VMEM((items, shards, 4, 2, half, LANES), BF16),
            dma((max(4, 2 * items + 2),)),
            dma((tops + groups,)),
            dma((2 * items,)),
            dma((2 * tops,)),
            dma((2 * tops,)),
            dma((2 * groups,)),
            dma((2 * groups,)),
            dma((2 * items * shards,)),
            dma((2 * items * shards,)),
        ],
        compiler_params=pltpu.CompilerParams(
            collective_id=1, has_side_effects=True, vmem_limit_bytes=63 * 2**20
        ),
        cost_estimate=pl.CostEstimate(
            flops=pairs * 10 * (2 * half) ** 2 * 256 + 8 * width * deep * hidden.shape[0],
            bytes_accessed=40 * 2**20,
            transcendentals=2 * pairs * (2 * half) ** 2,
        ),
    )(qkv_in, do_in, hidden, normed, grads, du, cosine, sine)


def scatter_sum(parts, axis_at, place, bits):
    lead, tail = parts.shape[:axis_at], parts.shape[axis_at + 1 :]
    total = len(bits)
    left = list(range(total - 1, -1, -1))
    value = parts.reshape(lead + (2,) * total + tail)
    for bit in bits:
        at = axis_at + left.index(bit)
        left.remove(bit)
        mine = (place >> bit) & 1
        send = lax.dynamic_index_in_dim(value, 1 - mine, at, keepdims=False)
        keep = lax.dynamic_index_in_dim(value, mine, at, keepdims=False)
        got = swap(send.astype(BF16), "ctx", 1 << bit)
        value = keep.astype(F32) + got.astype(F32)
    return value


def last_half(value, axis_at, place):
    mine = (place // 4) % 2
    send = lax.dynamic_index_in_dim(value, 1 - mine, axis_at, keepdims=False)
    keep = lax.dynamic_index_in_dim(value, mine, axis_at, keepdims=False)
    return keep.astype(F32) + swap(send, "ctx", 4).astype(F32)


def scatter_rows(parts):
    last = swap(parts[3].astype(BF16), "fsdp", 1).astype(F32)
    far = swap((parts[2] + last).astype(BF16), "fsdp", 2).astype(F32)
    near = swap(parts[1].astype(BF16), "fsdp", 1).astype(F32)
    return parts[0] + near + far


def total_sum(value):
    for axis in ("fsdp", "ctx"):
        bit = 1
        while bit < lax.axis_size(axis):
            value = value + swap(value, axis, bit)
            bit *= 2
    return value


def on_device(
    inputs,
    norm_gain,
    norm_shift,
    qkv_weight,
    qkv_bias,
    out_weight,
    out_bias,
    up_weight,
    up_bias,
    down_weight,
    down_bias,
    cotangent,
):
    rows = inputs.shape[1]
    width = inputs.shape[2]
    hidden_width = up_weight.shape[1]
    half = rows // 2
    shards = lax.axis_size("ctx")
    groups = lax.axis_size("fsdp")
    place = lax.axis_index("ctx")
    member = lax.axis_index("fsdp")
    wide = width // groups
    deep = hidden_width // groups
    x_first = list(range(shards.bit_length() - 1))
    z_first = x_first[1:2] + x_first[:1] + x_first[2:]

    tokens = inputs[0].astype(F32)
    mean = jnp.mean(tokens, axis=-1, keepdims=True)
    centred = tokens - mean
    inv_scale = lax.rsqrt(jnp.mean(centred * centred, axis=-1, keepdims=True) + EPS)
    normal = centred * inv_scale
    grad_low = cotangent[0]
    grad_full = grad_low.astype(F32)

    pairs = wide // LANES
    heads_in_pair = LANES // HD
    units = pairs * groups
    dup = max(1, shards // units)
    slot_groups = shards // (pairs * dup)
    per_group = groups // slot_groups
    heads = heads_in_pair // dup

    cos_full, sin_full = rotary(shards * rows)
    normed, grads, qkv_own, up_own, hidden, grad_up, qkv_in, grad_in = begin_layer(
        inputs[0],
        norm_gain,
        norm_shift,
        grad_low,
        qkv_weight,
        qkv_bias,
        up_weight,
        up_bias,
        out_weight,
        down_weight,
        cos_full,
        sin_full,
        shards,
        groups,
        pairs,
        slot_groups,
        per_group,
        dup,
    )

    def assembled(back):
        back = back.reshape(pairs, slot_groups, dup, 4, rows, LANES)
        back = jnp.sum(back, axis=2) if dup > 1 else back[:, :, 0]
        return back.transpose(2, 1, 3, 0, 4).reshape(4, slot_groups * rows, wide)

    hw = deep // shards
    if len(x_first) == 3 and dup == 1:
        back_in, down_sum, up_sum = middle(
            qkv_in.reshape(per_group, shards, 3, 2, half, LANES),
            grad_in.reshape(shards, per_group, 2, half, LANES),
            hidden,
            normed,
            grads,
            grad_up,
            cos_full,
            sin_full,
            heads,
            groups,
        )
        backs = [assembled(back_in[item]) for item in range(per_group)]
        down_weight_grad = last_half(down_sum, 0, place)
        up_part = last_half(up_sum, 1, place)
    else:
        down_grad = contract_rows(hidden, grads).astype(BF16)
        up_grad = contract_rows(normed, grad_up).astype(BF16)
        down_weight_grad = scatter_sum(
            down_grad.reshape(shards, hw, width), 0, place, x_first
        )
        up_part = scatter_sum(
            up_grad.reshape(groups, shards, wide // shards, deep), 1, place, z_first
        )

        backs = []
        for item in range(per_group):
            back = attend(
                qkv_in.reshape(per_group, shards, 3, 2, half, LANES),
                grad_in.reshape(shards, per_group, 2, half, LANES),
                item,
                cos_full,
                sin_full,
                heads,
                dup,
            )
            back = lax.all_to_all(back, "ctx", 0, 0)
            back = back.reshape(pairs, slot_groups, dup, 4, rows, LANES)
            back = jnp.sum(back, axis=2) if dup > 1 else back[:, :, 0]
            backs.append(back.transpose(2, 1, 3, 0, 4).reshape(4, slot_groups * rows, wide))
        back = jnp.concatenate(backs, axis=1)
        attended = back[0]
        grad_qkv = jnp.concatenate([back[1], back[2], back[3]], axis=1)

        share = matmul(hidden, down_weight) + matmul(attended, out_weight)
        result = tokens + scatter_rows(list(share.reshape(groups, rows, width))) + out_bias + down_bias

        grad_share = contract_cols(grad_up, up_own) + contract_cols(grad_qkv, qkv_own)
        grad_normed = scatter_rows(list(grad_share.reshape(groups, rows, width)))
        grad_full = grad_low.astype(F32)
        grad_normal = grad_normed * norm_gain
        grad_tokens = inv_scale * (
            grad_normal
            - jnp.mean(grad_normal, axis=-1, keepdims=True)
            - normal * jnp.mean(grad_normal * normal, axis=-1, keepdims=True)
        )
        input_grad = (grad_full + grad_tokens).astype(BF16)

        qkv_grad = contract_rows(normed, grad_qkv).astype(BF16)
        out_grad = contract_rows(attended, grads).astype(BF16)
        ow = wide // shards
        out_weight_grad = scatter_sum(out_grad.reshape(shards, ow, width), 0, place, z_first)
        qkv_part = scatter_sum(
            qkv_grad.reshape(groups, shards, ow, 3 * wide), 1, place, x_first
        )

        def relative(value):
            return [
                lax.dynamic_index_in_dim(value, member ^ j, 0, keepdims=False) for j in range(groups)
            ]

        def exchange(part):
            sent = relative(part.astype(BF16))
            got = [sent[0]] + [swap(sent[j], "fsdp", j) for j in range(1, groups)]
            return relative(jnp.stack(got))

        up_weight_grad = jnp.concatenate(exchange(up_part), axis=1).astype(F32)
        qkv_weight_grad = jnp.concatenate(
            [item.reshape(ow, 3, 1, wide) for item in exchange(qkv_part)], axis=2
        ).reshape(ow, 3 * width).astype(F32)

        qkv_bias_cols = jnp.sum(grad_qkv.astype(F32), axis=0).reshape(3, 1, wide)
        backs = []
        for item in range(per_group):
            back = attend(
                qkv_in.reshape(per_group, shards, 3, 2, half, LANES),
                grad_in.reshape(shards, per_group, 2, half, LANES),
                item,
                cos_full,
                sin_full,
                heads,
                dup,
            )
            back = lax.all_to_all(back, "ctx", 0, 0)
            backs.append(assembled(back))
    back = jnp.concatenate(backs, axis=1)
    attended = back[0]
    grad_qkv = jnp.concatenate([back[1], back[2], back[3]], axis=1)

    share = matmul(hidden, down_weight) + matmul(attended, out_weight)
    result = tokens + scatter_rows(list(share.reshape(groups, rows, width))) + out_bias + down_bias

    grad_share = contract_cols(grad_up, up_own) + contract_cols(grad_qkv, qkv_own)
    grad_normed = scatter_rows(list(grad_share.reshape(groups, rows, width)))
    grad_full = grad_low.astype(F32)
    grad_normal = grad_normed * norm_gain
    grad_tokens = inv_scale * (
        grad_normal
        - jnp.mean(grad_normal, axis=-1, keepdims=True)
        - normal * jnp.mean(grad_normal * normal, axis=-1, keepdims=True)
    )
    input_grad = (grad_full + grad_tokens).astype(BF16)

    qkv_grad = contract_rows(normed, grad_qkv).astype(BF16)
    out_grad = contract_rows(attended, grads).astype(BF16)
    ow = wide // shards
    out_weight_grad = scatter_sum(out_grad.reshape(shards, ow, width), 0, place, z_first)
    qkv_part = scatter_sum(
        qkv_grad.reshape(groups, shards, ow, 3 * wide), 1, place, x_first
    )

    def relative(value):
        return [
            lax.dynamic_index_in_dim(value, member ^ j, 0, keepdims=False) for j in range(groups)
        ]

    def exchange(part):
        sent = relative(part.astype(BF16))
        got = [sent[0]] + [swap(sent[j], "fsdp", j) for j in range(1, groups)]
        return relative(jnp.stack(got))

    up_weight_grad = jnp.concatenate(exchange(up_part), axis=1).astype(F32)
    qkv_weight_grad = jnp.concatenate(
        [item.reshape(ow, 3, 1, wide) for item in exchange(qkv_part)], axis=2
    ).reshape(ow, 3 * width).astype(F32)

    qkv_bias_cols = jnp.sum(grad_qkv.astype(F32), axis=0).reshape(3, 1, wide)
    up_bias_cols = jnp.sum(grad_up.astype(F32), axis=0).reshape(1, deep)
    qkv_bias_all = lax.dynamic_update_slice(
        jnp.zeros((3, groups, wide), F32), qkv_bias_cols, (0, member, 0)
    ).reshape(-1)
    up_bias_all = lax.dynamic_update_slice(
        jnp.zeros((groups, deep), F32), up_bias_cols, (member, 0)
    ).reshape(-1)
    early = total_sum(jnp.concatenate([jnp.sum(grad_full, axis=0), up_bias_all]))
    late = total_sum(
        jnp.concatenate(
            [jnp.sum(grad_normed * normal, axis=0), jnp.sum(grad_normed, axis=0), qkv_bias_all]
        )
    )
    out_bias_grad, up_bias_grad = early[:width], early[width:]
    gain_grad, shift_grad, qkv_bias_grad = late[:width], late[width : 2 * width], late[2 * width :]
    return (
        result.astype(BF16)[None],
        input_grad[None],
        gain_grad,
        shift_grad,
        qkv_weight_grad,
        qkv_bias_grad,
        out_weight_grad,
        out_bias_grad,
        up_weight_grad,
        up_bias_grad,
        down_weight_grad,
        out_bias_grad,
    )


def solution(mesh):
    in_specs = (
        P("fsdp", "ctx", None),
        P(),
        P(),
        P("fsdp", None),
        P(),
        P("fsdp", None),
        P(),
        P("fsdp", None),
        P(),
        P("fsdp", None),
        P(),
        P("fsdp", "ctx", None),
    )
    out_specs = (
        P("fsdp", "ctx", None),
        P("fsdp", "ctx", None),
        P(),
        P(),
        P(("fsdp", "ctx"), None),
        P(),
        P(("fsdp", "ctx"), None),
        P(),
        P(("fsdp", "ctx"), None),
        P(),
        P(("fsdp", "ctx"), None),
        P(),
    )
    return jax.shard_map(
        on_device, mesh=mesh, in_specs=in_specs, out_specs=out_specs, check_vma=False
    )
```

```python
from functools import partial

import jax
import jax.numpy as jnp
import numpy as np
from jax import lax
from jax.experimental import pallas as pl
from jax.experimental.pallas import tpu as pltpu
from jax.sharding import PartitionSpec as P

HD = 64
ROT = 32
LANES = 128

EPS = 1e-05
ROOT = 0.7978845608028654
CUBIC = 0.044715
F32 = jnp.float32
BF16 = jnp.bfloat16


def gelu_value(value):
    return 0.5 * value * (1.0 + jnp.tanh(ROOT * (value + CUBIC * value * value * value)))


def gelu_slope(value):
    tangent = jnp.tanh(ROOT * (value + CUBIC * value * value * value))
    return 0.5 * (1.0 + tangent) + 0.5 * value * (1.0 - tangent * tangent) * ROOT * (
        1.0 + 3.0 * CUBIC * value * value
    )


def contract_rows(left, right):
    return lax.dot_general(left, right, (((0,), (0,)), ((), ())), preferred_element_type=F32)


def contract_cols(left, right):
    return lax.dot_general(left, right, (((1,), (1,)), ((), ())), preferred_element_type=F32)


def matmul(left, right):
    return jnp.dot(left, right, preferred_element_type=F32)


def swap(value, axis, bit):
    size = lax.axis_size(axis)
    return lax.ppermute(value, axis, [(i, i ^ bit) for i in range(size)])


def after(value, *events):
    return lax.optimization_barrier((value,) + events)[0]


def rotary(length):
    quarter = ROT // 2
    inverse = np.float32(10000.0) ** (-np.arange(quarter, dtype=np.float32) * 2.0 / ROT)
    angle = np.arange(length, dtype=np.float32)[:, None] * inverse.astype(np.float32)[None, :]
    cosine, sine = np.cos(angle), np.sin(angle)
    one = np.concatenate([cosine, cosine, np.ones((length, HD - ROT))], axis=1)
    two = np.concatenate([-sine, sine, np.zeros((length, HD - ROT))], axis=1)
    copies = (1, LANES // HD)
    return (
        jnp.asarray(np.tile(one, copies), F32),
        jnp.asarray(np.tile(two, copies), F32),
    )


def turn(rows, cosine, sine):
    lane = lax.broadcasted_iota(jnp.int32, rows.shape, 1) % HD
    quarter = ROT // 2
    other = jnp.where(
        lane < quarter,
        pltpu.roll(rows, LANES - quarter, 1),
        pltpu.roll(rows, quarter, 1),
    )
    return rows * cosine + other * sine


def remote(src, dst, sends, recvs, at, target):
    return pltpu.make_async_remote_copy(
        src_ref=src,
        dst_ref=dst,
        send_sem=sends.at[at],
        recv_sem=recvs.at[at],
        device_id=target,
        device_id_type=pl.DeviceIdType.MESH,
    )


def start_kernel(
    shards,
    groups,
    pairs,
    slot_groups,
    items,
    dup,
    x_ref,
    gain_ref,
    shift_ref,
    cot_ref,
    qkv_ref,
    qkv_bias_ref,
    up_ref,
    up_bias_ref,
    out_ref,
    down_ref,
    cos_ref,
    sin_ref,
    normed_out,
    grads_out,
    wqkv_out,
    wup_out,
    hidden_out,
    du_out,
    qkv_in,
    do_in,
    normed,
    grads,
    wqkv,
    wup,
    down,
    outw,
    cosine,
    sine,
    stage,
    dstage,
    dh,
    hidden,
    du,
    local_sem,
    store_sem,
    qs,
    qr,
    us,
    ur,
    rs,
    rr,
    as_,
    ar,
    ds_,
    dr,
):
    place = lax.axis_index("ctx")
    member = lax.axis_index("fsdp")
    side = place % 2
    rows, width = x_ref.shape
    half = rows // 2
    wide = width // groups
    deep = up_ref.shape[1] // groups
    part = wide // 2

    barrier = pltpu.get_barrier_semaphore()
    for j in range(1, groups):
        pl.semaphore_signal(
            barrier, inc=1, device_id={"fsdp": member ^ j}, device_id_type=pl.DeviceIdType.MESH
        )
    for k in range(1, shards):
        pl.semaphore_signal(
            barrier, inc=1, device_id={"ctx": place ^ k}, device_id_type=pl.DeviceIdType.MESH
        )

    def local(src, dst, at):
        copy = pltpu.make_async_copy(src, dst, local_sem.at[at])
        copy.start()
        return copy

    def block(at, size):
        return pl.ds(pl.multiple_of(at, size), size)

    own_rows = block(member * wide, wide)
    loads = [
        local(
            qkv_ref.at[:, block(p * width + member * wide, wide)],
            wqkv.at[own_rows, pl.ds(p * wide, wide)],
            p,
        )
        for p in range(3)
    ]
    loads.append(local(up_ref.at[:, block(member * deep, deep)], wup.at[own_rows, :], 3))
    loads.append(local(cot_ref, grads.at[pl.ds(0, rows)], 4))
    loads.append(local(out_ref, outw, 5))
    loads.append(local(down_ref, down, 6))
    upper = 2 * shards - 1 - place
    for at, (table, held) in enumerate(((cos_ref, cosine), (sin_ref, sine))):
        loads.append(
            local(table.at[block(place * half, half)], held.at[pl.ds(0, half)], 7 + 2 * at)
        )
        loads.append(
            local(table.at[block(upper * half, half)], held.at[pl.ds(half, half)], 8 + 2 * at)
        )
    pl.semaphore_wait(barrier, groups - 1 + shards - 1)

    half_rows = block(member * wide + side * part, part)
    started = []

    def begin(copy):
        copy.start()
        started.append(copy)
        return copy

    q_far = {}
    for j in (2, 3):
        for p in range(3):
            q_far[j, p] = begin(
                remote(
                    qkv_ref.at[block(side * part, part), block(p * width + (member ^ j) * wide, wide)],
                    wqkv.at[half_rows, pl.ds(p * wide, wide)],
                    qs,
                    qr,
                    (j - 2) * 3 + p,
                    {"fsdp": member ^ j},
                )
            )

    tokens = x_ref[...].astype(F32)
    centred = tokens - jnp.mean(tokens, axis=-1, keepdims=True)
    spread = lax.rsqrt(jnp.mean(centred * centred, axis=-1, keepdims=True) + EPS)
    normed[0:rows, :] = (centred * spread * gain_ref[...] + shift_ref[...]).astype(BF16)
    n_far = begin(
        remote(
            normed.at[pl.ds(0, rows)], normed.at[pl.ds(2 * rows, rows)], rs, rr, 0, {"fsdp": member ^ 2}
        )
    )
    n_near = begin(
        remote(normed.at[pl.ds(0, rows)], normed.at[pl.ds(rows, rows)], rs, rr, 1, {"fsdp": member ^ 1})
    )
    q_near = [
        begin(
            remote(
                qkv_ref.at[:, block(p * width + (member ^ 1) * wide, wide)],
                wqkv.at[own_rows, pl.ds(p * wide, wide)],
                qs,
                qr,
                6 + p,
                {"fsdp": member ^ 1},
            )
        )
        for p in range(3)
    ]

    q_side = []
    for j in (2, 3):
        for p in range(3):
            q_far[j, p].wait_recv()
            spot = wqkv.at[block((member ^ j) * wide + side * part, part), pl.ds(p * wide, wide)]
            q_side.append(
                begin(remote(spot, spot, qs, qr, 9 + (j - 2) * 3 + p, {"ctx": place ^ 1}))
            )
    n_far.wait_recv()
    n_last = begin(
        remote(
            normed.at[pl.ds(2 * rows, rows)],
            normed.at[pl.ds(3 * rows, rows)],
            rs,
            rr,
            2,
            {"fsdp": member ^ 1},
        )
    )

    loads[4].wait()
    g_far = begin(
        remote(
            grads.at[pl.ds(0, rows)], grads.at[pl.ds(2 * rows, rows)], rs, rr, 3, {"fsdp": member ^ 2}
        )
    )
    g_near = begin(
        remote(grads.at[pl.ds(0, rows)], grads.at[pl.ds(rows, rows)], rs, rr, 4, {"fsdp": member ^ 1})
    )
    u_far = [
        begin(
            remote(
                up_ref.at[block(side * part, part), block((member ^ j) * deep, deep)],
                wup.at[half_rows, :],
                us,
                ur,
                j - 2,
                {"fsdp": member ^ j},
            )
        )
        for j in (2, 3)
    ]
    u_near = begin(
        remote(
            up_ref.at[:, block((member ^ 1) * deep, deep)],
            wup.at[own_rows, :],
            us,
            ur,
            2,
            {"fsdp": member ^ 1},
        )
    )

    for at in (0, 1, 2, 7, 8, 9, 10):
        loads[at].wait()
    for copy in q_near + q_side:
        copy.wait_recv()
    n_near.wait_recv()
    arrivals = []
    stores = []

    def keep(src, dst):
        copy = pltpu.make_async_copy(src, dst, store_sem.at[len(stores)])
        copy.start()
        stores.append(copy)

    def owner(target):
        return target // (slot_groups * dup), (target // dup) % slot_groups

    for item in range(items):
        if item == items - 1:
            n_last.wait_recv()

        def project(p, _, item=item):
            for g in range(slot_groups):
                slot = item * slot_groups + g
                acc = qkv_bias_ref[p * groups + member] + jnp.dot(
                    normed[slot * rows : (slot + 1) * rows, :],
                    wqkv[:, block(p * wide, wide)],
                    preferred_element_type=F32,
                )
                for h in range(pairs):
                    cols = acc[:, h * LANES : (h + 1) * LANES]
                    turned = turn(cols, cosine[...], sine[...])
                    stage[item, h, g, p] = jnp.where(p < 2, turned, cols).astype(BF16)
            return 0

        lax.fori_loop(0, 3, project, 0)
        for k in range(1, shards):
            pair, group = owner(place ^ k)
            arrivals.append(
                begin(
                    remote(
                        stage.at[item, pair, group],
                        qkv_in.at[item, place],
                        as_,
                        ar,
                        item * shards + k,
                        {"ctx": place ^ k},
                    )
                )
            )
        pair, group = owner(place)
        keep(stage.at[item, pair, group], qkv_in.at[item, place])

    g_far.wait_recv()
    g_last = begin(
        remote(
            grads.at[pl.ds(2 * rows, rows)],
            grads.at[pl.ds(3 * rows, rows)],
            rs,
            rr,
            5,
            {"fsdp": member ^ 1},
        )
    )
    g_near.wait_recv()
    loads[5].wait()
    g_last.wait_recv()
    for slot in range(groups):
        item, g = slot // slot_groups, slot % slot_groups
        att = contract_cols(grads[slot * rows : (slot + 1) * rows, :], outw[...]).astype(BF16)
        for h in range(pairs):
            dstage[h, g, item] = att[:, h * LANES : (h + 1) * LANES]
    for k in range(1, shards):
        pair, group = owner(place ^ k)
        arrivals.append(
            begin(
                remote(
                    dstage.at[pair, group],
                    do_in.at[place],
                    ds_,
                    dr,
                    k,
                    {"ctx": place ^ k},
                )
            )
        )
    pair, group = owner(place)
    keep(dstage.at[pair, group], do_in.at[place])
    keep(normed, normed_out)
    keep(grads, grads_out)
    keep(wqkv, wqkv_out)

    u_side = []
    for j in (2, 3):
        u_far[j - 2].wait_recv()
        spot = wup.at[block((member ^ j) * wide + side * part, part), :]
        u_side.append(begin(remote(spot, spot, us, ur, 3 + j - 2, {"ctx": place ^ 1})))

    loads[6].wait()
    tile = 512
    high = 2 * rows

    def spot_of(at):
        return block((at % 2) * high, high), block((at // 2) * tile, tile)

    def back(at, _):
        r, c = spot_of(at)
        dh[r, c] = contract_cols(grads[r, :], down[c, :])
        return 0

    lax.fori_loop(0, 2 * (deep // tile), back, 0)
    loads[3].wait()
    u_near.wait_recv()
    for copy in u_side:
        copy.wait_recv()
    keep(wup, wup_out)

    def forward(at, _):
        r, c = spot_of(at)
        value = matmul(normed[r, :], wup[:, c]) + up_bias_ref[member, :, c]
        hidden[r, c] = gelu_value(value).astype(BF16)
        du[r, c] = (dh[r, c] * gelu_slope(value)).astype(BF16)
        return 0

    lax.fori_loop(0, 2 * (deep // tile), forward, 0)
    keep(hidden, hidden_out)
    keep(du, du_out)
    for copy in arrivals:
        copy.wait_recv()
    for copy in started:
        copy.wait_send()
    for copy in stores:
        copy.wait()


def begin_layer(
    x, gain, shift, cot, qkv_w, qkv_b, up_w, up_b, out_w, down_w, cosine, sine,
    shards, groups, pairs, slot_groups, items, dup,
):
    rows, width = x.shape
    wide = width // groups
    deep = up_w.shape[1] // groups
    total = rows * groups
    whole = pl.BlockSpec(memory_space=pltpu.VMEM)
    apart = pl.BlockSpec(memory_space=pl.ANY)
    dma = pltpu.SemaphoreType.DMA
    shape = jax.ShapeDtypeStruct
    stores = items + 1 + 6
    return pl.pallas_call(
        partial(start_kernel, shards, groups, pairs, slot_groups, items, dup),
        out_shape=[
            shape((total, width), BF16),
            shape((total, width), BF16),
            shape((width, 3 * wide), BF16),
            shape((width, deep), BF16),
            shape((total, deep), BF16),
            shape((total, deep), BF16),
            shape((items, shards, 3, rows, LANES), BF16),
            shape((shards, items, rows, LANES), BF16),
        ],
        in_specs=[whole, whole, whole, apart, apart, whole, apart, whole, apart, apart, apart, apart],
        out_specs=[apart] * 8,
        scratch_shapes=[
            pltpu.VMEM((total, width), BF16),
            pltpu.VMEM((total, width), BF16),
            pltpu.VMEM((width, 3 * wide), BF16),
            pltpu.VMEM((width, deep), BF16),
            pltpu.VMEM((deep, width), BF16),
            pltpu.VMEM((wide, width), BF16),
            pltpu.VMEM((rows, LANES), F32),
            pltpu.VMEM((rows, LANES), F32),
            pltpu.VMEM((items, pairs, slot_groups, 3, rows, LANES), BF16),
            pltpu.VMEM((pairs, slot_groups, items, rows, LANES), BF16),
            pltpu.VMEM((total, deep), F32),
            pltpu.VMEM((total, deep), BF16),
            pltpu.VMEM((total, deep), BF16),
            dma((11,)),
            dma((stores,)),
            dma((15,)),
            dma((15,)),
            dma((5,)),
            dma((5,)),
            dma((6,)),
            dma((6,)),
            dma((items * shards,)),
            dma((items * shards,)),
            dma((shards,)),
            dma((shards,)),
        ],
        compiler_params=pltpu.CompilerParams(
            collective_id=0, has_side_effects=True, vmem_limit_bytes=62 * 2**20
        ),
        cost_estimate=pl.CostEstimate(
            flops=2 * total * width * (3 * wide + wide + 2 * deep),
            bytes_accessed=60 * 2**20,
            transcendentals=total * deep,
        ),
    )(
        x,
        gain.reshape(1, width),
        shift.reshape(1, width),
        cot,
        qkv_w,
        qkv_b.reshape(3 * groups, 1, wide),
        up_w,
        up_b.reshape(groups, 1, deep),
        out_w,
        down_w,
        cosine,
        sine,
    )


def attend_kernel(
    shards, heads, dup, qkv_ref, do_ref, cos_ref, sin_ref, out_ref, s_buf, dp_buf, dk_buf, dv_buf
):
    half = qkv_ref.shape[-2]
    block = 2 * half
    count = shards
    base = lax.axis_index("ctx") % dup
    lane = lax.broadcasted_iota(jnp.int32, (block, LANES), 1) // HD
    own = [lane == (base + h) for h in range(heads)]
    scale = HD**-0.5

    def where_is(item):
        low = item < count // 2
        first = jnp.where(low, 2 * item, 2 * count - 1 - 2 * item)
        second = jnp.where(low, 2 * item + 1, 2 * count - 2 - 2 * item)
        return first, second, jnp.where(low, 0, 1)

    def load(part, item):
        first, second, side = where_is(item)
        return jnp.concatenate(
            [qkv_ref[0, first, part, side], qkv_ref[0, second, part, side]], axis=0
        )

    def load_do(item):
        first, second, side = where_is(item)
        return jnp.concatenate([do_ref[first, 0, side], do_ref[second, 0, side]], axis=0)

    def store(part, item, value):
        first, second, side = where_is(item)
        out_ref[first, 0, part, side] = value[:half].astype(out_ref.dtype)
        out_ref[second, 0, part, side] = value[half:].astype(out_ref.dtype)

    dk_buf[...] = jnp.zeros_like(dk_buf)
    dv_buf[...] = jnp.zeros_like(dv_buf)
    nothing = jnp.zeros((block, LANES), BF16)
    key_at = lax.broadcasted_iota(jnp.int32, (block, block), 0)
    query_at = lax.broadcasted_iota(jnp.int32, (block, block), 1)

    def per_query(item, _):
        query = load(0, item) * jnp.asarray(scale, BF16)
        grad = load_do(item)
        queries = [jnp.where(own[h], query, nothing) for h in range(heads)]
        grads = [jnp.where(own[h], grad, nothing) for h in range(heads)]

        def measure(key_item, state, diagonal):
            keys, values = load(1, key_item), load(2, key_item)
            new = []
            for h in range(heads):
                top, total, dot = state[h]
                s = contract_cols(keys, queries[h])
                if diagonal:
                    s = jnp.where(key_at <= query_at, s, -1e30)
                dp = contract_cols(values, grads[h])
                s_buf[h, key_item] = s
                dp_buf[h, key_item] = dp
                new_top = jnp.maximum(top, jnp.max(s, axis=0, keepdims=True))
                e = jnp.exp(s - new_top)
                fade = jnp.exp(top - new_top)
                new.append(
                    (
                        new_top,
                        total * fade + jnp.sum(e, axis=0, keepdims=True),
                        dot * fade + jnp.sum(e * dp, axis=0, keepdims=True),
                    )
                )
            return tuple(new)

        zero = jnp.zeros((1, block), F32)
        start = tuple((zero - 1e30, zero, zero) for _ in range(heads))
        state = lax.fori_loop(0, item, lambda k, st: measure(k, st, False), start)
        state = measure(item, state, True)
        logs = [top + jnp.log(total) for top, total, _ in state]
        deltas = [dot / total for _, total, dot in state]

        def apply(key_item, state):
            keys, values = load(1, key_item), load(2, key_item)
            out, dq = state
            dk, dv = dk_buf[key_item], dv_buf[key_item]
            for h in range(heads):
                p = jnp.exp(s_buf[h, key_item] - logs[h])
                ds = (p * (dp_buf[h, key_item] - deltas[h])).astype(BF16)
                p = p.astype(BF16)
                dv = dv + matmul(p, grads[h])
                dk = dk + matmul(ds, queries[h])
                out = out + jnp.where(own[h], contract_rows(p, values), 0.0)
                dq = dq + jnp.where(own[h], contract_rows(ds, keys), 0.0)
            dk_buf[key_item] = dk
            dv_buf[key_item] = dv
            return out, dq

        empty = jnp.zeros((block, LANES), F32)
        out, dq = lax.fori_loop(0, item + 1, apply, (empty, empty))
        store(0, item, out)
        rows = pl.ds(pl.multiple_of(item * block, block), block)
        store(1, item, turn(dq * scale, cos_ref[rows, :], -sin_ref[rows, :]))
        return 0

    lax.fori_loop(0, count, per_query, 0)

    def finish(item, _):
        rows = pl.ds(pl.multiple_of(item * block, block), block)
        store(2, item, turn(dk_buf[item], cos_ref[rows, :], -sin_ref[rows, :]))
        store(3, item, dv_buf[item])
        return 0

    lax.fori_loop(0, count, finish, 0)


def attend(qkv, grads, item, cosine, sine, heads, dup):
    shards, items = qkv.shape[1], 1
    half = qkv.shape[-2]
    tokens = shards * 2 * half
    block = 2 * half
    once = pl.Buffered(1)
    pairs = shards * (shards + 1) // 2 * items * heads
    return pl.pallas_call(
        partial(attend_kernel, shards, heads, dup),
        grid=(items,),
        out_shape=jax.ShapeDtypeStruct((shards, items, 4, 2, half, LANES), BF16),
        in_specs=[
            pl.BlockSpec(
                (1, shards, 3, 2, half, LANES), lambda i: (item, 0, 0, 0, 0, 0), pipeline_mode=once
            ),
            pl.BlockSpec(
                (shards, 1, 2, half, LANES), lambda i: (0, item, 0, 0, 0), pipeline_mode=once
            ),
            pl.BlockSpec((tokens, LANES), lambda i: (0, 0), pipeline_mode=once),
            pl.BlockSpec((tokens, LANES), lambda i: (0, 0), pipeline_mode=once),
        ],
        out_specs=pl.BlockSpec(
            (shards, 1, 4, 2, half, LANES), lambda i: (0, i, 0, 0, 0, 0), pipeline_mode=once
        ),
        scratch_shapes=[
            pltpu.VMEM((heads, shards, block, block), F32),
            pltpu.VMEM((heads, shards, block, block), F32),
            pltpu.VMEM((shards, block, LANES), F32),
            pltpu.VMEM((shards, block, LANES), F32),
        ],
        compiler_params=pltpu.CompilerParams(vmem_limit_bytes=58 * 2**20),
        cost_estimate=pl.CostEstimate(
            flops=pairs * 5 * 2 * block * block * 256,
            bytes_accessed=16 * 2**20,
            transcendentals=2 * pairs * block * block,
        ),
    )(qkv, grads, cosine, sine)


def middle_kernel(
    items,
    heads,
    qkv_in,
    do_in,
    hidden_in,
    normed_in,
    grads_in,
    du_in,
    cos_in,
    sin_in,
    back_in,
    down_out,
    up_out,
    d_send,
    d_keep,
    d_recv,
    d_last,
    u_send,
    u_keep,
    u_recv,
    u_last,
    out,
    local_sem,
    store_sem,
    own_sem,
    ds_,
    dr,
    us,
    ur,
    bs,
    br,
):
    place = lax.axis_index("ctx")
    shards = out.shape[1]
    x_at, z_at = place % 2, (place // 2) % 2
    near, over = {"ctx": place ^ 1}, {"ctx": place ^ 2}
    barrier = pltpu.get_barrier_semaphore()
    for k in range(1, shards):
        pl.semaphore_signal(
            barrier, inc=1, device_id={"ctx": place ^ k}, device_id_type=pl.DeviceIdType.MESH
        )

    def fetch(src, dst, at):
        copy = pltpu.make_async_copy(src, dst, local_sem.at[at])
        copy.start()
        return copy

    def block(at, size):
        return pl.ds(pl.multiple_of(at, size), size)

    members, tops, lanes, width = u_send.shape
    wide = lanes * 2 * tops
    units = d_send.shape[2]
    piece = lanes // 2

    def down_one(top):
        return remote(d_send.at[top], d_recv.at[top], ds_, dr, top, near)

    def down_two(top):
        return remote(d_send.at[top, 0], d_last.at[top], ds_, dr, tops + top, over)

    def up_one(member):
        return remote(u_send.at[member], u_recv.at[member], us, ur, member, over)

    def up_two(member):
        return remote(
            u_send.at[member, :, pl.ds(0, piece)], u_last.at[member], us, ur, members + member, near
        )

    def back_one(item, part, k):
        return remote(
            out.at[item, place ^ k, :, part],
            back_in.at[item, place, :, part],
            bs,
            br,
            (item * 2 + part) * shards + k,
            {"ctx": place ^ k},
        )

    def back_own(item, part):
        return pltpu.make_async_copy(
            out.at[item, place, :, part],
            back_in.at[item, place, :, part],
            own_sem.at[item * 2 + part],
        )

    def sums(hidden, normed, grads, du):
        loads = [
            fetch(src, dst, at)
            for at, (src, dst) in enumerate(
                ((hidden_in, hidden), (grads_in, grads), (normed_in, normed), (du_in, du))
            )
        ]
        loads[0].wait()
        loads[1].wait()
        pl.semaphore_wait(barrier, shards - 1)

        def down(which, into, top):
            def one(low, _):
                at = ((top * 2 + low) * 2 + which) * units
                into[top, low] = contract_rows(hidden[:, block(at, units)], grads[...]).astype(BF16)
                return 0

            lax.fori_loop(0, 2, one, 0)

        for top in range(tops):
            down(1 - x_at, d_send, top)
            down_one(top).start()
        loads[2].wait()
        loads[3].wait()

        def up(which, into, member):
            def one(top, _):
                at = member * wide + (top * 2 + which) * lanes
                into[member, top] = contract_rows(normed[:, block(at, lanes)], du[...]).astype(BF16)
                return 0

            lax.fori_loop(0, tops, one, 0)

        for member in range(members):
            up(1 - z_at, u_send, member)
            up_one(member).start()
        for top in range(tops):
            down(x_at, d_keep, top)
        for member in range(members):
            up(z_at, u_keep, member)

    tokens = hidden_in.shape[0]
    pl.run_scoped(
        sums,
        pltpu.VMEM(hidden_in.shape, BF16),
        pltpu.VMEM((tokens, width), BF16),
        pltpu.VMEM((tokens, width), BF16),
        pltpu.VMEM(du_in.shape, BF16),
    )

    half = out.shape[-2]
    size = 2 * half

    def attention(qkv, do, cosine, sine, s_buf, dp_buf, dk_buf, dv_buf):
        loads = []
        for item in range(items):
            loads.append(fetch(qkv_in.at[item], qkv.at[item], 2 * item))
            loads.append(fetch(do_in.at[:, item], do.at[item], 2 * item + 1))
        loads.append(fetch(cos_in, cosine, 2 * items))
        loads.append(fetch(sin_in, sine, 2 * items + 1))
        for load in loads:
            load.wait()
        lane = lax.broadcasted_iota(jnp.int32, (size, LANES), 1) // HD
        own = [lane == h for h in range(heads)]
        key_at = lax.broadcasted_iota(jnp.int32, (size, size), 0)
        query_at = lax.broadcasted_iota(jnp.int32, (size, size), 1)
        nothing = jnp.zeros((size, LANES), BF16)
        scale = HD**-0.5

        for item in range(items):
            dk_buf[...] = jnp.zeros_like(dk_buf)
            dv_buf[...] = jnp.zeros_like(dv_buf)
            for part in (1, 0):

                def where_is(at, part=part):
                    if part:
                        return 2 * shards - 1 - 2 * at, 2 * shards - 2 - 2 * at
                    return 2 * at, 2 * at + 1

                def shard_of(at):
                    low = at < shards // 2
                    first = jnp.where(low, 2 * at, 2 * shards - 1 - 2 * at)
                    second = jnp.where(low, 2 * at + 1, 2 * shards - 2 - 2 * at)
                    return first, second, jnp.where(low, 0, 1)

                def load(which, at, item=item):
                    first, second, side = shard_of(at)
                    return jnp.concatenate(
                        [qkv[item, first, which, side], qkv[item, second, which, side]], axis=0
                    )

                def store(which, at, value, item=item, part=part, where_is=where_is):
                    first, second = where_is(at)
                    out[item, first, which, part] = value[:half].astype(BF16)
                    out[item, second, which, part] = value[half:].astype(BF16)

                def per_query(at, _, item=item, load=load, store=store, shard_of=shard_of):
                    query = load(0, at) * jnp.asarray(scale, BF16)
                    first, second, where = shard_of(at)
                    grad = jnp.concatenate([do[item, first, where], do[item, second, where]], axis=0)
                    queries = [jnp.where(own[h], query, nothing) for h in range(heads)]
                    grads = [jnp.where(own[h], grad, nothing) for h in range(heads)]

                    def measure(key, state, diagonal):
                        keys, values = load(1, key), load(2, key)
                        new = []
                        for h in range(heads):
                            top, total, dot = state[h]
                            s = contract_cols(keys, queries[h])
                            if diagonal:
                                s = jnp.where(key_at <= query_at, s, -1e30)
                            dp = contract_cols(values, grads[h])
                            s_buf[h, key] = s
                            dp_buf[h, key] = dp
                            new_top = jnp.maximum(top, jnp.max(s, axis=0, keepdims=True))
                            e = jnp.exp(s - new_top)
                            fade = jnp.exp(top - new_top)
                            new.append(
                                (
                                    new_top,
                                    total * fade + jnp.sum(e, axis=0, keepdims=True),
                                    dot * fade + jnp.sum(e * dp, axis=0, keepdims=True),
                                )
                            )
                        return tuple(new)

                    zero = jnp.zeros((1, size), F32)
                    start = tuple((zero - 1e30, zero, zero) for _ in range(heads))
                    state = lax.fori_loop(0, at, lambda k, st: measure(k, st, False), start)
                    state = measure(at, state, True)
                    logs = [top + jnp.log(total) for top, total, _ in state]
                    deltas = [dot / total for _, total, dot in state]

                    def apply(key, state):
                        keys, values = load(1, key), load(2, key)
                        attended, dq = state
                        dk, dv = dk_buf[key], dv_buf[key]
                        for h in range(heads):
                            p = jnp.exp(s_buf[h, key] - logs[h])
                            ds = (p * (dp_buf[h, key] - deltas[h])).astype(BF16)
                            p = p.astype(BF16)
                            dv = dv + matmul(p, grads[h])
                            dk = dk + matmul(ds, queries[h])
                            attended = attended + jnp.where(own[h], contract_rows(p, values), 0.0)
                            dq = dq + jnp.where(own[h], contract_rows(ds, keys), 0.0)
                        dk_buf[key] = dk
                        dv_buf[key] = dv
                        return attended, dq

                    empty = jnp.zeros((size, LANES), F32)
                    attended, dq = lax.fori_loop(0, at + 1, apply, (empty, empty))
                    store(0, at, attended)
                    rows = block(at * size, size)
                    store(1, at, turn(dq * scale, cosine[rows, :], -sine[rows, :]))
                    return 0

                low = part * (shards // 2)
                lax.fori_loop(low, low + shards // 2, per_query, 0)

                def finish(at, _, store=store):
                    rows = block(at * size, size)
                    store(2, at, turn(dk_buf[at], cosine[rows, :], -sine[rows, :]))
                    store(3, at, dv_buf[at])
                    return 0

                lax.fori_loop(low, low + shards // 2, finish, 0)
                for k in range(1, shards):
                    back_one(item, part, k).start()
                back_own(item, part).start()

    pl.run_scoped(
        attention,
        pltpu.VMEM((items,) + qkv_in.shape[1:], BF16),
        pltpu.VMEM((items, shards) + do_in.shape[2:], BF16),
        pltpu.VMEM(cos_in.shape, F32),
        pltpu.VMEM(sin_in.shape, F32),
        pltpu.VMEM((heads, shards, size, size), F32),
        pltpu.VMEM((heads, shards, size, size), F32),
        pltpu.VMEM((shards, size, LANES), F32),
        pltpu.VMEM((shards, size, LANES), F32),
    )

    for top in range(tops):
        down_one(top).wait()
    for top in range(tops):
        d_send[top, 0] = (
            d_keep[top, 1 - z_at].astype(F32) + d_recv[top, 1 - z_at].astype(F32)
        ).astype(BF16)
        down_two(top).start()
    theirs = block((1 - x_at) * piece, piece)
    mine = block(x_at * piece, piece)
    for member in range(members):
        up_one(member).wait()
    for member in range(members):
        for top in range(tops):
            u_send[member, top, pl.ds(0, piece)] = (
                u_keep[member, top, theirs].astype(F32) + u_recv[member, top, theirs].astype(F32)
            ).astype(BF16)
        up_two(member).start()
    stores = []
    for top in range(tops):
        d_keep[top, z_at] = (
            d_keep[top, z_at].astype(F32) + d_recv[top, z_at].astype(F32)
        ).astype(BF16)
    for member in range(members):
        for top in range(tops):
            u_keep[member, top, mine] = (
                u_keep[member, top, mine].astype(F32) + u_recv[member, top, mine].astype(F32)
            ).astype(BF16)
    for top in range(tops):
        down_two(top).wait_recv()
        d_last[top] = (d_keep[top, z_at].astype(F32) + d_last[top].astype(F32)).astype(BF16)
        stores.append(pltpu.make_async_copy(d_last.at[top], down_out.at[top], store_sem.at[top]))
        stores[-1].start()
    for member in range(members):
        up_two(member).wait_recv()
        for top in range(tops):
            u_last[member, top] = (
                u_keep[member, top, mine].astype(F32) + u_last[member, top].astype(F32)
            ).astype(BF16)
        stores.append(
            pltpu.make_async_copy(u_last.at[member], up_out.at[member], store_sem.at[tops + member])
        )
        stores[-1].start()
    for item in range(items):
        for part in (1, 0):
            for k in range(1, shards):
                back_one(item, part, k).wait()
            back_own(item, part).wait()
    for top in range(tops):
        down_two(top).wait_send()
    for member in range(members):
        up_two(member).wait_send()
    for copy in stores:
        copy.wait()


def middle(qkv_in, do_in, hidden, normed, grads, du, cosine, sine, heads, groups):
    items, shards = qkv_in.shape[:2]
    half = qkv_in.shape[-2]
    width = normed.shape[1]
    deep = hidden.shape[1]
    units = deep // shards
    tops = shards // 4
    lanes = width // groups // tops // 2
    apart = pl.BlockSpec(memory_space=pl.ANY)
    dma = pltpu.SemaphoreType.DMA
    shape = jax.ShapeDtypeStruct
    pairs = shards * (shards + 1) // 2 * items * heads
    return pl.pallas_call(
        partial(middle_kernel, items, heads),
        out_shape=[
            shape((items, shards, 4, 2, half, LANES), BF16),
            shape((tops, units, width), BF16),
            shape((groups, tops, lanes // 2, deep), BF16),
        ],
        in_specs=[apart] * 8,
        out_specs=[apart] * 3,
        scratch_shapes=[
            pltpu.VMEM((tops, 2, units, width), BF16),
            pltpu.VMEM((tops, 2, units, width), BF16),
            pltpu.VMEM((tops, 2, units, width), BF16),
            pltpu.VMEM((tops, units, width), BF16),
            pltpu.VMEM((groups, tops, lanes, deep), BF16),
            pltpu.VMEM((groups, tops, lanes, deep), BF16),
            pltpu.VMEM((groups, tops, lanes, deep), BF16),
            pltpu.VMEM((groups, tops, lanes // 2, deep), BF16),
            pltpu.VMEM((items, shards, 4, 2, half, LANES), BF16),
            dma((max(4, 2 * items + 2),)),
            dma((tops + groups,)),
            dma((2 * items,)),
            dma((2 * tops,)),
            dma((2 * tops,)),
            dma((2 * groups,)),
            dma((2 * groups,)),
            dma((2 * items * shards,)),
            dma((2 * items * shards,)),
        ],
        compiler_params=pltpu.CompilerParams(
            collective_id=1, has_side_effects=True, vmem_limit_bytes=63 * 2**20
        ),
        cost_estimate=pl.CostEstimate(
            flops=pairs * 10 * (2 * half) ** 2 * 256 + 8 * width * deep * hidden.shape[0],
            bytes_accessed=40 * 2**20,
            transcendentals=2 * pairs * (2 * half) ** 2,
        ),
    )(qkv_in, do_in, hidden, normed, grads, du, cosine, sine)


FLIGHTS = 64


def finish_kernel(
    items,
    pairs,
    slot_groups,
    back_in,
    normed_in,
    grads_in,
    hidden_in,
    du_in,
    wqkv_in,
    wup_in,
    outw_in,
    down_in,
    d_in,
    u_in,
    x_in,
    cot_in,
    gain_ref,
    out_bias_ref,
    down_bias_ref,
    result_out,
    input_out,
    qkv_out,
    up_out,
    o_out,
    d_out,
    sums_out,
    big,
    q_send,
    q_keep,
    q_recv,
    q_two,
    q_three,
    q_done,
    o_send,
    o_keep,
    o_recv,
    o_two,
    o_three,
    d_three,
    u_three,
    u_done,
    p_send,
    p_recv,
    p_own,
    n_send,
    n_recv,
    n_own,
    sums,
    s_recv,
    s_part,
    s_all,
    local_sem,
    store_sem,
    sends,
    recvs,
):
    place = lax.axis_index("ctx")
    member = lax.axis_index("fsdp")
    shards = back_in.shape[1]
    groups, tops, _, piece, qcols = q_send.shape
    rows, width = p_own.shape
    wide = width // groups
    deep = hidden_in.shape[1]
    x_at, z_at, top_at = place % 2, (place // 2) % 2, place // 4
    near, over, far = {"ctx": place ^ 1}, {"ctx": place ^ 2}, {"ctx": place ^ 4}

    barrier = pltpu.get_barrier_semaphore()
    for j in range(1, groups):
        pl.semaphore_signal(
            barrier, inc=1, device_id={"fsdp": member ^ j}, device_id_type=pl.DeviceIdType.MESH
        )
    for k in range(1, shards):
        pl.semaphore_signal(
            barrier, inc=1, device_id={"ctx": place ^ k}, device_id_type=pl.DeviceIdType.MESH
        )

    def block(at, size):
        return pl.ds(pl.multiple_of(at, size), size)

    names = {}

    def flight(name, src, dst, target):
        at = names.setdefault(name, len(names))
        return remote(src, dst, sends, recvs, at, target)

    def fetch(src, dst, at):
        copy = pltpu.make_async_copy(src, dst, local_sem.at[at])
        copy.start()
        return copy

    def core(j):
        return {"fsdp": member ^ j}

    def d_last():
        return flight("d", d_in.at[1 - top_at], d_three, far)

    def u_last():
        return flight("u", u_in.at[:, 1 - top_at], u_three, far)

    def o_first(top):
        return flight(("o1", top), o_send.at[top], o_recv.at[top], over)

    def o_second():
        return flight("o2", o_send.at[:, pl.ds(0, piece)], o_two, near)

    def o_last():
        return flight("o3", o_send.at[0, pl.ds(piece, piece)], o_three, far)

    def q_first(f):
        return flight(("q1", f), q_send.at[f], q_recv.at[f], near)

    def q_second(f):
        return flight(("q2", f), q_send.at[f, :, 0], q_two.at[f], over)

    def q_last(f):
        return flight(("q3", f), q_send.at[f, 0, 1], q_three.at[f], far)

    def q_swap(j):
        return flight(("q4", j), q_done.at[member ^ j], qkv_out.at[member], core(j))

    def u_swap(j):
        return flight(("u4", j), u_done.at[member ^ j], up_out.at[member], core(j))

    def rows_last(name, send, recv):
        return flight((name, 3), send.at[0], recv.at[0], core(1))

    def rows_far(name, send, recv):
        return flight((name, 2), send.at[1], recv.at[1], core(2))

    def rows_near(name, send, recv):
        return flight((name, 1), send.at[2], recv.at[2], core(1))

    def sums_one(j):
        return flight(("s1", j), sums, s_recv.at[j - 1], core(j))

    span = width // shards

    def sums_two(k):
        return flight(
            ("s2", k), s_all.at[:, block((place ^ k) * span, span)], s_part.at[k], {"ctx": place ^ k}
        )

    def sums_three(k):
        mine = block(place * span, span)
        return flight(("s3", k), sums_out.at[:, mine], sums_out.at[:, mine], {"ctx": place ^ k})

    pl.semaphore_wait(barrier, groups - 1 + shards - 1)
    d_last().start()
    u_last().start()

    def phase_a(normed, grads):
        loads = [fetch(normed_in, normed, 0), fetch(grads_in, grads, 1)]
        for item in range(items):
            for owner in range(shards):
                pair, g = owner // slot_groups, owner % slot_groups
                spot = pl.ds((item * slot_groups + g) * rows, rows)
                for kind in range(4):
                    loads.append(
                        fetch(
                            back_in.at[item, owner, kind],
                            big.at[spot, pl.ds(kind * wide + pair * LANES, LANES)],
                            2 + (item * shards + owner) * 4 + kind,
                        )
                    )
        sums[...] = jnp.zeros_like(sums)
        for load in loads:
            load.wait()

        def out_grad(top, low, into):
            at = (top * 2 + low) * LANES
            into[top] = contract_rows(big[:, block(at, LANES)], grads[...]).astype(BF16)

        for top in range(tops):
            out_grad(top, 1 - z_at, o_send)
            o_first(top).start()

        for f in range(groups):

            def one(at, _, f=f):
                top, low = at // 2, at % 2
                value = contract_rows(
                    normed[:, block(f * wide + at * LANES, LANES)], big[:, wide:]
                )
                first, second = value[:piece], value[piece:]
                q_send[f, top, low] = jnp.where(x_at == 0, second, first).astype(BF16)
                q_keep[f, top, low] = jnp.where(x_at == 0, first, second).astype(BF16)
                return 0

            lax.fori_loop(0, 2 * tops, one, 0)
            q_first(f).start()
        for top in range(tops):
            out_grad(top, z_at, o_keep)
        for kind in range(3):
            cols = big[:, (kind + 1) * wide : (kind + 2) * wide].astype(F32)
            sums[2 + kind : 3 + kind, block(member * wide, wide)] = jnp.sum(
                cols, axis=0, keepdims=True
            )

    total = rows * groups
    pl.run_scoped(
        phase_a, pltpu.VMEM((total, width), BF16), pltpu.VMEM((total, width), BF16)
    )

    tile = 256

    def keep_share(pair, at, value, send, own):
        cols = block(at * tile, tile)
        if pair == 1:
            send[1, :, cols] = value[:rows].astype(BF16)
            send[0, :, cols] = value[rows:].astype(BF16)
        else:
            own[:, cols] = value[:rows]
            send[2, :, cols] = value[rows:].astype(BF16)

    def phase_b(hidden, down, outw):
        loads = [
            fetch(hidden_in, hidden, 0),
            fetch(down_in, down, 1),
            fetch(outw_in, outw, 2),
        ]
        for load in loads:
            load.wait()
        for pair in (1, 0):
            spot = pl.ds(pair * 2 * rows, 2 * rows)

            def one(at, _, pair=pair, spot=spot):
                cols = block(at * tile, tile)
                value = matmul(hidden[spot, :], down[:, cols]) + matmul(
                    big[spot, pl.ds(0, wide)], outw[:, cols]
                )
                keep_share(pair, at, value, p_send, p_own)
                return 0

            lax.fori_loop(0, width // tile, one, 0)
            if pair == 1:
                rows_last("p", p_send, p_recv).start()
            else:
                rows_near("p", p_send, p_recv).start()

    pl.run_scoped(
        phase_b,
        pltpu.VMEM(hidden_in.shape, BF16),
        pltpu.VMEM(down_in.shape, BF16),
        pltpu.VMEM(outw_in.shape, BF16),
    )

    def pass_rows(name, send, recv):
        rows_last(name, send, recv).wait_recv()
        send[1] = (send[1].astype(F32) + recv[0].astype(F32)).astype(BF16)
        rows_far(name, send, recv).start()

    pass_rows("p", p_send, p_recv)

    theirs = block((1 - x_at) * piece, piece)
    mine = block(x_at * piece, piece)
    for top in range(tops):
        o_first(top).wait()
    for top in range(tops):
        o_send[top, pl.ds(0, piece)] = (
            o_keep[top, theirs].astype(F32) + o_recv[top, theirs].astype(F32)
        ).astype(BF16)
    o_second().start()

    def q_pass(f):
        q_first(f).wait()
        for top in range(tops):
            q_send[f, top, 0] = (
                q_keep[f, top, 1 - z_at].astype(F32) + q_recv[f, top, 1 - z_at].astype(F32)
            ).astype(BF16)
        q_second(f).start()

    def q_turn(f):
        q_second(f).wait_recv()
        other = 1 - top_at
        q_send[f, 0, 1] = (
            q_keep[f, other, z_at].astype(F32)
            + q_recv[f, other, z_at].astype(F32)
            + q_two[f, other].astype(F32)
        ).astype(BF16)
        q_last(f).start()

    for f in range(groups // 2):
        q_pass(f)

    def phase_c(du, wup, wqkv):
        loads = [
            fetch(du_in, du, 0),
            fetch(wup_in, wup, 1),
            fetch(wqkv_in, wqkv, 2),
        ]
        for load in loads:
            load.wait()
        for pair in (1, 0):
            spot = pl.ds(pair * 2 * rows, 2 * rows)

            def one(at, _, pair=pair, spot=spot):
                cols = block(at * tile, tile)
                value = contract_cols(du[spot, :], wup[cols, :]) + contract_cols(
                    big[spot, pl.ds(wide, 3 * wide)], wqkv[cols, :]
                )
                keep_share(pair, at, value, n_send, n_own)
                return 0

            lax.fori_loop(0, width // tile, one, 0)
            if pair == 1:
                rows_last("n", n_send, n_recv).start()
            else:
                rows_near("n", n_send, n_recv).start()
        step = deep // groups

        def column_sums(at, _):
            cols = block(at * step, step)
            value = jnp.sum(du[:, cols].astype(F32), axis=0, keepdims=True)
            for j in range(groups):
                sums[5 + j : 6 + j, cols] = jnp.where(member == j, value, 0.0)
            return 0

        lax.fori_loop(0, groups, column_sums, 0)

    pl.run_scoped(
        phase_c,
        pltpu.VMEM(du_in.shape, BF16),
        pltpu.VMEM(wup_in.shape, BF16),
        pltpu.VMEM(wqkv_in.shape, BF16),
    )
    pass_rows("n", n_send, n_recv)
    for f in range(groups // 2, groups):
        q_pass(f)
    for f in range(groups // 2):
        q_turn(f)
    o_second().wait_recv()
    o_send[0, pl.ds(piece, piece)] = (
        o_keep[1 - top_at, mine].astype(F32)
        + o_recv[1 - top_at, mine].astype(F32)
        + o_two[1 - top_at].astype(F32)
    ).astype(BF16)
    o_last().start()

    def phase_d(x, cot, out, d_own, d_sum, o_sum):
        loads = [
            fetch(x_in, x, 0),
            fetch(cot_in, cot, 1),
            fetch(u_in.at[:, top_at], u_done, 2),
            fetch(d_in.at[top_at], d_own, 3),
        ]
        for load in loads:
            load.wait()

        u_last().wait_recv()
        for f in range(groups):
            u_done[f] = (u_done[f].astype(F32) + u_three[f].astype(F32)).astype(BF16)
        for j in range(1, groups):
            u_swap(j).start()
        own_up = pltpu.make_async_copy(u_done.at[member], up_out.at[member], store_sem.at[0])
        own_up.start()

        for f in range(groups // 2, groups):
            q_turn(f)
        rows_near("n", n_send, n_recv).wait_recv()
        rows_far("n", n_send, n_recv).wait_recv()
        step = 64

        def normal_part(at, _):
            r = block(at * step, step)
            tokens = x[r, :].astype(F32)
            centred = tokens - jnp.mean(tokens, axis=-1, keepdims=True)
            spread = lax.rsqrt(jnp.mean(centred * centred, axis=-1, keepdims=True) + EPS)
            normal = centred * spread
            dn = n_own[r, :] + n_recv[2, r, :].astype(F32) + n_recv[1, r, :].astype(F32)
            sums[0:1, :] = sums[0:1, :] + jnp.sum(dn * normal, axis=0, keepdims=True)
            sums[1:2, :] = sums[1:2, :] + jnp.sum(dn, axis=0, keepdims=True)
            dnorm = dn * gain_ref[...]
            grad = cot[r, :].astype(F32)
            sums[9:10, :] = sums[9:10, :] + jnp.sum(grad, axis=0, keepdims=True)
            change = spread * (
                dnorm
                - jnp.mean(dnorm, axis=-1, keepdims=True)
                - normal * jnp.mean(dnorm * normal, axis=-1, keepdims=True)
            )
            cot[r, :] = (grad + change).astype(BF16)
            return 0

        lax.fori_loop(0, rows // step, normal_part, 0)
        for j in range(1, groups):
            sums_one(j).start()
        own_input = pltpu.make_async_copy(cot, input_out, store_sem.at[1])
        own_input.start()

        rows_near("p", p_send, p_recv).wait_recv()
        rows_far("p", p_send, p_recv).wait_recv()

        def output_part(at, _):
            r = block(at * step, step)
            value = x[r, :].astype(F32) + p_own[r, :] + p_recv[2, r, :].astype(F32)
            value = value + p_recv[1, r, :].astype(F32) + out_bias_ref[...] + down_bias_ref[...]
            out[r, :] = value.astype(BF16)
            return 0

        lax.fori_loop(0, rows // step, output_part, 0)
        own_out = pltpu.make_async_copy(out, result_out, store_sem.at[2])
        own_out.start()

        for j in range(1, groups):
            sums_one(j).wait_recv()
        s_all[...] = sums[...] + s_recv[0] + s_recv[1] + s_recv[2]
        for k in range(1, shards):
            sums_two(k).start()
        d_last().wait_recv()
        d_sum[...] = d_own[...].astype(F32) + d_three[...].astype(F32)
        own_down = pltpu.make_async_copy(d_sum, d_out, store_sem.at[3])
        own_down.start()

        for f in range(groups):
            q_last(f).wait_recv()
            q_done[f] = (
                q_keep[f, top_at, z_at].astype(F32)
                + q_recv[f, top_at, z_at].astype(F32)
                + q_two[f, top_at].astype(F32)
                + q_three[f].astype(F32)
            ).astype(BF16)
        for j in range(1, groups):
            q_swap(j).start()
        own_q = pltpu.make_async_copy(q_done.at[member], qkv_out.at[member], store_sem.at[4])
        own_q.start()
        o_last().wait_recv()
        o_sum[...] = (
            o_keep[top_at, mine].astype(F32)
            + o_recv[top_at, mine].astype(F32)
            + o_two[top_at].astype(F32)
            + o_three[...].astype(F32)
        )
        own_o = pltpu.make_async_copy(o_sum, o_out, store_sem.at[5])
        own_o.start()
        for k in range(1, shards):
            sums_two(k).wait()
        cols = block(place * span, span)
        value = s_all[:, cols]
        for k in range(1, shards):
            value = value + s_part[k]
        sums_out[:, cols] = value
        for k in range(1, shards):
            sums_three(k).start()
        for copy in (own_up, own_input, own_out, own_down, own_q, own_o):
            copy.wait()

    pl.run_scoped(
        phase_d,
        pltpu.VMEM((rows, width), BF16),
        pltpu.VMEM((rows, width), BF16),
        pltpu.VMEM((rows, width), BF16),
        pltpu.VMEM(d_in.shape[1:], BF16),
        pltpu.VMEM(d_in.shape[1:], F32),
        pltpu.VMEM((piece, width), F32),
    )
    d_last().wait_send()
    u_last().wait_send()
    o_second().wait_send()
    o_last().wait_send()
    for f in range(groups):
        q_second(f).wait_send()
        q_last(f).wait_send()
    for j in range(1, groups):
        q_swap(j).wait()
        u_swap(j).wait()
        sums_one(j).wait_send()
    for name, send, recv in (("p", p_send, p_recv), ("n", n_send, n_recv)):
        rows_last(name, send, recv).wait_send()
        rows_far(name, send, recv).wait_send()
        rows_near(name, send, recv).wait_send()
    for k in range(1, shards):
        sums_three(k).wait()


def finish(
    back_in, normed, grads, hidden, du, wqkv, wup, outw, down, d_sum, u_sum,
    x, cot, gain, out_bias, down_bias, groups, slot_groups,
):
    items, shards = back_in.shape[:2]
    rows, width = x.shape
    wide = width // groups
    deep = hidden.shape[1]
    tops = shards // 4
    piece = wide // shards
    pairs = wide // LANES
    units = deep // shards
    apart = pl.BlockSpec(memory_space=pl.ANY)
    whole = pl.BlockSpec(memory_space=pltpu.VMEM)
    dma = pltpu.SemaphoreType.DMA
    shape = jax.ShapeDtypeStruct
    return pl.pallas_call(
        partial(finish_kernel, items, pairs, slot_groups),
        out_shape=[
            shape((rows, width), BF16),
            shape((rows, width), BF16),
            shape((groups, piece, 3 * wide), BF16),
            shape((groups, piece, deep), BF16),
            shape((piece, width), F32),
            shape((units, width), F32),
            shape((16, width), F32),
        ],
        in_specs=[apart] * 13 + [whole] * 3,
        out_specs=[apart] * 6 + [whole],
        scratch_shapes=[
            pltpu.VMEM((rows * groups, 4 * wide), BF16),
            pltpu.VMEM((groups, tops, 2, piece, 3 * wide), BF16),
            pltpu.VMEM((groups, tops, 2, piece, 3 * wide), BF16),
            pltpu.VMEM((groups, tops, 2, piece, 3 * wide), BF16),
            pltpu.VMEM((groups, tops, piece, 3 * wide), BF16),
            pltpu.VMEM((groups, piece, 3 * wide), BF16),
            pltpu.VMEM((groups, piece, 3 * wide), BF16),
            pltpu.VMEM((tops, 2 * piece, width), BF16),
            pltpu.VMEM((tops, 2 * piece, width), BF16),
            pltpu.VMEM((tops, 2 * piece, width), BF16),
            pltpu.VMEM((tops, piece, width), BF16),
            pltpu.VMEM((piece, width), BF16),
            pltpu.VMEM((units, width), BF16),
            pltpu.VMEM((groups, piece, deep), BF16),
            pltpu.VMEM((groups, piece, deep), BF16),
            pltpu.VMEM((3, rows, width), BF16),
            pltpu.VMEM((3, rows, width), BF16),
            pltpu.VMEM((rows, width), F32),
            pltpu.VMEM((3, rows, width), BF16),
            pltpu.VMEM((3, rows, width), BF16),
            pltpu.VMEM((rows, width), F32),
            pltpu.VMEM((16, width), F32),
            pltpu.VMEM((3, 16, width), F32),
            pltpu.VMEM((shards, 16, width // shards), F32),
            pltpu.VMEM((16, width), F32),
            dma((2 + items * shards * 4,)),
            dma((6,)),
            dma((FLIGHTS,)),
            dma((FLIGHTS,)),
        ],
        compiler_params=pltpu.CompilerParams(
            collective_id=2, has_side_effects=True, vmem_limit_bytes=63 * 2**20
        ),
        cost_estimate=pl.CostEstimate(
            flops=2 * rows * groups * width * (2 * deep + 8 * wide),
            bytes_accessed=60 * 2**20,
            transcendentals=0,
        ),
    )(
        back_in, normed, grads, hidden, du, wqkv, wup, outw, down, d_sum, u_sum, x, cot,
        gain.reshape(1, width), out_bias.reshape(1, width), down_bias.reshape(1, width),
    )


def scatter_sum(parts, axis_at, place, bits):
    lead, tail = parts.shape[:axis_at], parts.shape[axis_at + 1 :]
    total = len(bits)
    left = list(range(total - 1, -1, -1))
    value = parts.reshape(lead + (2,) * total + tail)
    for bit in bits:
        at = axis_at + left.index(bit)
        left.remove(bit)
        mine = (place >> bit) & 1
        send = lax.dynamic_index_in_dim(value, 1 - mine, at, keepdims=False)
        keep = lax.dynamic_index_in_dim(value, mine, at, keepdims=False)
        got = swap(send.astype(BF16), "ctx", 1 << bit)
        value = keep.astype(F32) + got.astype(F32)
    return value


def scatter_rows(parts):
    last = swap(parts[3].astype(BF16), "fsdp", 1).astype(F32)
    far = swap((parts[2] + last).astype(BF16), "fsdp", 2).astype(F32)
    near = swap(parts[1].astype(BF16), "fsdp", 1).astype(F32)
    return parts[0] + near + far


def total_sum(value):
    for axis in ("fsdp", "ctx"):
        bit = 1
        while bit < lax.axis_size(axis):
            value = value + swap(value, axis, bit)
            bit *= 2
    return value


def on_device(
    inputs,
    norm_gain,
    norm_shift,
    qkv_weight,
    qkv_bias,
    out_weight,
    out_bias,
    up_weight,
    up_bias,
    down_weight,
    down_bias,
    cotangent,
):
    rows = inputs.shape[1]
    width = inputs.shape[2]
    hidden_width = up_weight.shape[1]
    half = rows // 2
    shards = lax.axis_size("ctx")
    groups = lax.axis_size("fsdp")
    place = lax.axis_index("ctx")
    member = lax.axis_index("fsdp")
    wide = width // groups
    deep = hidden_width // groups
    x_first = list(range(shards.bit_length() - 1))
    z_first = x_first[1:2] + x_first[:1] + x_first[2:]

    tokens = inputs[0].astype(F32)
    mean = jnp.mean(tokens, axis=-1, keepdims=True)
    centred = tokens - mean
    inv_scale = lax.rsqrt(jnp.mean(centred * centred, axis=-1, keepdims=True) + EPS)
    normal = centred * inv_scale
    grad_low = cotangent[0]
    grad_full = grad_low.astype(F32)

    pairs = wide // LANES
    heads_in_pair = LANES // HD
    units = pairs * groups
    dup = max(1, shards // units)
    slot_groups = shards // (pairs * dup)
    per_group = groups // slot_groups
    heads = heads_in_pair // dup

    cos_full, sin_full = rotary(shards * rows)
    normed, grads, qkv_own, up_own, hidden, grad_up, qkv_in, grad_in = begin_layer(
        inputs[0],
        norm_gain,
        norm_shift,
        grad_low,
        qkv_weight,
        qkv_bias,
        up_weight,
        up_bias,
        out_weight,
        down_weight,
        cos_full,
        sin_full,
        shards,
        groups,
        pairs,
        slot_groups,
        per_group,
        dup,
    )

    def assembled(back):
        back = back.reshape(pairs, slot_groups, dup, 4, rows, LANES)
        back = jnp.sum(back, axis=2) if dup > 1 else back[:, :, 0]
        return back.transpose(2, 1, 3, 0, 4).reshape(4, slot_groups * rows, wide)

    hw = deep // shards
    if len(x_first) == 3 and dup == 1:
        back_in, down_sum, up_sum = middle(
            qkv_in.reshape(per_group, shards, 3, 2, half, LANES),
            grad_in.reshape(shards, per_group, 2, half, LANES),
            hidden,
            normed,
            grads,
            grad_up,
            cos_full,
            sin_full,
            heads,
            groups,
        )
        result, input_grad, qkv_parts, up_parts, out_weight_grad, down_weight_grad, sums = finish(
            back_in.reshape(per_group, shards, 4, rows, LANES),
            normed,
            grads,
            hidden,
            grad_up,
            qkv_own,
            up_own,
            out_weight,
            down_weight,
            down_sum,
            up_sum,
            inputs[0],
            grad_low,
            norm_gain,
            out_bias,
            down_bias,
            groups,
            slot_groups,
        )
        ow = wide // shards
        return (
            result[None],
            input_grad[None],
            sums[0],
            sums[1],
            qkv_parts.reshape(groups, ow, 3, wide)
            .transpose(1, 2, 0, 3)
            .reshape(ow, 3 * width)
            .astype(F32),
            sums[2:5].reshape(-1),
            out_weight_grad,
            sums[9],
            up_parts.transpose(1, 0, 2).reshape(ow, hidden_width).astype(F32),
            sums[5 : 5 + groups].reshape(-1),
            down_weight_grad,
            sums[9],
        )
    else:
        down_grad = contract_rows(hidden, grads).astype(BF16)
        up_grad = contract_rows(normed, grad_up).astype(BF16)
        down_weight_grad = scatter_sum(
            down_grad.reshape(shards, hw, width), 0, place, x_first
        )
        up_part = scatter_sum(
            up_grad.reshape(groups, shards, wide // shards, deep), 1, place, z_first
        )

        backs = []
        for item in range(per_group):
            back = attend(
                qkv_in.reshape(per_group, shards, 3, 2, half, LANES),
                grad_in.reshape(shards, per_group, 2, half, LANES),
                item,
                cos_full,
                sin_full,
                heads,
                dup,
            )
            back = lax.all_to_all(back, "ctx", 0, 0)
            back = back.reshape(pairs, slot_groups, dup, 4, rows, LANES)
            back = jnp.sum(back, axis=2) if dup > 1 else back[:, :, 0]
            backs.append(back.transpose(2, 1, 3, 0, 4).reshape(4, slot_groups * rows, wide))
        back = jnp.concatenate(backs, axis=1)
        attended = back[0]
        grad_qkv = jnp.concatenate([back[1], back[2], back[3]], axis=1)

        share = matmul(hidden, down_weight) + matmul(attended, out_weight)
        result = tokens + scatter_rows(list(share.reshape(groups, rows, width))) + out_bias + down_bias

        grad_share = contract_cols(grad_up, up_own) + contract_cols(grad_qkv, qkv_own)
        grad_normed = scatter_rows(list(grad_share.reshape(groups, rows, width)))
        grad_full = grad_low.astype(F32)
        grad_normal = grad_normed * norm_gain
        grad_tokens = inv_scale * (
            grad_normal
            - jnp.mean(grad_normal, axis=-1, keepdims=True)
            - normal * jnp.mean(grad_normal * normal, axis=-1, keepdims=True)
        )
        input_grad = (grad_full + grad_tokens).astype(BF16)

        qkv_grad = contract_rows(normed, grad_qkv).astype(BF16)
        out_grad = contract_rows(attended, grads).astype(BF16)
        ow = wide // shards
        out_weight_grad = scatter_sum(out_grad.reshape(shards, ow, width), 0, place, z_first)
        qkv_part = scatter_sum(
            qkv_grad.reshape(groups, shards, ow, 3 * wide), 1, place, x_first
        )

        def relative(value):
            return [
                lax.dynamic_index_in_dim(value, member ^ j, 0, keepdims=False) for j in range(groups)
            ]

        def exchange(part):
            sent = relative(part.astype(BF16))
            got = [sent[0]] + [swap(sent[j], "fsdp", j) for j in range(1, groups)]
            return relative(jnp.stack(got))

        up_weight_grad = jnp.concatenate(exchange(up_part), axis=1).astype(F32)
        qkv_weight_grad = jnp.concatenate(
            [item.reshape(ow, 3, 1, wide) for item in exchange(qkv_part)], axis=2
        ).reshape(ow, 3 * width).astype(F32)

        qkv_bias_cols = jnp.sum(grad_qkv.astype(F32), axis=0).reshape(3, 1, wide)
        backs = []
        for item in range(per_group):
            back = attend(
                qkv_in.reshape(per_group, shards, 3, 2, half, LANES),
                grad_in.reshape(shards, per_group, 2, half, LANES),
                item,
                cos_full,
                sin_full,
                heads,
                dup,
            )
            back = lax.all_to_all(back, "ctx", 0, 0)
            backs.append(assembled(back))
    back = jnp.concatenate(backs, axis=1)
    attended = back[0]
    grad_qkv = jnp.concatenate([back[1], back[2], back[3]], axis=1)

    share = matmul(hidden, down_weight) + matmul(attended, out_weight)
    result = tokens + scatter_rows(list(share.reshape(groups, rows, width))) + out_bias + down_bias

    grad_share = contract_cols(grad_up, up_own) + contract_cols(grad_qkv, qkv_own)
    grad_normed = scatter_rows(list(grad_share.reshape(groups, rows, width)))
    grad_full = grad_low.astype(F32)
    grad_normal = grad_normed * norm_gain
    grad_tokens = inv_scale * (
        grad_normal
        - jnp.mean(grad_normal, axis=-1, keepdims=True)
        - normal * jnp.mean(grad_normal * normal, axis=-1, keepdims=True)
    )
    input_grad = (grad_full + grad_tokens).astype(BF16)

    qkv_grad = contract_rows(normed, grad_qkv).astype(BF16)
    out_grad = contract_rows(attended, grads).astype(BF16)
    ow = wide // shards
    out_weight_grad = scatter_sum(out_grad.reshape(shards, ow, width), 0, place, z_first)
    qkv_part = scatter_sum(
        qkv_grad.reshape(groups, shards, ow, 3 * wide), 1, place, x_first
    )

    def relative(value):
        return [
            lax.dynamic_index_in_dim(value, member ^ j, 0, keepdims=False) for j in range(groups)
        ]

    def exchange(part):
        sent = relative(part.astype(BF16))
        got = [sent[0]] + [swap(sent[j], "fsdp", j) for j in range(1, groups)]
        return relative(jnp.stack(got))

    up_weight_grad = jnp.concatenate(exchange(up_part), axis=1).astype(F32)
    qkv_weight_grad = jnp.concatenate(
        [item.reshape(ow, 3, 1, wide) for item in exchange(qkv_part)], axis=2
    ).reshape(ow, 3 * width).astype(F32)

    qkv_bias_cols = jnp.sum(grad_qkv.astype(F32), axis=0).reshape(3, 1, wide)
    up_bias_cols = jnp.sum(grad_up.astype(F32), axis=0).reshape(1, deep)
    qkv_bias_all = lax.dynamic_update_slice(
        jnp.zeros((3, groups, wide), F32), qkv_bias_cols, (0, member, 0)
    ).reshape(-1)
    up_bias_all = lax.dynamic_update_slice(
        jnp.zeros((groups, deep), F32), up_bias_cols, (member, 0)
    ).reshape(-1)
    early = total_sum(jnp.concatenate([jnp.sum(grad_full, axis=0), up_bias_all]))
    late = total_sum(
        jnp.concatenate(
            [jnp.sum(grad_normed * normal, axis=0), jnp.sum(grad_normed, axis=0), qkv_bias_all]
        )
    )
    out_bias_grad, up_bias_grad = early[:width], early[width:]
    gain_grad, shift_grad, qkv_bias_grad = late[:width], late[width : 2 * width], late[2 * width :]
    return (
        result.astype(BF16)[None],
        input_grad[None],
        gain_grad,
        shift_grad,
        qkv_weight_grad,
        qkv_bias_grad,
        out_weight_grad,
        out_bias_grad,
        up_weight_grad,
        up_bias_grad,
        down_weight_grad,
        out_bias_grad,
    )


def solution(mesh):
    in_specs = (
        P("fsdp", "ctx", None),
        P(),
        P(),
        P("fsdp", None),
        P(),
        P("fsdp", None),
        P(),
        P("fsdp", None),
        P(),
        P("fsdp", None),
        P(),
        P("fsdp", "ctx", None),
    )
    out_specs = (
        P("fsdp", "ctx", None),
        P("fsdp", "ctx", None),
        P(),
        P(),
        P(("fsdp", "ctx"), None),
        P(),
        P(("fsdp", "ctx"), None),
        P(),
        P(("fsdp", "ctx"), None),
        P(),
        P(("fsdp", "ctx"), None),
        P(),
    )
    return jax.shard_map(
        on_device, mesh=mesh, in_specs=in_specs, out_specs=out_specs, check_vma=False
    )
```

```python
from functools import partial

import jax
import jax.numpy as jnp
import numpy as np
from jax import lax
from jax.experimental import pallas as pl
from jax.experimental.pallas import tpu as pltpu
from jax.sharding import PartitionSpec as P

HD = 64
ROT = 32
LANES = 128

EPS = 1e-05
ROOT = 0.7978845608028654
CUBIC = 0.044715
F32 = jnp.float32
BF16 = jnp.bfloat16


def gelu_value(value):
    return 0.5 * value * (1.0 + jnp.tanh(ROOT * (value + CUBIC * value * value * value)))


def gelu_slope(value):
    tangent = jnp.tanh(ROOT * (value + CUBIC * value * value * value))
    return 0.5 * (1.0 + tangent) + 0.5 * value * (1.0 - tangent * tangent) * ROOT * (
        1.0 + 3.0 * CUBIC * value * value
    )


def contract_rows(left, right):
    return lax.dot_general(left, right, (((0,), (0,)), ((), ())), preferred_element_type=F32)


def contract_cols(left, right):
    return lax.dot_general(left, right, (((1,), (1,)), ((), ())), preferred_element_type=F32)


def matmul(left, right):
    return jnp.dot(left, right, preferred_element_type=F32)


def swap(value, axis, bit):
    size = lax.axis_size(axis)
    return lax.ppermute(value, axis, [(i, i ^ bit) for i in range(size)])


def after(value, *events):
    return lax.optimization_barrier((value,) + events)[0]


def rotary(length):
    quarter = ROT // 2
    inverse = np.float32(10000.0) ** (-np.arange(quarter, dtype=np.float32) * 2.0 / ROT)
    angle = np.arange(length, dtype=np.float32)[:, None] * inverse.astype(np.float32)[None, :]
    cosine, sine = np.cos(angle), np.sin(angle)
    one = np.concatenate([cosine, cosine, np.ones((length, HD - ROT))], axis=1)
    two = np.concatenate([-sine, sine, np.zeros((length, HD - ROT))], axis=1)
    copies = (1, LANES // HD)
    return (
        jnp.asarray(np.tile(one, copies), F32),
        jnp.asarray(np.tile(two, copies), F32),
    )


def turn(rows, cosine, sine):
    lane = lax.broadcasted_iota(jnp.int32, rows.shape, 1) % HD
    quarter = ROT // 2
    other = jnp.where(
        lane < quarter,
        pltpu.roll(rows, LANES - quarter, 1),
        pltpu.roll(rows, quarter, 1),
    )
    return rows * cosine + other * sine


def remote(src, dst, sends, recvs, at, target):
    return pltpu.make_async_remote_copy(
        src_ref=src,
        dst_ref=dst,
        send_sem=sends.at[at],
        recv_sem=recvs.at[at],
        device_id=target,
        device_id_type=pl.DeviceIdType.MESH,
    )


def start_kernel(
    shards,
    groups,
    pairs,
    slot_groups,
    items,
    dup,
    x_ref,
    gain_ref,
    shift_ref,
    cot_ref,
    qkv_ref,
    qkv_bias_ref,
    up_ref,
    up_bias_ref,
    out_ref,
    down_ref,
    cos_ref,
    sin_ref,
    normed_out,
    grads_out,
    wqkv_out,
    wup_out,
    hidden_out,
    du_out,
    qkv_in,
    do_in,
    normed,
    grads,
    wqkv,
    wup,
    down,
    outw,
    cosine,
    sine,
    stage,
    dstage,
    dh,
    hidden,
    du,
    local_sem,
    store_sem,
    qs,
    qr,
    us,
    ur,
    rs,
    rr,
    as_,
    ar,
    ds_,
    dr,
):
    place = lax.axis_index("ctx")
    member = lax.axis_index("fsdp")
    side = place % 2
    rows, width = x_ref.shape
    half = rows // 2
    wide = width // groups
    deep = up_ref.shape[1] // groups
    part = wide // 2

    barrier = pltpu.get_barrier_semaphore()
    for j in range(1, groups):
        pl.semaphore_signal(
            barrier, inc=1, device_id={"fsdp": member ^ j}, device_id_type=pl.DeviceIdType.MESH
        )
    for k in range(1, shards):
        pl.semaphore_signal(
            barrier, inc=1, device_id={"ctx": place ^ k}, device_id_type=pl.DeviceIdType.MESH
        )

    def local(src, dst, at):
        copy = pltpu.make_async_copy(src, dst, local_sem.at[at])
        copy.start()
        return copy

    def block(at, size):
        return pl.ds(pl.multiple_of(at, size), size)

    own_rows = block(member * wide, wide)
    loads = [
        local(
            qkv_ref.at[:, block(p * width + member * wide, wide)],
            wqkv.at[own_rows, pl.ds(p * wide, wide)],
            p,
        )
        for p in range(3)
    ]
    loads.append(local(up_ref.at[:, block(member * deep, deep)], wup.at[own_rows, :], 3))
    loads.append(local(cot_ref, grads.at[pl.ds(0, rows)], 4))
    loads.append(local(out_ref, outw, 5))
    loads.append(local(down_ref, down, 6))
    upper = 2 * shards - 1 - place
    for at, (table, held) in enumerate(((cos_ref, cosine), (sin_ref, sine))):
        loads.append(
            local(table.at[block(place * half, half)], held.at[pl.ds(0, half)], 7 + 2 * at)
        )
        loads.append(
            local(table.at[block(upper * half, half)], held.at[pl.ds(half, half)], 8 + 2 * at)
        )
    pl.semaphore_wait(barrier, groups - 1 + shards - 1)

    half_rows = block(member * wide + side * part, part)
    started = []

    def begin(copy):
        copy.start()
        started.append(copy)
        return copy

    q_far = {}
    for j in (2, 3):
        for p in range(3):
            q_far[j, p] = begin(
                remote(
                    qkv_ref.at[block(side * part, part), block(p * width + (member ^ j) * wide, wide)],
                    wqkv.at[half_rows, pl.ds(p * wide, wide)],
                    qs,
                    qr,
                    (j - 2) * 3 + p,
                    {"fsdp": member ^ j},
                )
            )

    tokens = x_ref[...].astype(F32)
    centred = tokens - jnp.mean(tokens, axis=-1, keepdims=True)
    spread = lax.rsqrt(jnp.mean(centred * centred, axis=-1, keepdims=True) + EPS)
    normed[0:rows, :] = (centred * spread * gain_ref[...] + shift_ref[...]).astype(BF16)
    n_near = begin(
        remote(normed.at[pl.ds(0, rows)], normed.at[pl.ds(rows, rows)], rs, rr, 1, {"fsdp": member ^ 1})
    )
    q_near = [
        begin(
            remote(
                qkv_ref.at[:, block(p * width + (member ^ 1) * wide, wide)],
                wqkv.at[own_rows, pl.ds(p * wide, wide)],
                qs,
                qr,
                6 + p,
                {"fsdp": member ^ 1},
            )
        )
        for p in range(3)
    ]

    q_side = []
    for j in (2, 3):
        for p in range(3):
            q_far[j, p].wait_recv()
            spot = wqkv.at[block((member ^ j) * wide + side * part, part), pl.ds(p * wide, wide)]
            q_side.append(
                begin(remote(spot, spot, qs, qr, 9 + (j - 2) * 3 + p, {"ctx": place ^ 1}))
            )
    n_far = begin(
        remote(
            normed.at[pl.ds(0, rows)], normed.at[pl.ds(2 * rows, rows)], rs, rr, 0, {"fsdp": member ^ 2}
        )
    )
    for at in (0, 1, 2, 7, 8, 9, 10):
        loads[at].wait()
    for copy in q_near + q_side:
        copy.wait_recv()
    n_near.wait_recv()
    arrivals = []
    stores = []

    def keep(src, dst):
        copy = pltpu.make_async_copy(src, dst, store_sem.at[len(stores)])
        copy.start()
        stores.append(copy)

    def owner(target):
        return target // (slot_groups * dup), (target // dup) % slot_groups

    for item in range(items):
        if item == items - 1:
            n_far.wait_recv()
            n_last = begin(
                remote(
                    normed.at[pl.ds(2 * rows, rows)],
                    normed.at[pl.ds(3 * rows, rows)],
                    rs,
                    rr,
                    2,
                    {"fsdp": member ^ 1},
                )
            )
            loads[4].wait()
            g_far = begin(
                remote(
                    grads.at[pl.ds(0, rows)],
                    grads.at[pl.ds(2 * rows, rows)],
                    rs,
                    rr,
                    3,
                    {"fsdp": member ^ 2},
                )
            )
            g_near = begin(
                remote(
                    grads.at[pl.ds(0, rows)],
                    grads.at[pl.ds(rows, rows)],
                    rs,
                    rr,
                    4,
                    {"fsdp": member ^ 1},
                )
            )
            u_near = begin(
                remote(
                    up_ref.at[:, block((member ^ 1) * deep, deep)],
                    wup.at[own_rows, :],
                    us,
                    ur,
                    0,
                    {"fsdp": member ^ 1},
                )
            )
            n_last.wait_recv()

        def project(p, _, item=item):
            for g in range(slot_groups):
                slot = item * slot_groups + g
                acc = qkv_bias_ref[p * groups + member] + jnp.dot(
                    normed[slot * rows : (slot + 1) * rows, :],
                    wqkv[:, block(p * wide, wide)],
                    preferred_element_type=F32,
                )
                for h in range(pairs):
                    cols = acc[:, h * LANES : (h + 1) * LANES]
                    turned = turn(cols, cosine[...], sine[...])
                    stage[item, h, g, p] = jnp.where(p < 2, turned, cols).astype(BF16)
            return 0

        lax.fori_loop(0, 3, project, 0)
        for k in range(1, shards):
            pair, group = owner(place ^ k)
            arrivals.append(
                begin(
                    remote(
                        stage.at[item, pair, group],
                        qkv_in.at[item, place],
                        as_,
                        ar,
                        item * shards + k,
                        {"ctx": place ^ k},
                    )
                )
            )
        pair, group = owner(place)
        keep(stage.at[item, pair, group], qkv_in.at[item, place])

    g_far.wait_recv()
    g_last = begin(
        remote(
            grads.at[pl.ds(2 * rows, rows)],
            grads.at[pl.ds(3 * rows, rows)],
            rs,
            rr,
            5,
            {"fsdp": member ^ 1},
        )
    )
    tile = 512
    tiles = deep // tile
    u_far = {}
    for c in range(tiles):
        for j in (2, 3):
            u_far[c, j] = begin(
                remote(
                    up_ref.at[block(side * part, part), block((member ^ j) * deep + c * tile, tile)],
                    wup.at[half_rows, pl.ds(c * tile, tile)],
                    us,
                    ur,
                    1 + c * 2 + j - 2,
                    {"fsdp": member ^ j},
                )
            )
    g_near.wait_recv()
    loads[5].wait()
    g_last.wait_recv()
    for slot in range(groups):
        item, g = slot // slot_groups, slot % slot_groups
        att = contract_cols(grads[slot * rows : (slot + 1) * rows, :], outw[...]).astype(BF16)
        for h in range(pairs):
            dstage[h, g, item] = att[:, h * LANES : (h + 1) * LANES]
    for k in range(1, shards):
        pair, group = owner(place ^ k)
        arrivals.append(
            begin(
                remote(
                    dstage.at[pair, group],
                    do_in.at[place],
                    ds_,
                    dr,
                    k,
                    {"ctx": place ^ k},
                )
            )
        )
    pair, group = owner(place)
    keep(dstage.at[pair, group], do_in.at[place])
    keep(normed, normed_out)
    keep(grads, grads_out)
    keep(wqkv, wqkv_out)

    loads[6].wait()
    high = 2 * rows

    def back(at, _):
        r, c = block((at % 2) * high, high), block((at // 2) * tile, tile)
        dh[r, c] = contract_cols(grads[r, :], down[c, :])
        return 0

    def forward(c):
        cols = pl.ds(c * tile, tile)

        def one(at, _):
            r = block(at * high, high)
            value = matmul(normed[r, :], wup[:, cols]) + up_bias_ref[member, :, cols]
            hidden[r, cols] = gelu_value(value).astype(BF16)
            du[r, cols] = (dh[r, cols] * gelu_slope(value)).astype(BF16)
            return 0

        lax.fori_loop(0, 2, one, 0)

    lax.fori_loop(0, 2 * tiles, back, 0)
    loads[3].wait()
    u_near.wait_recv()
    u_side = []
    for c in range(tiles + 1):
        if c < tiles:
            for j in (2, 3):
                u_far[c, j].wait_recv()
                spot = wup.at[
                    block((member ^ j) * wide + side * part, part), pl.ds(c * tile, tile)
                ]
                u_side.append(
                    begin(
                        remote(spot, spot, us, ur, 1 + 2 * (tiles + c) + j - 2, {"ctx": place ^ 1})
                    )
                )
        if c > 0:
            u_side[2 * c - 2].wait_recv()
            u_side[2 * c - 1].wait_recv()
            forward(c - 1)
    keep(wup, wup_out)
    keep(hidden, hidden_out)
    keep(du, du_out)
    for copy in arrivals:
        copy.wait_recv()
    for copy in started:
        copy.wait_send()
    for copy in stores:
        copy.wait()


def begin_layer(
    x, gain, shift, cot, qkv_w, qkv_b, up_w, up_b, out_w, down_w, cosine, sine,
    shards, groups, pairs, slot_groups, items, dup,
):
    rows, width = x.shape
    wide = width // groups
    deep = up_w.shape[1] // groups
    total = rows * groups
    whole = pl.BlockSpec(memory_space=pltpu.VMEM)
    apart = pl.BlockSpec(memory_space=pl.ANY)
    dma = pltpu.SemaphoreType.DMA
    shape = jax.ShapeDtypeStruct
    stores = items + 1 + 6
    return pl.pallas_call(
        partial(start_kernel, shards, groups, pairs, slot_groups, items, dup),
        out_shape=[
            shape((total, width), BF16),
            shape((total, width), BF16),
            shape((width, 3 * wide), BF16),
            shape((width, deep), BF16),
            shape((total, deep), BF16),
            shape((total, deep), BF16),
            shape((items, shards, 3, rows, LANES), BF16),
            shape((shards, items, rows, LANES), BF16),
        ],
        in_specs=[whole, whole, whole, apart, apart, whole, apart, whole, apart, apart, apart, apart],
        out_specs=[apart] * 8,
        scratch_shapes=[
            pltpu.VMEM((total, width), BF16),
            pltpu.VMEM((total, width), BF16),
            pltpu.VMEM((width, 3 * wide), BF16),
            pltpu.VMEM((width, deep), BF16),
            pltpu.VMEM((deep, width), BF16),
            pltpu.VMEM((wide, width), BF16),
            pltpu.VMEM((rows, LANES), F32),
            pltpu.VMEM((rows, LANES), F32),
            pltpu.VMEM((items, pairs, slot_groups, 3, rows, LANES), BF16),
            pltpu.VMEM((pairs, slot_groups, items, rows, LANES), BF16),
            pltpu.VMEM((total, deep), F32),
            pltpu.VMEM((total, deep), BF16),
            pltpu.VMEM((total, deep), BF16),
            dma((11,)),
            dma((stores,)),
            dma((15,)),
            dma((15,)),
            dma((1 + 4 * (deep // 512),)),
            dma((1 + 4 * (deep // 512),)),
            dma((6,)),
            dma((6,)),
            dma((items * shards,)),
            dma((items * shards,)),
            dma((shards,)),
            dma((shards,)),
        ],
        compiler_params=pltpu.CompilerParams(
            collective_id=0, has_side_effects=True, vmem_limit_bytes=62 * 2**20
        ),
        cost_estimate=pl.CostEstimate(
            flops=2 * total * width * (3 * wide + wide + 2 * deep),
            bytes_accessed=60 * 2**20,
            transcendentals=total * deep,
        ),
    )(
        x,
        gain.reshape(1, width),
        shift.reshape(1, width),
        cot,
        qkv_w,
        qkv_b.reshape(3 * groups, 1, wide),
        up_w,
        up_b.reshape(groups, 1, deep),
        out_w,
        down_w,
        cosine,
        sine,
    )


def attend_kernel(
    shards, heads, dup, qkv_ref, do_ref, cos_ref, sin_ref, out_ref, s_buf, dp_buf, dk_buf, dv_buf
):
    half = qkv_ref.shape[-2]
    block = 2 * half
    count = shards
    base = lax.axis_index("ctx") % dup
    lane = lax.broadcasted_iota(jnp.int32, (block, LANES), 1) // HD
    own = [lane == (base + h) for h in range(heads)]
    scale = HD**-0.5

    def where_is(item):
        low = item < count // 2
        first = jnp.where(low, 2 * item, 2 * count - 1 - 2 * item)
        second = jnp.where(low, 2 * item + 1, 2 * count - 2 - 2 * item)
        return first, second, jnp.where(low, 0, 1)

    def load(part, item):
        first, second, side = where_is(item)
        return jnp.concatenate(
            [qkv_ref[0, first, part, side], qkv_ref[0, second, part, side]], axis=0
        )

    def load_do(item):
        first, second, side = where_is(item)
        return jnp.concatenate([do_ref[first, 0, side], do_ref[second, 0, side]], axis=0)

    def store(part, item, value):
        first, second, side = where_is(item)
        out_ref[first, 0, part, side] = value[:half].astype(out_ref.dtype)
        out_ref[second, 0, part, side] = value[half:].astype(out_ref.dtype)

    dk_buf[...] = jnp.zeros_like(dk_buf)
    dv_buf[...] = jnp.zeros_like(dv_buf)
    nothing = jnp.zeros((block, LANES), BF16)
    key_at = lax.broadcasted_iota(jnp.int32, (block, block), 0)
    query_at = lax.broadcasted_iota(jnp.int32, (block, block), 1)

    def per_query(item, _):
        query = load(0, item) * jnp.asarray(scale, BF16)
        grad = load_do(item)
        queries = [jnp.where(own[h], query, nothing) for h in range(heads)]
        grads = [jnp.where(own[h], grad, nothing) for h in range(heads)]

        def measure(key_item, state, diagonal):
            keys, values = load(1, key_item), load(2, key_item)
            new = []
            for h in range(heads):
                top, total, dot = state[h]
                s = contract_cols(keys, queries[h])
                if diagonal:
                    s = jnp.where(key_at <= query_at, s, -1e30)
                dp = contract_cols(values, grads[h])
                s_buf[h, key_item] = s
                dp_buf[h, key_item] = dp
                new_top = jnp.maximum(top, jnp.max(s, axis=0, keepdims=True))
                e = jnp.exp(s - new_top)
                fade = jnp.exp(top - new_top)
                new.append(
                    (
                        new_top,
                        total * fade + jnp.sum(e, axis=0, keepdims=True),
                        dot * fade + jnp.sum(e * dp, axis=0, keepdims=True),
                    )
                )
            return tuple(new)

        zero = jnp.zeros((1, block), F32)
        start = tuple((zero - 1e30, zero, zero) for _ in range(heads))
        state = lax.fori_loop(0, item, lambda k, st: measure(k, st, False), start)
        state = measure(item, state, True)
        logs = [top + jnp.log(total) for top, total, _ in state]
        deltas = [dot / total for _, total, dot in state]

        def apply(key_item, state):
            keys, values = load(1, key_item), load(2, key_item)
            out, dq = state
            dk, dv = dk_buf[key_item], dv_buf[key_item]
            for h in range(heads):
                p = jnp.exp(s_buf[h, key_item] - logs[h])
                ds = (p * (dp_buf[h, key_item] - deltas[h])).astype(BF16)
                p = p.astype(BF16)
                dv = dv + matmul(p, grads[h])
                dk = dk + matmul(ds, queries[h])
                out = out + jnp.where(own[h], contract_rows(p, values), 0.0)
                dq = dq + jnp.where(own[h], contract_rows(ds, keys), 0.0)
            dk_buf[key_item] = dk
            dv_buf[key_item] = dv
            return out, dq

        empty = jnp.zeros((block, LANES), F32)
        out, dq = lax.fori_loop(0, item + 1, apply, (empty, empty))
        store(0, item, out)
        rows = pl.ds(pl.multiple_of(item * block, block), block)
        store(1, item, turn(dq * scale, cos_ref[rows, :], -sin_ref[rows, :]))
        return 0

    lax.fori_loop(0, count, per_query, 0)

    def finish(item, _):
        rows = pl.ds(pl.multiple_of(item * block, block), block)
        store(2, item, turn(dk_buf[item], cos_ref[rows, :], -sin_ref[rows, :]))
        store(3, item, dv_buf[item])
        return 0

    lax.fori_loop(0, count, finish, 0)


def attend(qkv, grads, item, cosine, sine, heads, dup):
    shards, items = qkv.shape[1], 1
    half = qkv.shape[-2]
    tokens = shards * 2 * half
    block = 2 * half
    once = pl.Buffered(1)
    pairs = shards * (shards + 1) // 2 * items * heads
    return pl.pallas_call(
        partial(attend_kernel, shards, heads, dup),
        grid=(items,),
        out_shape=jax.ShapeDtypeStruct((shards, items, 4, 2, half, LANES), BF16),
        in_specs=[
            pl.BlockSpec(
                (1, shards, 3, 2, half, LANES), lambda i: (item, 0, 0, 0, 0, 0), pipeline_mode=once
            ),
            pl.BlockSpec(
                (shards, 1, 2, half, LANES), lambda i: (0, item, 0, 0, 0), pipeline_mode=once
            ),
            pl.BlockSpec((tokens, LANES), lambda i: (0, 0), pipeline_mode=once),
            pl.BlockSpec((tokens, LANES), lambda i: (0, 0), pipeline_mode=once),
        ],
        out_specs=pl.BlockSpec(
            (shards, 1, 4, 2, half, LANES), lambda i: (0, i, 0, 0, 0, 0), pipeline_mode=once
        ),
        scratch_shapes=[
            pltpu.VMEM((heads, shards, block, block), F32),
            pltpu.VMEM((heads, shards, block, block), F32),
            pltpu.VMEM((shards, block, LANES), F32),
            pltpu.VMEM((shards, block, LANES), F32),
        ],
        compiler_params=pltpu.CompilerParams(vmem_limit_bytes=58 * 2**20),
        cost_estimate=pl.CostEstimate(
            flops=pairs * 5 * 2 * block * block * 256,
            bytes_accessed=16 * 2**20,
            transcendentals=2 * pairs * block * block,
        ),
    )(qkv, grads, cosine, sine)


def middle_kernel(
    items,
    heads,
    qkv_in,
    do_in,
    hidden_in,
    normed_in,
    grads_in,
    du_in,
    cos_in,
    sin_in,
    back_in,
    down_out,
    far_out,
    up_out,
    d_send,
    d_keep,
    d_recv,
    d_last,
    u_send,
    u_keep,
    u_recv,
    u_last,
    out,
    local_sem,
    store_sem,
    own_sem,
    ds_,
    dr,
    us,
    ur,
    bs,
    br,
):
    place = lax.axis_index("ctx")
    shards = out.shape[1]
    x_at, z_at = place % 2, (place // 2) % 2
    top_at = place // 4
    near, over = {"ctx": place ^ 1}, {"ctx": place ^ 2}
    barrier = pltpu.get_barrier_semaphore()
    for k in range(1, shards):
        pl.semaphore_signal(
            barrier, inc=1, device_id={"ctx": place ^ k}, device_id_type=pl.DeviceIdType.MESH
        )

    def fetch(src, dst, at):
        copy = pltpu.make_async_copy(src, dst, local_sem.at[at])
        copy.start()
        return copy

    def block(at, size):
        return pl.ds(pl.multiple_of(at, size), size)

    members, tops, lanes, width = u_send.shape
    wide = lanes * 2 * tops
    units = d_send.shape[2]

    def down_one(top):
        spot = (1 - top_at) if top == 0 else top_at
        return remote(d_send.at[spot], d_recv.at[spot], ds_, dr, top, near)

    def down_two():
        return remote(d_send.at[1 - top_at, 0], d_last, ds_, dr, tops, over)

    def up_one(member):
        return remote(u_send.at[member], u_recv.at[member], us, ur, member, over)

    piece = lanes // 2

    def up_two(member):
        return remote(
            u_send.at[member, :, pl.ds(0, piece)], u_last.at[member], us, ur, members + member, near
        )

    def back_one(item, part, k):
        return remote(
            out.at[item, place ^ k, :, part],
            back_in.at[item, place, :, part],
            bs,
            br,
            (item * 2 + part) * shards + k,
            {"ctx": place ^ k},
        )

    def back_own(item, part):
        return pltpu.make_async_copy(
            out.at[item, place, :, part],
            back_in.at[item, place, :, part],
            own_sem.at[item * 2 + part],
        )

    def sums(hidden, normed, grads, du):
        loads = [
            fetch(src, dst, at)
            for at, (src, dst) in enumerate(
                ((hidden_in, hidden), (grads_in, grads), (normed_in, normed), (du_in, du))
            )
        ]
        loads[0].wait()
        loads[1].wait()
        pl.semaphore_wait(barrier, shards - 1)

        def down(which, into, top):
            def one(low, _):
                at = ((top * 2 + low) * 2 + which) * units
                into[top, low] = contract_rows(hidden[:, block(at, units)], grads[...]).astype(BF16)
                return 0

            lax.fori_loop(0, 2, one, 0)

        for top in range(tops):
            down(1 - x_at, d_send, (1 - top_at) if top == 0 else top_at)
            down_one(top).start()
        loads[2].wait()
        loads[3].wait()

        def up(which, into, member):
            def one(top, _):
                at = member * wide + (top * 2 + which) * lanes
                into[member, top] = contract_rows(normed[:, block(at, lanes)], du[...]).astype(BF16)
                return 0

            lax.fori_loop(0, tops, one, 0)

        for member in range(members):
            up(1 - z_at, u_send, member)
            up_one(member).start()
        for top in range(tops):
            down(x_at, d_keep, top)
        for member in range(members):
            up(z_at, u_keep, member)

    tokens = hidden_in.shape[0]
    pl.run_scoped(
        sums,
        pltpu.VMEM(hidden_in.shape, BF16),
        pltpu.VMEM((tokens, width), BF16),
        pltpu.VMEM((tokens, width), BF16),
        pltpu.VMEM(du_in.shape, BF16),
    )

    half = out.shape[-2]
    size = 2 * half

    def attention(qkv, do, cosine, sine, s_buf, dp_buf, dk_buf, dv_buf):
        loads = []
        for item in range(items):
            loads.append(fetch(qkv_in.at[item], qkv.at[item], 2 * item))
            loads.append(fetch(do_in.at[:, item], do.at[item], 2 * item + 1))
        loads.append(fetch(cos_in, cosine, 2 * items))
        loads.append(fetch(sin_in, sine, 2 * items + 1))
        for load in loads:
            load.wait()
        lane = lax.broadcasted_iota(jnp.int32, (size, LANES), 1) // HD
        own = [lane == h for h in range(heads)]
        key_at = lax.broadcasted_iota(jnp.int32, (size, size), 0)
        query_at = lax.broadcasted_iota(jnp.int32, (size, size), 1)
        nothing = jnp.zeros((size, LANES), BF16)
        scale = HD**-0.5

        for item in range(items):
            dk_buf[...] = jnp.zeros_like(dk_buf)
            dv_buf[...] = jnp.zeros_like(dv_buf)
            for part in (1, 0):

                def where_is(at, part=part):
                    if part:
                        return 2 * shards - 1 - 2 * at, 2 * shards - 2 - 2 * at
                    return 2 * at, 2 * at + 1

                def shard_of(at):
                    low = at < shards // 2
                    first = jnp.where(low, 2 * at, 2 * shards - 1 - 2 * at)
                    second = jnp.where(low, 2 * at + 1, 2 * shards - 2 - 2 * at)
                    return first, second, jnp.where(low, 0, 1)

                def load(which, at, item=item):
                    first, second, side = shard_of(at)
                    return jnp.concatenate(
                        [qkv[item, first, which, side], qkv[item, second, which, side]], axis=0
                    )

                def store(which, at, value, item=item, part=part, where_is=where_is):
                    first, second = where_is(at)
                    out[item, first, which, part] = value[:half].astype(BF16)
                    out[item, second, which, part] = value[half:].astype(BF16)

                def per_query(at, _, item=item, load=load, store=store, shard_of=shard_of):
                    query = load(0, at) * jnp.asarray(scale, BF16)
                    first, second, where = shard_of(at)
                    grad = jnp.concatenate([do[item, first, where], do[item, second, where]], axis=0)
                    queries = [jnp.where(own[h], query, nothing) for h in range(heads)]
                    grads = [jnp.where(own[h], grad, nothing) for h in range(heads)]

                    def measure(key, state, diagonal):
                        keys, values = load(1, key), load(2, key)
                        new = []
                        for h in range(heads):
                            top, total, dot = state[h]
                            s = contract_cols(keys, queries[h])
                            if diagonal:
                                s = jnp.where(key_at <= query_at, s, -1e30)
                            dp = contract_cols(values, grads[h])
                            s_buf[h, key] = s
                            dp_buf[h, key] = dp
                            new_top = jnp.maximum(top, jnp.max(s, axis=0, keepdims=True))
                            e = jnp.exp(s - new_top)
                            fade = jnp.exp(top - new_top)
                            new.append(
                                (
                                    new_top,
                                    total * fade + jnp.sum(e, axis=0, keepdims=True),
                                    dot * fade + jnp.sum(e * dp, axis=0, keepdims=True),
                                )
                            )
                        return tuple(new)

                    zero = jnp.zeros((1, size), F32)
                    start = tuple((zero - 1e30, zero, zero) for _ in range(heads))
                    state = lax.fori_loop(0, at, lambda k, st: measure(k, st, False), start)
                    state = measure(at, state, True)
                    logs = [top + jnp.log(total) for top, total, _ in state]
                    deltas = [dot / total for _, total, dot in state]

                    def apply(key, state):
                        keys, values = load(1, key), load(2, key)
                        attended, dq = state
                        dk, dv = dk_buf[key], dv_buf[key]
                        for h in range(heads):
                            p = jnp.exp(s_buf[h, key] - logs[h])
                            ds = (p * (dp_buf[h, key] - deltas[h])).astype(BF16)
                            p = p.astype(BF16)
                            dv = dv + matmul(p, grads[h])
                            dk = dk + matmul(ds, queries[h])
                            attended = attended + jnp.where(own[h], contract_rows(p, values), 0.0)
                            dq = dq + jnp.where(own[h], contract_rows(ds, keys), 0.0)
                        dk_buf[key] = dk
                        dv_buf[key] = dv
                        return attended, dq

                    empty = jnp.zeros((size, LANES), F32)
                    attended, dq = lax.fori_loop(0, at + 1, apply, (empty, empty))
                    store(0, at, attended)
                    rows = block(at * size, size)
                    store(1, at, turn(dq * scale, cosine[rows, :], -sine[rows, :]))
                    return 0

                low = part * (shards // 2)
                lax.fori_loop(low, low + shards // 2, per_query, 0)

                def finish(at, _, store=store):
                    rows = block(at * size, size)
                    store(2, at, turn(dk_buf[at], cosine[rows, :], -sine[rows, :]))
                    store(3, at, dv_buf[at])
                    return 0

                lax.fori_loop(low, low + shards // 2, finish, 0)
                for k in range(1, shards):
                    back_one(item, part, k).start()
                back_own(item, part).start()

    pl.run_scoped(
        attention,
        pltpu.VMEM((items,) + qkv_in.shape[1:], BF16),
        pltpu.VMEM((items, shards) + do_in.shape[2:], BF16),
        pltpu.VMEM(cos_in.shape, F32),
        pltpu.VMEM(sin_in.shape, F32),
        pltpu.VMEM((heads, shards, size, size), F32),
        pltpu.VMEM((heads, shards, size, size), F32),
        pltpu.VMEM((shards, size, LANES), F32),
        pltpu.VMEM((shards, size, LANES), F32),
    )

    stores = []

    def keep(src, dst):
        copy = pltpu.make_async_copy(src, dst, store_sem.at[len(stores)])
        copy.start()
        stores.append(copy)

    theirs = block((1 - x_at) * piece, piece)
    mine = block(x_at * piece, piece)
    down_one(0).wait()
    d_send[1 - top_at, 0] = (
        d_keep[1 - top_at, 1 - z_at].astype(F32) + d_recv[1 - top_at, 1 - z_at].astype(F32)
    ).astype(BF16)
    down_two().start()
    for member in range(members):
        up_one(member).wait()

        def pass_up(top, _, member=member):
            u_send[member, top, pl.ds(0, piece)] = (
                u_keep[member, top, theirs].astype(F32) + u_recv[member, top, theirs].astype(F32)
            ).astype(BF16)
            return 0

        lax.fori_loop(0, tops, pass_up, 0)
        up_two(member).start()
    down_one(1).wait()

    def add_down(low, _):
        d_keep[top_at, low] = (
            d_keep[top_at, low].astype(F32) + d_recv[top_at, low].astype(F32)
        ).astype(BF16)
        return 0

    lax.fori_loop(0, 2, add_down, 0)
    keep(d_keep.at[top_at], down_out)
    down_two().wait_recv()
    d_last[...] = (
        d_keep[1 - top_at, z_at].astype(F32)
        + d_recv[1 - top_at, z_at].astype(F32)
        + d_last[...].astype(F32)
    ).astype(BF16)
    keep(d_last, far_out)
    for member in range(members):
        up_two(member).wait_recv()

        def add_up(top, _, member=member):
            u_last[member, top] = (
                u_keep[member, top, mine].astype(F32)
                + u_recv[member, top, mine].astype(F32)
                + u_last[member, top].astype(F32)
            ).astype(BF16)
            return 0

        lax.fori_loop(0, tops, add_up, 0)
        keep(u_last.at[member], up_out.at[member])
    for item in range(items):
        for part in (1, 0):
            for k in range(1, shards):
                back_one(item, part, k).wait()
            back_own(item, part).wait()
    down_two().wait_send()
    for member in range(members):
        up_two(member).wait_send()
    for copy in stores:
        copy.wait()


def middle(qkv_in, do_in, hidden, normed, grads, du, cosine, sine, heads, groups):
    items, shards = qkv_in.shape[:2]
    half = qkv_in.shape[-2]
    width = normed.shape[1]
    deep = hidden.shape[1]
    units = deep // shards
    tops = shards // 4
    lanes = width // groups // tops // 2
    apart = pl.BlockSpec(memory_space=pl.ANY)
    dma = pltpu.SemaphoreType.DMA
    shape = jax.ShapeDtypeStruct
    pairs = shards * (shards + 1) // 2 * items * heads
    return pl.pallas_call(
        partial(middle_kernel, items, heads),
        out_shape=[
            shape((items, shards, 4, 2, half, LANES), BF16),
            shape((2, units, width), BF16),
            shape((units, width), BF16),
            shape((groups, tops, lanes // 2, deep), BF16),
        ],
        in_specs=[apart] * 8,
        out_specs=[apart] * 4,
        scratch_shapes=[
            pltpu.VMEM((tops, 2, units, width), BF16),
            pltpu.VMEM((tops, 2, units, width), BF16),
            pltpu.VMEM((tops, 2, units, width), BF16),
            pltpu.VMEM((units, width), BF16),
            pltpu.VMEM((groups, tops, lanes, deep), BF16),
            pltpu.VMEM((groups, tops, lanes, deep), BF16),
            pltpu.VMEM((groups, tops, lanes, deep), BF16),
            pltpu.VMEM((groups, tops, lanes // 2, deep), BF16),
            pltpu.VMEM((items, shards, 4, 2, half, LANES), BF16),
            dma((max(4, 2 * items + 2),)),
            dma((tops + groups,)),
            dma((2 * items,)),
            dma((tops + 1,)),
            dma((tops + 1,)),
            dma((2 * groups,)),
            dma((2 * groups,)),
            dma((2 * items * shards,)),
            dma((2 * items * shards,)),
        ],
        compiler_params=pltpu.CompilerParams(
            collective_id=1, has_side_effects=True, vmem_limit_bytes=63 * 2**20
        ),
        cost_estimate=pl.CostEstimate(
            flops=pairs * 10 * (2 * half) ** 2 * 256 + 8 * width * deep * hidden.shape[0],
            bytes_accessed=40 * 2**20,
            transcendentals=2 * pairs * (2 * half) ** 2,
        ),
    )(qkv_in, do_in, hidden, normed, grads, du, cosine, sine)


FLIGHTS = 64


def finish_kernel(
    items,
    pairs,
    slot_groups,
    back_in,
    normed_in,
    grads_in,
    hidden_in,
    du_in,
    wqkv_in,
    wup_in,
    outw_in,
    down_in,
    d_in,
    far_in,
    u_in,
    x_in,
    cot_in,
    gain_ref,
    out_bias_ref,
    down_bias_ref,
    result_out,
    input_out,
    qkv_out,
    up_out,
    o_out,
    d_out,
    sums_out,
    qkv_land,
    up_land,
    d_two,
    big,
    q_send,
    q_keep,
    q_recv,
    q_two,
    q_three,
    q_done,
    o_send,
    o_keep,
    o_recv,
    o_two,
    o_three,
    d_three,
    u_three,
    u_done,
    p_send,
    p_recv,
    p_own,
    n_send,
    n_recv,
    n_own,
    sums,
    s_recv,
    s_part,
    s_all,
    local_sem,
    store_sem,
    sends,
    recvs,
):
    place = lax.axis_index("ctx")
    member = lax.axis_index("fsdp")
    shards = back_in.shape[1]
    groups, tops, _, piece, qcols = q_send.shape
    rows, width = p_own.shape
    wide = width // groups
    deep = hidden_in.shape[1]
    x_at, z_at, top_at = place % 2, (place // 2) % 2, place // 4
    near, over, far = {"ctx": place ^ 1}, {"ctx": place ^ 2}, {"ctx": place ^ 4}

    barrier = pltpu.get_barrier_semaphore()
    for j in range(1, groups):
        pl.semaphore_signal(
            barrier, inc=1, device_id={"fsdp": member ^ j}, device_id_type=pl.DeviceIdType.MESH
        )
    for k in range(1, shards):
        pl.semaphore_signal(
            barrier, inc=1, device_id={"ctx": place ^ k}, device_id_type=pl.DeviceIdType.MESH
        )

    def block(at, size):
        return pl.ds(pl.multiple_of(at, size), size)

    names = {}

    def flight(name, src, dst, target):
        at = names.setdefault(name, len(names))
        return remote(src, dst, sends, recvs, at, target)

    def fetch(src, dst, at):
        copy = pltpu.make_async_copy(src, dst, local_sem.at[at])
        copy.start()
        return copy

    def core(j):
        return {"fsdp": member ^ j}

    theirs = block((1 - x_at) * piece, piece)
    mine = block(x_at * piece, piece)

    def d_second():
        return flight("d2", d_in.at[1 - z_at], d_two, over)

    def d_last():
        return flight("d", far_in, d_three, far)

    def u_last():
        return flight("u", u_in.at[:, 1 - top_at], u_three, far)

    def o_first(top):
        return flight(("o1", top), o_send.at[top], o_recv.at[top], over)

    def o_second():
        return flight("o2", o_send.at[:, pl.ds(0, piece)], o_two, near)

    def o_last():
        return flight("o3", o_send.at[0, pl.ds(piece, piece)], o_three, far)

    def q_first(f):
        return flight(("q1", f), q_send.at[f], q_recv.at[f], near)

    def q_second(f):
        return flight(("q2", f), q_send.at[f, :, 0], q_two.at[f], over)

    def q_last(f):
        return flight(("q3", f), q_send.at[f, 0, 1], q_three.at[f], far)

    def q_swap(j):
        return flight(("q4", j), q_done.at[member ^ j], qkv_land.at[member], core(j))

    def u_swap(j):
        return flight(("u4", j), u_done.at[member ^ j], up_land.at[member], core(j))

    def rows_last(name, send, recv):
        return flight((name, 3), send.at[0], recv.at[0], core(1))

    def rows_far(name, send, recv):
        return flight((name, 2), send.at[1], recv.at[1], core(2))

    def rows_near(name, send, recv):
        return flight((name, 1), send.at[2], recv.at[2], core(1))

    def sums_one(j):
        return flight(("s1", j), sums, s_recv.at[j - 1], core(j))

    span = width // shards

    def sums_two(k):
        return flight(
            ("s2", k), s_all.at[:, block((place ^ k) * span, span)], s_part.at[k], {"ctx": place ^ k}
        )

    def sums_three(k):
        mine = block(place * span, span)
        return flight(("s3", k), sums_out.at[:, mine], sums_out.at[:, mine], {"ctx": place ^ k})

    pl.semaphore_wait(barrier, groups - 1 + shards - 1)
    d_second().start()
    u_last().start()
    d_last().start()

    def phase_a(normed, grads):
        loads = [fetch(normed_in, normed, 0), fetch(grads_in, grads, 1)]
        for item in range(items):
            for owner in range(shards):
                pair, g = owner // slot_groups, owner % slot_groups
                spot = pl.ds((item * slot_groups + g) * rows, rows)
                for kind in range(4):
                    loads.append(
                        fetch(
                            back_in.at[item, owner, kind],
                            big.at[spot, pl.ds(kind * wide + pair * LANES, LANES)],
                            2 + (item * shards + owner) * 4 + kind,
                        )
                    )
        sums[...] = jnp.zeros_like(sums)
        for load in loads:
            load.wait()

        def out_grad(top, low, into):
            at = (top * 2 + low) * LANES
            into[top] = contract_rows(big[:, block(at, LANES)], grads[...]).astype(BF16)

        for top in range(tops):
            out_grad(top, 1 - z_at, o_send)
            o_first(top).start()

        for f in range(groups):

            def one(at, _, f=f):
                top, low = at // 2, at % 2
                value = contract_rows(
                    normed[:, block(f * wide + at * LANES, LANES)], big[:, wide:]
                )
                first, second = value[:piece], value[piece:]
                q_send[f, top, low] = jnp.where(x_at == 0, second, first).astype(BF16)
                q_keep[f, top, low] = jnp.where(x_at == 0, first, second).astype(BF16)
                return 0

            lax.fori_loop(0, 2 * tops, one, 0)
            q_first(f).start()
        for top in range(tops):
            out_grad(top, z_at, o_keep)
        for kind in range(3):
            cols = big[:, (kind + 1) * wide : (kind + 2) * wide].astype(F32)
            sums[2 + kind : 3 + kind, block(member * wide, wide)] = jnp.sum(
                cols, axis=0, keepdims=True
            )

    total = rows * groups
    pl.run_scoped(
        phase_a, pltpu.VMEM((total, width), BF16), pltpu.VMEM((total, width), BF16)
    )

    tile = 256

    def keep_share(pair, at, value, send, own):
        cols = block(at * tile, tile)
        if pair == 1:
            send[1, :, cols] = value[:rows].astype(BF16)
            send[0, :, cols] = value[rows:].astype(BF16)
        else:
            own[:, cols] = value[:rows]
            send[2, :, cols] = value[rows:].astype(BF16)

    def phase_b(hidden, down, outw):
        loads = [
            fetch(hidden_in, hidden, 0),
            fetch(down_in, down, 1),
            fetch(outw_in, outw, 2),
        ]
        for load in loads:
            load.wait()
        for pair in (1, 0):
            spot = pl.ds(pair * 2 * rows, 2 * rows)

            def one(at, _, pair=pair, spot=spot):
                cols = block(at * tile, tile)
                value = matmul(hidden[spot, :], down[:, cols]) + matmul(
                    big[spot, pl.ds(0, wide)], outw[:, cols]
                )
                keep_share(pair, at, value, p_send, p_own)
                return 0

            lax.fori_loop(0, width // tile, one, 0)
            if pair == 1:
                rows_last("p", p_send, p_recv).start()
            else:
                rows_near("p", p_send, p_recv).start()

    pl.run_scoped(
        phase_b,
        pltpu.VMEM(hidden_in.shape, BF16),
        pltpu.VMEM(down_in.shape, BF16),
        pltpu.VMEM(outw_in.shape, BF16),
    )

    def pass_rows(name, send, recv):
        rows_last(name, send, recv).wait_recv()
        send[1] = (send[1].astype(F32) + recv[0].astype(F32)).astype(BF16)
        rows_far(name, send, recv).start()

    pass_rows("p", p_send, p_recv)

    for top in range(tops):
        o_first(top).wait()
    for top in range(tops):
        o_send[top, pl.ds(0, piece)] = (
            o_keep[top, theirs].astype(F32) + o_recv[top, theirs].astype(F32)
        ).astype(BF16)
    o_second().start()

    def q_pass(f):
        q_first(f).wait()
        for top in range(tops):
            q_send[f, top, 0] = (
                q_keep[f, top, 1 - z_at].astype(F32) + q_recv[f, top, 1 - z_at].astype(F32)
            ).astype(BF16)
        q_second(f).start()

    def q_turn(f):
        q_second(f).wait_recv()
        other = 1 - top_at
        q_send[f, 0, 1] = (
            q_keep[f, other, z_at].astype(F32)
            + q_recv[f, other, z_at].astype(F32)
            + q_two[f, other].astype(F32)
        ).astype(BF16)
        q_last(f).start()

    for f in range(groups // 2):
        q_pass(f)
    def phase_c(du, wup, wqkv):
        loads = [
            fetch(du_in, du, 0),
            fetch(wup_in, wup, 1),
            fetch(wqkv_in, wqkv, 2),
        ]
        for load in loads:
            load.wait()
        for pair in (1, 0):
            spot = pl.ds(pair * 2 * rows, 2 * rows)

            def one(at, _, pair=pair, spot=spot):
                cols = block(at * tile, tile)
                value = contract_cols(du[spot, :], wup[cols, :]) + contract_cols(
                    big[spot, pl.ds(wide, 3 * wide)], wqkv[cols, :]
                )
                keep_share(pair, at, value, n_send, n_own)
                return 0

            lax.fori_loop(0, width // tile, one, 0)
            if pair == 1:
                rows_last("n", n_send, n_recv).start()
            else:
                rows_near("n", n_send, n_recv).start()
        step = deep // groups

        def column_sums(at, _):
            cols = block(at * step, step)
            value = jnp.sum(du[:, cols].astype(F32), axis=0, keepdims=True)
            for j in range(groups):
                sums[5 + j : 6 + j, cols] = jnp.where(member == j, value, 0.0)
            return 0

        lax.fori_loop(0, groups, column_sums, 0)

    pl.run_scoped(
        phase_c,
        pltpu.VMEM(du_in.shape, BF16),
        pltpu.VMEM(wup_in.shape, BF16),
        pltpu.VMEM(wqkv_in.shape, BF16),
    )
    pass_rows("n", n_send, n_recv)
    for f in range(groups // 2, groups):
        q_pass(f)
    for f in range(groups // 2):
        q_turn(f)
    o_second().wait_recv()
    o_send[0, pl.ds(piece, piece)] = (
        o_keep[1 - top_at, mine].astype(F32)
        + o_recv[1 - top_at, mine].astype(F32)
        + o_two[1 - top_at].astype(F32)
    ).astype(BF16)
    o_last().start()

    d_second().wait_recv()

    def phase_d(x, cot, out, d_own, d_more, d_sum, o_sum, u_more, q_full, u_full):
        loads = [
            fetch(x_in, x, 0),
            fetch(cot_in, cot, 1),
            fetch(u_in.at[:, top_at], u_done, 2),
            fetch(d_in.at[z_at], d_own, 3),
            fetch(d_two, d_more, 4),
        ]
        for load in loads:
            load.wait()

        for f in range(groups // 2, groups):
            q_turn(f)
        rows_near("n", n_send, n_recv).wait_recv()
        rows_far("n", n_send, n_recv).wait_recv()
        step = 64

        def normal_part(at, _):
            r = block(at * step, step)
            tokens = x[r, :].astype(F32)
            centred = tokens - jnp.mean(tokens, axis=-1, keepdims=True)
            spread = lax.rsqrt(jnp.mean(centred * centred, axis=-1, keepdims=True) + EPS)
            normal = centred * spread
            dn = n_own[r, :] + n_recv[2, r, :].astype(F32) + n_recv[1, r, :].astype(F32)
            sums[0:1, :] = sums[0:1, :] + jnp.sum(dn * normal, axis=0, keepdims=True)
            sums[1:2, :] = sums[1:2, :] + jnp.sum(dn, axis=0, keepdims=True)
            dnorm = dn * gain_ref[...]
            grad = cot[r, :].astype(F32)
            sums[9:10, :] = sums[9:10, :] + jnp.sum(grad, axis=0, keepdims=True)
            change = spread * (
                dnorm
                - jnp.mean(dnorm, axis=-1, keepdims=True)
                - normal * jnp.mean(dnorm * normal, axis=-1, keepdims=True)
            )
            cot[r, :] = (grad + change).astype(BF16)
            return 0

        lax.fori_loop(0, rows // step, normal_part, 0)
        for j in range(1, groups):
            sums_one(j).start()
        own_input = pltpu.make_async_copy(cot, input_out, store_sem.at[1])
        own_input.start()

        rows_near("p", p_send, p_recv).wait_recv()
        rows_far("p", p_send, p_recv).wait_recv()

        def output_part(at, _):
            r = block(at * step, step)
            value = x[r, :].astype(F32) + p_own[r, :] + p_recv[2, r, :].astype(F32)
            value = value + p_recv[1, r, :].astype(F32) + out_bias_ref[...] + down_bias_ref[...]
            out[r, :] = value.astype(BF16)
            return 0

        lax.fori_loop(0, rows // step, output_part, 0)
        own_out = pltpu.make_async_copy(out, result_out, store_sem.at[2])
        own_out.start()

        u_last().wait_recv()
        for f in range(groups):
            u_done[f] = (
                u_done[f].astype(F32) + u_three[f].astype(F32)
            ).astype(BF16)
        for j in range(1, groups):
            u_swap(j).start()
        u_full[:, block(member * deep, deep)] = u_done[member].astype(F32)

        for j in range(1, groups):
            sums_one(j).wait_recv()
        s_all[...] = sums[...] + s_recv[0] + s_recv[1] + s_recv[2]
        for k in range(1, shards):
            sums_two(k).start()
        d_last().wait_recv()
        d_sum[...] = d_own[...].astype(F32) + d_more[...].astype(F32) + d_three[...].astype(F32)
        own_down = pltpu.make_async_copy(d_sum, d_out, store_sem.at[3])
        own_down.start()

        for f in range(groups):
            q_last(f).wait_recv()
            q_done[f] = (
                q_keep[f, top_at, z_at].astype(F32)
                + q_recv[f, top_at, z_at].astype(F32)
                + q_two[f, top_at].astype(F32)
                + q_three[f].astype(F32)
            ).astype(BF16)
        for j in range(1, groups):
            q_swap(j).start()
        for kind in range(3):
            q_full[:, block(kind * width + member * wide, wide)] = q_done[
                member, :, kind * wide : (kind + 1) * wide
            ].astype(F32)
        o_last().wait_recv()
        o_sum[...] = (
            o_keep[top_at, mine].astype(F32)
            + o_recv[top_at, mine].astype(F32)
            + o_two[top_at].astype(F32)
            + o_three[...].astype(F32)
        )
        own_o = pltpu.make_async_copy(o_sum, o_out, store_sem.at[5])
        own_o.start()
        for k in range(1, shards):
            sums_two(k).wait()
        cols = block(place * span, span)
        value = s_all[:, cols]
        for k in range(1, shards):
            value = value + s_part[k]
        sums_out[:, cols] = value
        for k in range(1, shards):
            sums_three(k).start()

        for j in range(1, groups):
            u_swap(j).wait_recv()
        for copy in (own_input, own_out):
            copy.wait()
        u_loads = [
            fetch(up_land.at[member ^ j], u_more.at[j], j) for j in range(1, groups)
        ]
        for j in range(1, groups):
            u_loads[j - 1].wait()
            u_full[:, block((member ^ j) * deep, deep)] = u_more[j].astype(F32)
        own_up = pltpu.make_async_copy(u_full, up_out, store_sem.at[0])
        own_up.start()
        for j in range(1, groups):
            q_swap(j).wait_recv()
        q_loads = [
            fetch(qkv_land.at[member ^ j], q_three.at[j], j) for j in range(1, groups)
        ]
        for j in range(1, groups):
            q_loads[j - 1].wait()
            for kind in range(3):
                q_full[:, block(kind * width + (member ^ j) * wide, wide)] = q_three[
                    j, :, kind * wide : (kind + 1) * wide
                ].astype(F32)
        own_q = pltpu.make_async_copy(q_full, qkv_out, store_sem.at[4])
        own_q.start()
        for copy in (own_up, own_down, own_q, own_o):
            copy.wait()

    pl.run_scoped(
        phase_d,
        pltpu.VMEM((rows, width), BF16),
        pltpu.VMEM((rows, width), BF16),
        pltpu.VMEM((rows, width), BF16),
        pltpu.VMEM(d_three.shape, BF16),
        pltpu.VMEM(d_three.shape, BF16),
        pltpu.VMEM(d_three.shape, F32),
        pltpu.VMEM((piece, width), F32),
        pltpu.VMEM(u_done.shape, BF16),
        pltpu.VMEM((piece, 3 * width), F32),
        pltpu.VMEM((piece, groups * deep), F32),
    )
    d_second().wait_send()
    u_last().wait_send()
    d_last().wait_send()
    o_second().wait_send()
    o_last().wait_send()
    for f in range(groups):
        q_second(f).wait_send()
        q_last(f).wait_send()
    for j in range(1, groups):
        q_swap(j).wait_send()
        u_swap(j).wait_send()
        sums_one(j).wait_send()
    for name, send, recv in (("p", p_send, p_recv), ("n", n_send, n_recv)):
        rows_last(name, send, recv).wait_send()
        rows_far(name, send, recv).wait_send()
        rows_near(name, send, recv).wait_send()
    for k in range(1, shards):
        sums_three(k).wait()


def finish(
    back_in, normed, grads, hidden, du, wqkv, wup, outw, down, d_sum, far_sum, u_sum,
    x, cot, gain, out_bias, down_bias, groups, slot_groups,
):
    items, shards = back_in.shape[:2]
    rows, width = x.shape
    wide = width // groups
    deep = hidden.shape[1]
    tops = shards // 4
    piece = wide // shards
    pairs = wide // LANES
    units = deep // shards
    apart = pl.BlockSpec(memory_space=pl.ANY)
    whole = pl.BlockSpec(memory_space=pltpu.VMEM)
    dma = pltpu.SemaphoreType.DMA
    shape = jax.ShapeDtypeStruct
    return pl.pallas_call(
        partial(finish_kernel, items, pairs, slot_groups),
        out_shape=[
            shape((rows, width), BF16),
            shape((rows, width), BF16),
            shape((piece, 3 * width), F32),
            shape((piece, groups * deep), F32),
            shape((piece, width), F32),
            shape((units, width), F32),
            shape((16, width), F32),
            shape((groups, piece, 3 * wide), BF16),
            shape((groups, piece, deep), BF16),
            shape((units, width), BF16),
        ],
        in_specs=[apart] * 14 + [whole] * 3,
        out_specs=[apart] * 6 + [whole] + [apart] * 3,
        scratch_shapes=[
            pltpu.VMEM((rows * groups, 4 * wide), BF16),
            pltpu.VMEM((groups, tops, 2, piece, 3 * wide), BF16),
            pltpu.VMEM((groups, tops, 2, piece, 3 * wide), BF16),
            pltpu.VMEM((groups, tops, 2, piece, 3 * wide), BF16),
            pltpu.VMEM((groups, tops, piece, 3 * wide), BF16),
            pltpu.VMEM((groups, piece, 3 * wide), BF16),
            pltpu.VMEM((groups, piece, 3 * wide), BF16),
            pltpu.VMEM((tops, 2 * piece, width), BF16),
            pltpu.VMEM((tops, 2 * piece, width), BF16),
            pltpu.VMEM((tops, 2 * piece, width), BF16),
            pltpu.VMEM((tops, piece, width), BF16),
            pltpu.VMEM((piece, width), BF16),
            pltpu.VMEM((units, width), BF16),
            pltpu.VMEM((groups, piece, deep), BF16),
            pltpu.VMEM((groups, piece, deep), BF16),
            pltpu.VMEM((3, rows, width), BF16),
            pltpu.VMEM((3, rows, width), BF16),
            pltpu.VMEM((rows, width), F32),
            pltpu.VMEM((3, rows, width), BF16),
            pltpu.VMEM((3, rows, width), BF16),
            pltpu.VMEM((rows, width), F32),
            pltpu.VMEM((16, width), F32),
            pltpu.VMEM((3, 16, width), F32),
            pltpu.VMEM((shards, 16, width // shards), F32),
            pltpu.VMEM((16, width), F32),
            dma((2 + items * shards * 4,)),
            dma((6,)),
            dma((FLIGHTS,)),
            dma((FLIGHTS,)),
        ],
        compiler_params=pltpu.CompilerParams(
            collective_id=2, has_side_effects=True, vmem_limit_bytes=63 * 2**20
        ),
        cost_estimate=pl.CostEstimate(
            flops=2 * rows * groups * width * (2 * deep + 8 * wide),
            bytes_accessed=60 * 2**20,
            transcendentals=0,
        ),
    )(
        back_in, normed, grads, hidden, du, wqkv, wup, outw, down, d_sum, far_sum, u_sum, x, cot,
        gain.reshape(1, width), out_bias.reshape(1, width), down_bias.reshape(1, width),
    )


def scatter_sum(parts, axis_at, place, bits):
    lead, tail = parts.shape[:axis_at], parts.shape[axis_at + 1 :]
    total = len(bits)
    left = list(range(total - 1, -1, -1))
    value = parts.reshape(lead + (2,) * total + tail)
    for bit in bits:
        at = axis_at + left.index(bit)
        left.remove(bit)
        mine = (place >> bit) & 1
        send = lax.dynamic_index_in_dim(value, 1 - mine, at, keepdims=False)
        keep = lax.dynamic_index_in_dim(value, mine, at, keepdims=False)
        got = swap(send.astype(BF16), "ctx", 1 << bit)
        value = keep.astype(F32) + got.astype(F32)
    return value


def scatter_rows(parts):
    last = swap(parts[3].astype(BF16), "fsdp", 1).astype(F32)
    far = swap((parts[2] + last).astype(BF16), "fsdp", 2).astype(F32)
    near = swap(parts[1].astype(BF16), "fsdp", 1).astype(F32)
    return parts[0] + near + far


def total_sum(value):
    for axis in ("fsdp", "ctx"):
        bit = 1
        while bit < lax.axis_size(axis):
            value = value + swap(value, axis, bit)
            bit *= 2
    return value


def on_device(
    inputs,
    norm_gain,
    norm_shift,
    qkv_weight,
    qkv_bias,
    out_weight,
    out_bias,
    up_weight,
    up_bias,
    down_weight,
    down_bias,
    cotangent,
):
    rows = inputs.shape[1]
    width = inputs.shape[2]
    hidden_width = up_weight.shape[1]
    half = rows // 2
    shards = lax.axis_size("ctx")
    groups = lax.axis_size("fsdp")
    place = lax.axis_index("ctx")
    member = lax.axis_index("fsdp")
    wide = width // groups
    deep = hidden_width // groups
    x_first = list(range(shards.bit_length() - 1))
    z_first = x_first[1:2] + x_first[:1] + x_first[2:]

    tokens = inputs[0].astype(F32)
    mean = jnp.mean(tokens, axis=-1, keepdims=True)
    centred = tokens - mean
    inv_scale = lax.rsqrt(jnp.mean(centred * centred, axis=-1, keepdims=True) + EPS)
    normal = centred * inv_scale
    grad_low = cotangent[0]
    grad_full = grad_low.astype(F32)

    pairs = wide // LANES
    heads_in_pair = LANES // HD
    units = pairs * groups
    dup = max(1, shards // units)
    slot_groups = shards // (pairs * dup)
    per_group = groups // slot_groups
    heads = heads_in_pair // dup

    cos_full, sin_full = rotary(shards * rows)
    normed, grads, qkv_own, up_own, hidden, grad_up, qkv_in, grad_in = begin_layer(
        inputs[0],
        norm_gain,
        norm_shift,
        grad_low,
        qkv_weight,
        qkv_bias,
        up_weight,
        up_bias,
        out_weight,
        down_weight,
        cos_full,
        sin_full,
        shards,
        groups,
        pairs,
        slot_groups,
        per_group,
        dup,
    )

    def assembled(back):
        back = back.reshape(pairs, slot_groups, dup, 4, rows, LANES)
        back = jnp.sum(back, axis=2) if dup > 1 else back[:, :, 0]
        return back.transpose(2, 1, 3, 0, 4).reshape(4, slot_groups * rows, wide)

    hw = deep // shards
    if len(x_first) == 3 and dup == 1:
        back_in, down_sum, far_sum, up_sum = middle(
            qkv_in.reshape(per_group, shards, 3, 2, half, LANES),
            grad_in.reshape(shards, per_group, 2, half, LANES),
            hidden,
            normed,
            grads,
            grad_up,
            cos_full,
            sin_full,
            heads,
            groups,
        )
        (
            result,
            input_grad,
            qkv_weight_grad,
            up_weight_grad,
            out_weight_grad,
            down_weight_grad,
            sums,
            *_,
        ) = finish(
            back_in.reshape(per_group, shards, 4, rows, LANES),
            normed,
            grads,
            hidden,
            grad_up,
            qkv_own,
            up_own,
            out_weight,
            down_weight,
            down_sum,
            far_sum,
            up_sum,
            inputs[0],
            grad_low,
            norm_gain,
            out_bias,
            down_bias,
            groups,
            slot_groups,
        )
        return (
            result[None],
            input_grad[None],
            sums[0],
            sums[1],
            qkv_weight_grad,
            sums[2:5].reshape(-1),
            out_weight_grad,
            sums[9],
            up_weight_grad,
            sums[5 : 5 + groups].reshape(-1),
            down_weight_grad,
            sums[9],
        )
    else:
        down_grad = contract_rows(hidden, grads).astype(BF16)
        up_grad = contract_rows(normed, grad_up).astype(BF16)
        down_weight_grad = scatter_sum(
            down_grad.reshape(shards, hw, width), 0, place, x_first
        )
        up_part = scatter_sum(
            up_grad.reshape(groups, shards, wide // shards, deep), 1, place, z_first
        )

        backs = []
        for item in range(per_group):
            back = attend(
                qkv_in.reshape(per_group, shards, 3, 2, half, LANES),
                grad_in.reshape(shards, per_group, 2, half, LANES),
                item,
                cos_full,
                sin_full,
                heads,
                dup,
            )
            back = lax.all_to_all(back, "ctx", 0, 0)
            back = back.reshape(pairs, slot_groups, dup, 4, rows, LANES)
            back = jnp.sum(back, axis=2) if dup > 1 else back[:, :, 0]
            backs.append(back.transpose(2, 1, 3, 0, 4).reshape(4, slot_groups * rows, wide))
        back = jnp.concatenate(backs, axis=1)
        attended = back[0]
        grad_qkv = jnp.concatenate([back[1], back[2], back[3]], axis=1)

        share = matmul(hidden, down_weight) + matmul(attended, out_weight)
        result = tokens + scatter_rows(list(share.reshape(groups, rows, width))) + out_bias + down_bias

        grad_share = contract_cols(grad_up, up_own) + contract_cols(grad_qkv, qkv_own)
        grad_normed = scatter_rows(list(grad_share.reshape(groups, rows, width)))
        grad_full = grad_low.astype(F32)
        grad_normal = grad_normed * norm_gain
        grad_tokens = inv_scale * (
            grad_normal
            - jnp.mean(grad_normal, axis=-1, keepdims=True)
            - normal * jnp.mean(grad_normal * normal, axis=-1, keepdims=True)
        )
        input_grad = (grad_full + grad_tokens).astype(BF16)

        qkv_grad = contract_rows(normed, grad_qkv).astype(BF16)
        out_grad = contract_rows(attended, grads).astype(BF16)
        ow = wide // shards
        out_weight_grad = scatter_sum(out_grad.reshape(shards, ow, width), 0, place, z_first)
        qkv_part = scatter_sum(
            qkv_grad.reshape(groups, shards, ow, 3 * wide), 1, place, x_first
        )

        def relative(value):
            return [
                lax.dynamic_index_in_dim(value, member ^ j, 0, keepdims=False) for j in range(groups)
            ]

        def exchange(part):
            sent = relative(part.astype(BF16))
            got = [sent[0]] + [swap(sent[j], "fsdp", j) for j in range(1, groups)]
            return relative(jnp.stack(got))

        up_weight_grad = jnp.concatenate(exchange(up_part), axis=1).astype(F32)
        qkv_weight_grad = jnp.concatenate(
            [item.reshape(ow, 3, 1, wide) for item in exchange(qkv_part)], axis=2
        ).reshape(ow, 3 * width).astype(F32)

        qkv_bias_cols = jnp.sum(grad_qkv.astype(F32), axis=0).reshape(3, 1, wide)
        backs = []
        for item in range(per_group):
            back = attend(
                qkv_in.reshape(per_group, shards, 3, 2, half, LANES),
                grad_in.reshape(shards, per_group, 2, half, LANES),
                item,
                cos_full,
                sin_full,
                heads,
                dup,
            )
            back = lax.all_to_all(back, "ctx", 0, 0)
            backs.append(assembled(back))
    back = jnp.concatenate(backs, axis=1)
    attended = back[0]
    grad_qkv = jnp.concatenate([back[1], back[2], back[3]], axis=1)

    share = matmul(hidden, down_weight) + matmul(attended, out_weight)
    result = tokens + scatter_rows(list(share.reshape(groups, rows, width))) + out_bias + down_bias

    grad_share = contract_cols(grad_up, up_own) + contract_cols(grad_qkv, qkv_own)
    grad_normed = scatter_rows(list(grad_share.reshape(groups, rows, width)))
    grad_full = grad_low.astype(F32)
    grad_normal = grad_normed * norm_gain
    grad_tokens = inv_scale * (
        grad_normal
        - jnp.mean(grad_normal, axis=-1, keepdims=True)
        - normal * jnp.mean(grad_normal * normal, axis=-1, keepdims=True)
    )
    input_grad = (grad_full + grad_tokens).astype(BF16)

    qkv_grad = contract_rows(normed, grad_qkv).astype(BF16)
    out_grad = contract_rows(attended, grads).astype(BF16)
    ow = wide // shards
    out_weight_grad = scatter_sum(out_grad.reshape(shards, ow, width), 0, place, z_first)
    qkv_part = scatter_sum(
        qkv_grad.reshape(groups, shards, ow, 3 * wide), 1, place, x_first
    )

    def relative(value):
        return [
            lax.dynamic_index_in_dim(value, member ^ j, 0, keepdims=False) for j in range(groups)
        ]

    def exchange(part):
        sent = relative(part.astype(BF16))
        got = [sent[0]] + [swap(sent[j], "fsdp", j) for j in range(1, groups)]
        return relative(jnp.stack(got))

    up_weight_grad = jnp.concatenate(exchange(up_part), axis=1).astype(F32)
    qkv_weight_grad = jnp.concatenate(
        [item.reshape(ow, 3, 1, wide) for item in exchange(qkv_part)], axis=2
    ).reshape(ow, 3 * width).astype(F32)

    qkv_bias_cols = jnp.sum(grad_qkv.astype(F32), axis=0).reshape(3, 1, wide)
    up_bias_cols = jnp.sum(grad_up.astype(F32), axis=0).reshape(1, deep)
    qkv_bias_all = lax.dynamic_update_slice(
        jnp.zeros((3, groups, wide), F32), qkv_bias_cols, (0, member, 0)
    ).reshape(-1)
    up_bias_all = lax.dynamic_update_slice(
        jnp.zeros((groups, deep), F32), up_bias_cols, (member, 0)
    ).reshape(-1)
    early = total_sum(jnp.concatenate([jnp.sum(grad_full, axis=0), up_bias_all]))
    late = total_sum(
        jnp.concatenate(
            [jnp.sum(grad_normed * normal, axis=0), jnp.sum(grad_normed, axis=0), qkv_bias_all]
        )
    )
    out_bias_grad, up_bias_grad = early[:width], early[width:]
    gain_grad, shift_grad, qkv_bias_grad = late[:width], late[width : 2 * width], late[2 * width :]
    return (
        result.astype(BF16)[None],
        input_grad[None],
        gain_grad,
        shift_grad,
        qkv_weight_grad,
        qkv_bias_grad,
        out_weight_grad,
        out_bias_grad,
        up_weight_grad,
        up_bias_grad,
        down_weight_grad,
        out_bias_grad,
    )


def solution(mesh):
    in_specs = (
        P("fsdp", "ctx", None),
        P(),
        P(),
        P("fsdp", None),
        P(),
        P("fsdp", None),
        P(),
        P("fsdp", None),
        P(),
        P("fsdp", None),
        P(),
        P("fsdp", "ctx", None),
    )
    out_specs = (
        P("fsdp", "ctx", None),
        P("fsdp", "ctx", None),
        P(),
        P(),
        P(("fsdp", "ctx"), None),
        P(),
        P(("fsdp", "ctx"), None),
        P(),
        P(("fsdp", "ctx"), None),
        P(),
        P(("fsdp", "ctx"), None),
        P(),
    )
    return jax.shard_map(
        on_device, mesh=mesh, in_specs=in_specs, out_specs=out_specs, check_vma=False
    )
```

```python
from functools import partial

import jax
import jax.numpy as jnp
import numpy as np
from jax import lax
from jax.experimental import pallas as pl
from jax.experimental.pallas import tpu as pltpu
from jax.sharding import PartitionSpec as P

HD = 64
ROT = 32
LANES = 128

EPS = 1e-05
ROOT = 0.7978845608028654
CUBIC = 0.044715
F32 = jnp.float32
BF16 = jnp.bfloat16


def gelu_value(value):
    return 0.5 * value * (1.0 + jnp.tanh(ROOT * (value + CUBIC * value * value * value)))


def gelu_slope(value):
    tangent = jnp.tanh(ROOT * (value + CUBIC * value * value * value))
    return 0.5 * (1.0 + tangent) + 0.5 * value * (1.0 - tangent * tangent) * ROOT * (
        1.0 + 3.0 * CUBIC * value * value
    )


def contract_rows(left, right):
    return lax.dot_general(left, right, (((0,), (0,)), ((), ())), preferred_element_type=F32)


def contract_cols(left, right):
    return lax.dot_general(left, right, (((1,), (1,)), ((), ())), preferred_element_type=F32)


def matmul(left, right):
    return jnp.dot(left, right, preferred_element_type=F32)


def swap(value, axis, bit):
    size = lax.axis_size(axis)
    return lax.ppermute(value, axis, [(i, i ^ bit) for i in range(size)])


def after(value, *events):
    return lax.optimization_barrier((value,) + events)[0]


def rotary(length):
    quarter = ROT // 2
    inverse = np.float32(10000.0) ** (-np.arange(quarter, dtype=np.float32) * 2.0 / ROT)
    angle = np.arange(length, dtype=np.float32)[:, None] * inverse.astype(np.float32)[None, :]
    cosine, sine = np.cos(angle), np.sin(angle)
    one = np.concatenate([cosine, cosine, np.ones((length, HD - ROT))], axis=1)
    two = np.concatenate([-sine, sine, np.zeros((length, HD - ROT))], axis=1)
    copies = (1, LANES // HD)
    return (
        jnp.asarray(np.tile(one, copies), F32),
        jnp.asarray(np.tile(two, copies), F32),
    )


def turn(rows, cosine, sine):
    lane = lax.broadcasted_iota(jnp.int32, rows.shape, 1) % HD
    quarter = ROT // 2
    other = jnp.where(
        lane < quarter,
        pltpu.roll(rows, LANES - quarter, 1),
        pltpu.roll(rows, quarter, 1),
    )
    return rows * cosine + other * sine


def remote(src, dst, sends, recvs, at, target):
    return pltpu.make_async_remote_copy(
        src_ref=src,
        dst_ref=dst,
        send_sem=sends.at[at],
        recv_sem=recvs.at[at],
        device_id=target,
        device_id_type=pl.DeviceIdType.MESH,
    )


def start_kernel(
    shards,
    groups,
    pairs,
    slot_groups,
    items,
    dup,
    x_ref,
    gain_ref,
    shift_ref,
    cot_ref,
    qkv_ref,
    qkv_bias_ref,
    up_ref,
    up_bias_ref,
    out_ref,
    down_ref,
    cos_ref,
    sin_ref,
    normed_out,
    grads_out,
    wqkv_out,
    wup_out,
    hidden_out,
    du_out,
    qkv_in,
    do_in,
    normed,
    grads,
    wqkv,
    wup,
    down,
    outw,
    cosine,
    sine,
    stage,
    dstage,
    dh,
    hidden,
    du,
    local_sem,
    store_sem,
    qs,
    qr,
    us,
    ur,
    rs,
    rr,
    as_,
    ar,
    ds_,
    dr,
):
    place = lax.axis_index("ctx")
    member = lax.axis_index("fsdp")
    side = place % 2
    rows, width = x_ref.shape
    half = rows // 2
    wide = width // groups
    deep = up_ref.shape[1] // groups
    part = wide // 2

    barrier = pltpu.get_barrier_semaphore()
    for j in range(1, groups):
        pl.semaphore_signal(
            barrier, inc=1, device_id={"fsdp": member ^ j}, device_id_type=pl.DeviceIdType.MESH
        )
    for k in range(1, shards):
        pl.semaphore_signal(
            barrier, inc=1, device_id={"ctx": place ^ k}, device_id_type=pl.DeviceIdType.MESH
        )

    def local(src, dst, at):
        copy = pltpu.make_async_copy(src, dst, local_sem.at[at])
        copy.start()
        return copy

    def block(at, size):
        return pl.ds(pl.multiple_of(at, size), size)

    own_rows = block(member * wide, wide)
    loads = [
        local(
            qkv_ref.at[:, block(p * width + member * wide, wide)],
            wqkv.at[own_rows, pl.ds(p * wide, wide)],
            p,
        )
        for p in range(3)
    ]
    loads.append(local(up_ref.at[:, block(member * deep, deep)], wup.at[own_rows, :], 3))
    loads.append(local(cot_ref, grads.at[pl.ds(0, rows)], 4))
    loads.append(local(out_ref, outw, 5))
    loads.append(local(down_ref, down, 6))
    upper = 2 * shards - 1 - place
    for at, (table, held) in enumerate(((cos_ref, cosine), (sin_ref, sine))):
        loads.append(
            local(table.at[block(place * half, half)], held.at[pl.ds(0, half)], 7 + 2 * at)
        )
        loads.append(
            local(table.at[block(upper * half, half)], held.at[pl.ds(half, half)], 8 + 2 * at)
        )
    pl.semaphore_wait(barrier, groups - 1 + shards - 1)

    half_rows = block(member * wide + side * part, part)
    quarter = part // 2
    level = (place // 2) % 2
    own_quarter = (side * 2 + level) * quarter
    next_quarter = ((1 - side) * 2 + level) * quarter
    started = []

    def begin(copy):
        copy.start()
        started.append(copy)
        return copy

    q_far = {}
    for j in (2, 3):
        for p in range(3):
            q_far[j, p] = begin(
                remote(
                    qkv_ref.at[
                        block(own_quarter, quarter), block(p * width + (member ^ j) * wide, wide)
                    ],
                    wqkv.at[block(member * wide + own_quarter, quarter), pl.ds(p * wide, wide)],
                    qs,
                    qr,
                    (j - 2) * 3 + p,
                    {"fsdp": member ^ j},
                )
            )

    tokens = x_ref[...].astype(F32)
    centred = tokens - jnp.mean(tokens, axis=-1, keepdims=True)
    spread = lax.rsqrt(jnp.mean(centred * centred, axis=-1, keepdims=True) + EPS)
    normed[0:rows, :] = (centred * spread * gain_ref[...] + shift_ref[...]).astype(BF16)
    n_near = begin(
        remote(normed.at[pl.ds(0, rows)], normed.at[pl.ds(rows, rows)], rs, rr, 1, {"fsdp": member ^ 1})
    )
    q_near = [
        begin(
            remote(
                qkv_ref.at[:, block(p * width + (member ^ 1) * wide, wide)],
                wqkv.at[own_rows, pl.ds(p * wide, wide)],
                qs,
                qr,
                6 + p,
                {"fsdp": member ^ 1},
            )
        )
        for p in range(3)
    ]

    q_side = {}
    q_over = []
    for j in (2, 3):
        for p in range(3):
            at = (j - 2) * 3 + p
            q_far[j, p].wait_recv()
            spot = wqkv.at[
                block((member ^ j) * wide + own_quarter, quarter), pl.ds(p * wide, wide)
            ]
            q_side[j, p] = begin(remote(spot, spot, qs, qr, 9 + at, {"ctx": place ^ 1}))
            q_over.append(begin(remote(spot, spot, qs, qr, 15 + at, {"ctx": place ^ 2})))
    n_far = begin(
        remote(
            normed.at[pl.ds(0, rows)], normed.at[pl.ds(2 * rows, rows)], rs, rr, 0, {"fsdp": member ^ 2}
        )
    )
    for j in (2, 3):
        for p in range(3):
            q_side[j, p].wait_recv()
            spot = wqkv.at[
                block((member ^ j) * wide + next_quarter, quarter), pl.ds(p * wide, wide)
            ]
            q_over.append(
                begin(remote(spot, spot, qs, qr, 21 + (j - 2) * 3 + p, {"ctx": place ^ 2}))
            )

    for at in (0, 1, 2, 7, 8, 9, 10):
        loads[at].wait()
    for copy in q_near + q_over:
        copy.wait_recv()
    n_near.wait_recv()
    arrivals = []
    stores = []

    def keep(src, dst):
        copy = pltpu.make_async_copy(src, dst, store_sem.at[len(stores)])
        copy.start()
        stores.append(copy)

    def owner(target):
        return target // (slot_groups * dup), (target // dup) % slot_groups

    for item in range(items):
        if item == items - 1:
            n_far.wait_recv()
            n_last = begin(
                remote(
                    normed.at[pl.ds(2 * rows, rows)],
                    normed.at[pl.ds(3 * rows, rows)],
                    rs,
                    rr,
                    2,
                    {"fsdp": member ^ 1},
                )
            )
            loads[4].wait()
            g_far = begin(
                remote(
                    grads.at[pl.ds(0, rows)],
                    grads.at[pl.ds(2 * rows, rows)],
                    rs,
                    rr,
                    3,
                    {"fsdp": member ^ 2},
                )
            )
            g_near = begin(
                remote(
                    grads.at[pl.ds(0, rows)],
                    grads.at[pl.ds(rows, rows)],
                    rs,
                    rr,
                    4,
                    {"fsdp": member ^ 1},
                )
            )
            u_near = begin(
                remote(
                    up_ref.at[:, block((member ^ 1) * deep, deep)],
                    wup.at[own_rows, :],
                    us,
                    ur,
                    0,
                    {"fsdp": member ^ 1},
                )
            )
            n_last.wait_recv()

        def project(p, _, item=item):
            for g in range(slot_groups):
                slot = item * slot_groups + g
                acc = qkv_bias_ref[p * groups + member] + jnp.dot(
                    normed[slot * rows : (slot + 1) * rows, :],
                    wqkv[:, block(p * wide, wide)],
                    preferred_element_type=F32,
                )
                for h in range(pairs):
                    cols = acc[:, h * LANES : (h + 1) * LANES]
                    turned = turn(cols, cosine[...], sine[...])
                    stage[item, h, g, p] = jnp.where(p < 2, turned, cols).astype(BF16)
            return 0

        lax.fori_loop(0, 3, project, 0)
        for k in range(1, shards):
            pair, group = owner(place ^ k)
            arrivals.append(
                begin(
                    remote(
                        stage.at[item, pair, group],
                        qkv_in.at[item, place],
                        as_,
                        ar,
                        item * shards + k,
                        {"ctx": place ^ k},
                    )
                )
            )
        pair, group = owner(place)
        keep(stage.at[item, pair, group], qkv_in.at[item, place])

    g_far.wait_recv()
    g_last = begin(
        remote(
            grads.at[pl.ds(2 * rows, rows)],
            grads.at[pl.ds(3 * rows, rows)],
            rs,
            rr,
            5,
            {"fsdp": member ^ 1},
        )
    )
    tile = 512
    tiles = deep // tile
    u_far = {}
    for c in range(tiles):
        for j in (2, 3):
            u_far[c, j] = begin(
                remote(
                    up_ref.at[block(side * part, part), block((member ^ j) * deep + c * tile, tile)],
                    wup.at[half_rows, pl.ds(c * tile, tile)],
                    us,
                    ur,
                    1 + c * 2 + j - 2,
                    {"fsdp": member ^ j},
                )
            )
    g_near.wait_recv()
    loads[5].wait()
    g_last.wait_recv()
    for slot in range(groups):
        item, g = slot // slot_groups, slot % slot_groups
        att = contract_cols(grads[slot * rows : (slot + 1) * rows, :], outw[...]).astype(BF16)
        for h in range(pairs):
            dstage[h, g, item] = att[:, h * LANES : (h + 1) * LANES]
    for k in range(1, shards):
        pair, group = owner(place ^ k)
        arrivals.append(
            begin(
                remote(
                    dstage.at[pair, group],
                    do_in.at[place],
                    ds_,
                    dr,
                    k,
                    {"ctx": place ^ k},
                )
            )
        )
    pair, group = owner(place)
    keep(dstage.at[pair, group], do_in.at[place])
    keep(normed, normed_out)
    keep(grads, grads_out)
    keep(wqkv, wqkv_out)

    loads[6].wait()
    high = 2 * rows

    def back(at, _):
        r, c = block((at % 2) * high, high), block((at // 2) * tile, tile)
        dh[r, c] = contract_cols(grads[r, :], down[c, :])
        return 0

    def forward(c):
        cols = pl.ds(c * tile, tile)

        def one(at, _):
            r = block(at * high, high)
            value = matmul(normed[r, :], wup[:, cols]) + up_bias_ref[member, :, cols]
            hidden[r, cols] = gelu_value(value).astype(BF16)
            du[r, cols] = (dh[r, cols] * gelu_slope(value)).astype(BF16)
            return 0

        lax.fori_loop(0, 2, one, 0)

    lax.fori_loop(0, 2 * tiles, back, 0)
    loads[3].wait()
    u_near.wait_recv()
    u_side = []
    for c in range(tiles + 1):
        if c < tiles:
            for j in (2, 3):
                u_far[c, j].wait_recv()
                spot = wup.at[
                    block((member ^ j) * wide + side * part, part), pl.ds(c * tile, tile)
                ]
                u_side.append(
                    begin(
                        remote(spot, spot, us, ur, 1 + 2 * (tiles + c) + j - 2, {"ctx": place ^ 1})
                    )
                )
        if c > 0:
            u_side[2 * c - 2].wait_recv()
            u_side[2 * c - 1].wait_recv()
            forward(c - 1)
    keep(wup, wup_out)
    keep(hidden, hidden_out)
    keep(du, du_out)
    for copy in arrivals:
        copy.wait_recv()
    for copy in started:
        copy.wait_send()
    for copy in stores:
        copy.wait()


def begin_layer(
    x, gain, shift, cot, qkv_w, qkv_b, up_w, up_b, out_w, down_w, cosine, sine,
    shards, groups, pairs, slot_groups, items, dup,
):
    rows, width = x.shape
    wide = width // groups
    deep = up_w.shape[1] // groups
    total = rows * groups
    whole = pl.BlockSpec(memory_space=pltpu.VMEM)
    apart = pl.BlockSpec(memory_space=pl.ANY)
    dma = pltpu.SemaphoreType.DMA
    shape = jax.ShapeDtypeStruct
    stores = items + 1 + 6
    return pl.pallas_call(
        partial(start_kernel, shards, groups, pairs, slot_groups, items, dup),
        out_shape=[
            shape((total, width), BF16),
            shape((total, width), BF16),
            shape((width, 3 * wide), BF16),
            shape((width, deep), BF16),
            shape((total, deep), BF16),
            shape((total, deep), BF16),
            shape((items, shards, 3, rows, LANES), BF16),
            shape((shards, items, rows, LANES), BF16),
        ],
        in_specs=[whole, whole, whole, apart, apart, whole, apart, whole, apart, apart, apart, apart],
        out_specs=[apart] * 8,
        scratch_shapes=[
            pltpu.VMEM((total, width), BF16),
            pltpu.VMEM((total, width), BF16),
            pltpu.VMEM((width, 3 * wide), BF16),
            pltpu.VMEM((width, deep), BF16),
            pltpu.VMEM((deep, width), BF16),
            pltpu.VMEM((wide, width), BF16),
            pltpu.VMEM((rows, LANES), F32),
            pltpu.VMEM((rows, LANES), F32),
            pltpu.VMEM((items, pairs, slot_groups, 3, rows, LANES), BF16),
            pltpu.VMEM((pairs, slot_groups, items, rows, LANES), BF16),
            pltpu.VMEM((total, deep), F32),
            pltpu.VMEM((total, deep), BF16),
            pltpu.VMEM((total, deep), BF16),
            dma((11,)),
            dma((stores,)),
            dma((27,)),
            dma((27,)),
            dma((1 + 4 * (deep // 512),)),
            dma((1 + 4 * (deep // 512),)),
            dma((6,)),
            dma((6,)),
            dma((items * shards,)),
            dma((items * shards,)),
            dma((shards,)),
            dma((shards,)),
        ],
        compiler_params=pltpu.CompilerParams(
            collective_id=0, has_side_effects=True, vmem_limit_bytes=62 * 2**20
        ),
        cost_estimate=pl.CostEstimate(
            flops=2 * total * width * (3 * wide + wide + 2 * deep),
            bytes_accessed=60 * 2**20,
            transcendentals=total * deep,
        ),
    )(
        x,
        gain.reshape(1, width),
        shift.reshape(1, width),
        cot,
        qkv_w,
        qkv_b.reshape(3 * groups, 1, wide),
        up_w,
        up_b.reshape(groups, 1, deep),
        out_w,
        down_w,
        cosine,
        sine,
    )


def attend_kernel(
    shards, heads, dup, qkv_ref, do_ref, cos_ref, sin_ref, out_ref, s_buf, dp_buf, dk_buf, dv_buf
):
    half = qkv_ref.shape[-2]
    block = 2 * half
    count = shards
    base = lax.axis_index("ctx") % dup
    lane = lax.broadcasted_iota(jnp.int32, (block, LANES), 1) // HD
    own = [lane == (base + h) for h in range(heads)]
    scale = HD**-0.5

    def where_is(item):
        low = item < count // 2
        first = jnp.where(low, 2 * item, 2 * count - 1 - 2 * item)
        second = jnp.where(low, 2 * item + 1, 2 * count - 2 - 2 * item)
        return first, second, jnp.where(low, 0, 1)

    def load(part, item):
        first, second, side = where_is(item)
        return jnp.concatenate(
            [qkv_ref[0, first, part, side], qkv_ref[0, second, part, side]], axis=0
        )

    def load_do(item):
        first, second, side = where_is(item)
        return jnp.concatenate([do_ref[first, 0, side], do_ref[second, 0, side]], axis=0)

    def store(part, item, value):
        first, second, side = where_is(item)
        out_ref[first, 0, part, side] = value[:half].astype(out_ref.dtype)
        out_ref[second, 0, part, side] = value[half:].astype(out_ref.dtype)

    dk_buf[...] = jnp.zeros_like(dk_buf)
    dv_buf[...] = jnp.zeros_like(dv_buf)
    nothing = jnp.zeros((block, LANES), BF16)
    key_at = lax.broadcasted_iota(jnp.int32, (block, block), 0)
    query_at = lax.broadcasted_iota(jnp.int32, (block, block), 1)

    def per_query(item, _):
        query = load(0, item) * jnp.asarray(scale, BF16)
        grad = load_do(item)
        queries = [jnp.where(own[h], query, nothing) for h in range(heads)]
        grads = [jnp.where(own[h], grad, nothing) for h in range(heads)]

        def measure(key_item, state, diagonal):
            keys, values = load(1, key_item), load(2, key_item)
            new = []
            for h in range(heads):
                top, total, dot = state[h]
                s = contract_cols(keys, queries[h])
                if diagonal:
                    s = jnp.where(key_at <= query_at, s, -1e30)
                dp = contract_cols(values, grads[h])
                s_buf[h, key_item] = s
                dp_buf[h, key_item] = dp
                new_top = jnp.maximum(top, jnp.max(s, axis=0, keepdims=True))
                e = jnp.exp(s - new_top)
                fade = jnp.exp(top - new_top)
                new.append(
                    (
                        new_top,
                        total * fade + jnp.sum(e, axis=0, keepdims=True),
                        dot * fade + jnp.sum(e * dp, axis=0, keepdims=True),
                    )
                )
            return tuple(new)

        zero = jnp.zeros((1, block), F32)
        start = tuple((zero - 1e30, zero, zero) for _ in range(heads))
        state = lax.fori_loop(0, item, lambda k, st: measure(k, st, False), start)
        state = measure(item, state, True)
        logs = [top + jnp.log(total) for top, total, _ in state]
        deltas = [dot / total for _, total, dot in state]

        def apply(key_item, state):
            keys, values = load(1, key_item), load(2, key_item)
            out, dq = state
            dk, dv = dk_buf[key_item], dv_buf[key_item]
            for h in range(heads):
                p = jnp.exp(s_buf[h, key_item] - logs[h])
                ds = (p * (dp_buf[h, key_item] - deltas[h])).astype(BF16)
                p = p.astype(BF16)
                dv = dv + matmul(p, grads[h])
                dk = dk + matmul(ds, queries[h])
                out = out + jnp.where(own[h], contract_rows(p, values), 0.0)
                dq = dq + jnp.where(own[h], contract_rows(ds, keys), 0.0)
            dk_buf[key_item] = dk
            dv_buf[key_item] = dv
            return out, dq

        empty = jnp.zeros((block, LANES), F32)
        out, dq = lax.fori_loop(0, item + 1, apply, (empty, empty))
        store(0, item, out)
        rows = pl.ds(pl.multiple_of(item * block, block), block)
        store(1, item, turn(dq * scale, cos_ref[rows, :], -sin_ref[rows, :]))
        return 0

    lax.fori_loop(0, count, per_query, 0)

    def finish(item, _):
        rows = pl.ds(pl.multiple_of(item * block, block), block)
        store(2, item, turn(dk_buf[item], cos_ref[rows, :], -sin_ref[rows, :]))
        store(3, item, dv_buf[item])
        return 0

    lax.fori_loop(0, count, finish, 0)


def attend(qkv, grads, item, cosine, sine, heads, dup):
    shards, items = qkv.shape[1], 1
    half = qkv.shape[-2]
    tokens = shards * 2 * half
    block = 2 * half
    once = pl.Buffered(1)
    pairs = shards * (shards + 1) // 2 * items * heads
    return pl.pallas_call(
        partial(attend_kernel, shards, heads, dup),
        grid=(items,),
        out_shape=jax.ShapeDtypeStruct((shards, items, 4, 2, half, LANES), BF16),
        in_specs=[
            pl.BlockSpec(
                (1, shards, 3, 2, half, LANES), lambda i: (item, 0, 0, 0, 0, 0), pipeline_mode=once
            ),
            pl.BlockSpec(
                (shards, 1, 2, half, LANES), lambda i: (0, item, 0, 0, 0), pipeline_mode=once
            ),
            pl.BlockSpec((tokens, LANES), lambda i: (0, 0), pipeline_mode=once),
            pl.BlockSpec((tokens, LANES), lambda i: (0, 0), pipeline_mode=once),
        ],
        out_specs=pl.BlockSpec(
            (shards, 1, 4, 2, half, LANES), lambda i: (0, i, 0, 0, 0, 0), pipeline_mode=once
        ),
        scratch_shapes=[
            pltpu.VMEM((heads, shards, block, block), F32),
            pltpu.VMEM((heads, shards, block, block), F32),
            pltpu.VMEM((shards, block, LANES), F32),
            pltpu.VMEM((shards, block, LANES), F32),
        ],
        compiler_params=pltpu.CompilerParams(vmem_limit_bytes=58 * 2**20),
        cost_estimate=pl.CostEstimate(
            flops=pairs * 5 * 2 * block * block * 256,
            bytes_accessed=16 * 2**20,
            transcendentals=2 * pairs * block * block,
        ),
    )(qkv, grads, cosine, sine)


def middle_kernel(
    items,
    heads,
    qkv_in,
    do_in,
    hidden_in,
    normed_in,
    grads_in,
    du_in,
    cos_in,
    sin_in,
    back_in,
    down_out,
    far_out,
    up_out,
    d_send,
    d_keep,
    d_recv,
    d_last,
    u_send,
    u_keep,
    u_recv,
    u_last,
    out,
    local_sem,
    store_sem,
    own_sem,
    ds_,
    dr,
    us,
    ur,
    bs,
    br,
):
    place = lax.axis_index("ctx")
    shards = out.shape[1]
    x_at, z_at = place % 2, (place // 2) % 2
    top_at = place // 4
    near, over = {"ctx": place ^ 1}, {"ctx": place ^ 2}
    barrier = pltpu.get_barrier_semaphore()
    for k in range(1, shards):
        pl.semaphore_signal(
            barrier, inc=1, device_id={"ctx": place ^ k}, device_id_type=pl.DeviceIdType.MESH
        )

    def fetch(src, dst, at):
        copy = pltpu.make_async_copy(src, dst, local_sem.at[at])
        copy.start()
        return copy

    def block(at, size):
        return pl.ds(pl.multiple_of(at, size), size)

    members, tops, lanes, width = u_send.shape
    wide = lanes * 2 * tops
    units = d_send.shape[2]

    def down_one(top):
        spot = (1 - top_at) if top == 0 else top_at
        return remote(d_send.at[spot], d_recv.at[spot], ds_, dr, top, near)

    def down_two():
        return remote(d_send.at[1 - top_at, 0], d_last, ds_, dr, tops, over)

    def up_one(member):
        return remote(u_send.at[member], u_recv.at[member], us, ur, member, over)

    piece = lanes // 2

    def up_two(member):
        return remote(
            u_send.at[member, :, pl.ds(0, piece)], u_last.at[member], us, ur, members + member, near
        )

    def back_one(item, part, k):
        return remote(
            out.at[item, place ^ k, :, part],
            back_in.at[item, place, :, part],
            bs,
            br,
            (item * 2 + part) * shards + k,
            {"ctx": place ^ k},
        )

    def back_own(item, part):
        return pltpu.make_async_copy(
            out.at[item, place, :, part],
            back_in.at[item, place, :, part],
            own_sem.at[item * 2 + part],
        )

    def sums(hidden, normed, grads, du):
        loads = [
            fetch(src, dst, at)
            for at, (src, dst) in enumerate(
                ((hidden_in, hidden), (grads_in, grads), (normed_in, normed), (du_in, du))
            )
        ]
        loads[0].wait()
        loads[1].wait()
        pl.semaphore_wait(barrier, shards - 1)

        def down(which, into, top):
            def one(low, _):
                at = ((top * 2 + low) * 2 + which) * units
                into[top, low] = contract_rows(hidden[:, block(at, units)], grads[...]).astype(BF16)
                return 0

            lax.fori_loop(0, 2, one, 0)

        for top in range(tops):
            down(1 - x_at, d_send, (1 - top_at) if top == 0 else top_at)
            down_one(top).start()
        loads[2].wait()
        loads[3].wait()

        def up(which, into, member):
            def one(top, _):
                at = member * wide + (top * 2 + which) * lanes
                into[member, top] = contract_rows(normed[:, block(at, lanes)], du[...]).astype(BF16)
                return 0

            lax.fori_loop(0, tops, one, 0)

        for member in range(members):
            up(1 - z_at, u_send, member)
            up_one(member).start()
        for top in range(tops):
            down(x_at, d_keep, top)
        for member in range(members):
            up(z_at, u_keep, member)

    tokens = hidden_in.shape[0]
    pl.run_scoped(
        sums,
        pltpu.VMEM(hidden_in.shape, BF16),
        pltpu.VMEM((tokens, width), BF16),
        pltpu.VMEM((tokens, width), BF16),
        pltpu.VMEM(du_in.shape, BF16),
    )

    half = out.shape[-2]
    size = 2 * half

    def attention(qkv, do, cosine, sine, s_buf, dp_buf, dk_buf, dv_buf):
        loads = []
        for item in range(items):
            loads.append(fetch(qkv_in.at[item], qkv.at[item], 2 * item))
            loads.append(fetch(do_in.at[:, item], do.at[item], 2 * item + 1))
        loads.append(fetch(cos_in, cosine, 2 * items))
        loads.append(fetch(sin_in, sine, 2 * items + 1))
        for load in loads:
            load.wait()
        lane = lax.broadcasted_iota(jnp.int32, (size, LANES), 1) // HD
        own = [lane == h for h in range(heads)]
        key_at = lax.broadcasted_iota(jnp.int32, (size, size), 0)
        query_at = lax.broadcasted_iota(jnp.int32, (size, size), 1)
        nothing = jnp.zeros((size, LANES), BF16)
        scale = HD**-0.5

        for item in range(items):
            dk_buf[...] = jnp.zeros_like(dk_buf)
            dv_buf[...] = jnp.zeros_like(dv_buf)
            for part in (1, 0):

                def where_is(at, part=part):
                    if part:
                        return 2 * shards - 1 - 2 * at, 2 * shards - 2 - 2 * at
                    return 2 * at, 2 * at + 1

                def shard_of(at):
                    low = at < shards // 2
                    first = jnp.where(low, 2 * at, 2 * shards - 1 - 2 * at)
                    second = jnp.where(low, 2 * at + 1, 2 * shards - 2 - 2 * at)
                    return first, second, jnp.where(low, 0, 1)

                def load(which, at, item=item):
                    first, second, side = shard_of(at)
                    return jnp.concatenate(
                        [qkv[item, first, which, side], qkv[item, second, which, side]], axis=0
                    )

                def store(which, at, value, item=item, part=part, where_is=where_is):
                    first, second = where_is(at)
                    out[item, first, which, part] = value[:half].astype(BF16)
                    out[item, second, which, part] = value[half:].astype(BF16)

                def per_query(at, _, item=item, load=load, store=store, shard_of=shard_of):
                    query = load(0, at) * jnp.asarray(scale, BF16)
                    first, second, where = shard_of(at)
                    grad = jnp.concatenate([do[item, first, where], do[item, second, where]], axis=0)
                    queries = [jnp.where(own[h], query, nothing) for h in range(heads)]
                    grads = [jnp.where(own[h], grad, nothing) for h in range(heads)]

                    def measure(key, state, diagonal):
                        keys, values = load(1, key), load(2, key)
                        new = []
                        for h in range(heads):
                            top, total, dot = state[h]
                            s = contract_cols(keys, queries[h])
                            if diagonal:
                                s = jnp.where(key_at <= query_at, s, -1e30)
                            dp = contract_cols(values, grads[h])
                            s_buf[h, key] = s
                            dp_buf[h, key] = dp
                            new_top = jnp.maximum(top, jnp.max(s, axis=0, keepdims=True))
                            e = jnp.exp(s - new_top)
                            fade = jnp.exp(top - new_top)
                            new.append(
                                (
                                    new_top,
                                    total * fade + jnp.sum(e, axis=0, keepdims=True),
                                    dot * fade + jnp.sum(e * dp, axis=0, keepdims=True),
                                )
                            )
                        return tuple(new)

                    zero = jnp.zeros((1, size), F32)
                    start = tuple((zero - 1e30, zero, zero) for _ in range(heads))
                    state = lax.fori_loop(0, at, lambda k, st: measure(k, st, False), start)
                    state = measure(at, state, True)
                    logs = [top + jnp.log(total) for top, total, _ in state]
                    deltas = [dot / total for _, total, dot in state]

                    def apply(key, state):
                        keys, values = load(1, key), load(2, key)
                        attended, dq = state
                        dk, dv = dk_buf[key], dv_buf[key]
                        for h in range(heads):
                            p = jnp.exp(s_buf[h, key] - logs[h])
                            ds = (p * (dp_buf[h, key] - deltas[h])).astype(BF16)
                            p = p.astype(BF16)
                            dv = dv + matmul(p, grads[h])
                            dk = dk + matmul(ds, queries[h])
                            attended = attended + jnp.where(own[h], contract_rows(p, values), 0.0)
                            dq = dq + jnp.where(own[h], contract_rows(ds, keys), 0.0)
                        dk_buf[key] = dk
                        dv_buf[key] = dv
                        return attended, dq

                    empty = jnp.zeros((size, LANES), F32)
                    attended, dq = lax.fori_loop(0, at + 1, apply, (empty, empty))
                    store(0, at, attended)
                    rows = block(at * size, size)
                    store(1, at, turn(dq * scale, cosine[rows, :], -sine[rows, :]))
                    return 0

                low = part * (shards // 2)
                lax.fori_loop(low, low + shards // 2, per_query, 0)

                def finish(at, _, store=store):
                    rows = block(at * size, size)
                    store(2, at, turn(dk_buf[at], cosine[rows, :], -sine[rows, :]))
                    store(3, at, dv_buf[at])
                    return 0

                lax.fori_loop(low, low + shards // 2, finish, 0)
                for k in range(1, shards):
                    back_one(item, part, k).start()
                back_own(item, part).start()

    pl.run_scoped(
        attention,
        pltpu.VMEM((items,) + qkv_in.shape[1:], BF16),
        pltpu.VMEM((items, shards) + do_in.shape[2:], BF16),
        pltpu.VMEM(cos_in.shape, F32),
        pltpu.VMEM(sin_in.shape, F32),
        pltpu.VMEM((heads, shards, size, size), F32),
        pltpu.VMEM((heads, shards, size, size), F32),
        pltpu.VMEM((shards, size, LANES), F32),
        pltpu.VMEM((shards, size, LANES), F32),
    )

    stores = []

    def keep(src, dst):
        copy = pltpu.make_async_copy(src, dst, store_sem.at[len(stores)])
        copy.start()
        stores.append(copy)

    theirs = block((1 - x_at) * piece, piece)
    mine = block(x_at * piece, piece)
    down_one(0).wait()
    d_send[1 - top_at, 0] = (
        d_keep[1 - top_at, 1 - z_at].astype(F32) + d_recv[1 - top_at, 1 - z_at].astype(F32)
    ).astype(BF16)
    down_two().start()
    for member in range(members):
        up_one(member).wait()

        def pass_up(top, _, member=member):
            u_send[member, top, pl.ds(0, piece)] = (
                u_keep[member, top, theirs].astype(F32) + u_recv[member, top, theirs].astype(F32)
            ).astype(BF16)
            return 0

        lax.fori_loop(0, tops, pass_up, 0)
        up_two(member).start()
    down_one(1).wait()

    def add_down(low, _):
        d_keep[top_at, low] = (
            d_keep[top_at, low].astype(F32) + d_recv[top_at, low].astype(F32)
        ).astype(BF16)
        return 0

    lax.fori_loop(0, 2, add_down, 0)
    keep(d_keep.at[top_at], down_out)
    down_two().wait_recv()
    d_last[...] = (
        d_keep[1 - top_at, z_at].astype(F32)
        + d_recv[1 - top_at, z_at].astype(F32)
        + d_last[...].astype(F32)
    ).astype(BF16)
    keep(d_last, far_out)
    for member in range(members):
        up_two(member).wait_recv()

        def add_up(top, _, member=member):
            u_last[member, top] = (
                u_keep[member, top, mine].astype(F32)
                + u_recv[member, top, mine].astype(F32)
                + u_last[member, top].astype(F32)
            ).astype(BF16)
            return 0

        lax.fori_loop(0, tops, add_up, 0)
        keep(u_last.at[member], up_out.at[member])
    for item in range(items):
        for part in (1, 0):
            for k in range(1, shards):
                back_one(item, part, k).wait()
            back_own(item, part).wait()
    down_two().wait_send()
    for member in range(members):
        up_two(member).wait_send()
    for copy in stores:
        copy.wait()


def middle(qkv_in, do_in, hidden, normed, grads, du, cosine, sine, heads, groups):
    items, shards = qkv_in.shape[:2]
    half = qkv_in.shape[-2]
    width = normed.shape[1]
    deep = hidden.shape[1]
    units = deep // shards
    tops = shards // 4
    lanes = width // groups // tops // 2
    apart = pl.BlockSpec(memory_space=pl.ANY)
    dma = pltpu.SemaphoreType.DMA
    shape = jax.ShapeDtypeStruct
    pairs = shards * (shards + 1) // 2 * items * heads
    return pl.pallas_call(
        partial(middle_kernel, items, heads),
        out_shape=[
            shape((items, shards, 4, 2, half, LANES), BF16),
            shape((2, units, width), BF16),
            shape((units, width), BF16),
            shape((groups, tops, lanes // 2, deep), BF16),
        ],
        in_specs=[apart] * 8,
        out_specs=[apart] * 4,
        scratch_shapes=[
            pltpu.VMEM((tops, 2, units, width), BF16),
            pltpu.VMEM((tops, 2, units, width), BF16),
            pltpu.VMEM((tops, 2, units, width), BF16),
            pltpu.VMEM((units, width), BF16),
            pltpu.VMEM((groups, tops, lanes, deep), BF16),
            pltpu.VMEM((groups, tops, lanes, deep), BF16),
            pltpu.VMEM((groups, tops, lanes, deep), BF16),
            pltpu.VMEM((groups, tops, lanes // 2, deep), BF16),
            pltpu.VMEM((items, shards, 4, 2, half, LANES), BF16),
            dma((max(4, 2 * items + 2),)),
            dma((tops + groups,)),
            dma((2 * items,)),
            dma((tops + 1,)),
            dma((tops + 1,)),
            dma((2 * groups,)),
            dma((2 * groups,)),
            dma((2 * items * shards,)),
            dma((2 * items * shards,)),
        ],
        compiler_params=pltpu.CompilerParams(
            collective_id=1, has_side_effects=True, vmem_limit_bytes=63 * 2**20
        ),
        cost_estimate=pl.CostEstimate(
            flops=pairs * 10 * (2 * half) ** 2 * 256 + 8 * width * deep * hidden.shape[0],
            bytes_accessed=40 * 2**20,
            transcendentals=2 * pairs * (2 * half) ** 2,
        ),
    )(qkv_in, do_in, hidden, normed, grads, du, cosine, sine)


FLIGHTS = 64


def finish_kernel(
    items,
    pairs,
    slot_groups,
    back_in,
    normed_in,
    grads_in,
    hidden_in,
    du_in,
    wqkv_in,
    wup_in,
    outw_in,
    down_in,
    d_in,
    far_in,
    u_in,
    x_in,
    cot_in,
    gain_ref,
    out_bias_ref,
    down_bias_ref,
    result_out,
    input_out,
    qkv_out,
    up_out,
    o_out,
    d_out,
    sums_out,
    qkv_land,
    up_land,
    d_two,
    big,
    q_send,
    q_keep,
    q_recv,
    q_two,
    q_three,
    q_done,
    o_send,
    o_keep,
    o_recv,
    o_two,
    o_three,
    d_three,
    u_three,
    u_done,
    p_send,
    p_recv,
    p_own,
    n_send,
    n_recv,
    n_own,
    sums,
    s_recv,
    s_part,
    s_all,
    local_sem,
    store_sem,
    sends,
    recvs,
):
    place = lax.axis_index("ctx")
    member = lax.axis_index("fsdp")
    shards = back_in.shape[1]
    groups, tops, _, piece, qcols = q_send.shape
    rows, width = p_own.shape
    wide = width // groups
    deep = hidden_in.shape[1]
    x_at, z_at, top_at = place % 2, (place // 2) % 2, place // 4
    near, over, far = {"ctx": place ^ 1}, {"ctx": place ^ 2}, {"ctx": place ^ 4}

    barrier = pltpu.get_barrier_semaphore()
    for j in range(1, groups):
        pl.semaphore_signal(
            barrier, inc=1, device_id={"fsdp": member ^ j}, device_id_type=pl.DeviceIdType.MESH
        )
    for k in range(1, shards):
        pl.semaphore_signal(
            barrier, inc=1, device_id={"ctx": place ^ k}, device_id_type=pl.DeviceIdType.MESH
        )

    def block(at, size):
        return pl.ds(pl.multiple_of(at, size), size)

    names = {}

    def flight(name, src, dst, target):
        at = names.setdefault(name, len(names))
        return remote(src, dst, sends, recvs, at, target)

    def fetch(src, dst, at):
        copy = pltpu.make_async_copy(src, dst, local_sem.at[at])
        copy.start()
        return copy

    def core(j):
        return {"fsdp": member ^ j}

    theirs = block((1 - x_at) * piece, piece)
    mine = block(x_at * piece, piece)

    def d_second():
        return flight("d2", d_in.at[1 - z_at], d_two, over)

    def d_last():
        return flight("d", far_in, d_three, far)

    def u_last():
        return flight("u", u_in.at[:, 1 - top_at], u_three, far)

    def o_first(top):
        return flight(("o1", top), o_send.at[top], o_recv.at[top], over)

    def o_second():
        return flight("o2", o_send.at[:, pl.ds(0, piece)], o_two, near)

    def o_last():
        return flight("o3", o_send.at[0, pl.ds(piece, piece)], o_three, far)

    def q_first(f):
        return flight(("q1", f), q_send.at[f], q_recv.at[f], near)

    def q_second(f):
        return flight(("q2", f), q_send.at[f, :, 0], q_two.at[f], over)

    def q_last(f):
        return flight(("q3", f), q_send.at[f, 0, 1], q_three.at[f], far)

    def q_swap(j):
        return flight(("q4", j), q_done.at[member ^ j], qkv_land.at[member], core(j))

    def u_swap(j):
        return flight(("u4", j), u_done.at[member ^ j], up_land.at[member], core(j))

    def rows_last(name, send, recv):
        return flight((name, 3), send.at[0], recv.at[0], core(1))

    def rows_far(name, send, recv):
        return flight((name, 2), send.at[1], recv.at[1], core(2))

    def rows_near(name, send, recv):
        return flight((name, 1), send.at[2], recv.at[2], core(1))

    def sums_one(j):
        return flight(("s1", j), sums, s_recv.at[j - 1], core(j))

    span = width // shards

    def sums_two(k):
        return flight(
            ("s2", k), s_all.at[:, block((place ^ k) * span, span)], s_part.at[k], {"ctx": place ^ k}
        )

    def sums_three(k):
        mine = block(place * span, span)
        return flight(("s3", k), sums_out.at[:, mine], sums_out.at[:, mine], {"ctx": place ^ k})

    pl.semaphore_wait(barrier, groups - 1 + shards - 1)
    u_last().start()
    d_second().start()

    def phase_a(normed, grads):
        loads = [fetch(normed_in, normed, 0), fetch(grads_in, grads, 1)]
        for item in range(items):
            for owner in range(shards):
                pair, g = owner // slot_groups, owner % slot_groups
                spot = pl.ds((item * slot_groups + g) * rows, rows)
                for kind in range(4):
                    loads.append(
                        fetch(
                            back_in.at[item, owner, kind],
                            big.at[spot, pl.ds(kind * wide + pair * LANES, LANES)],
                            2 + (item * shards + owner) * 4 + kind,
                        )
                    )
        sums[...] = jnp.zeros_like(sums)
        for load in loads:
            load.wait()

        def out_grad(top, low, into):
            at = (top * 2 + low) * LANES
            into[top] = contract_rows(big[:, block(at, LANES)], grads[...]).astype(BF16)

        for top in range(tops):
            out_grad(top, 1 - z_at, o_send)
            o_first(top).start()

        for f in range(groups):

            def one(at, _, f=f):
                top, low = at // 2, at % 2
                value = contract_rows(
                    normed[:, block(f * wide + at * LANES, LANES)], big[:, wide:]
                )
                first, second = value[:piece], value[piece:]
                q_send[f, top, low] = jnp.where(x_at == 0, second, first).astype(BF16)
                q_keep[f, top, low] = jnp.where(x_at == 0, first, second).astype(BF16)
                return 0

            lax.fori_loop(0, 2 * tops, one, 0)
            q_first(f).start()
        for top in range(tops):
            out_grad(top, z_at, o_keep)
        for kind in range(3):
            cols = big[:, (kind + 1) * wide : (kind + 2) * wide].astype(F32)
            sums[2 + kind : 3 + kind, block(member * wide, wide)] = jnp.sum(
                cols, axis=0, keepdims=True
            )

    total = rows * groups
    pl.run_scoped(
        phase_a, pltpu.VMEM((total, width), BF16), pltpu.VMEM((total, width), BF16)
    )

    tile = 256

    def keep_share(pair, at, value, send, own):
        cols = block(at * tile, tile)
        if pair == 1:
            send[1, :, cols] = value[:rows].astype(BF16)
            send[0, :, cols] = value[rows:].astype(BF16)
        else:
            own[:, cols] = value[:rows]
            send[2, :, cols] = value[rows:].astype(BF16)

    def phase_b(hidden, down, outw):
        loads = [
            fetch(hidden_in, hidden, 0),
            fetch(down_in, down, 1),
            fetch(outw_in, outw, 2),
        ]
        for load in loads:
            load.wait()
        for pair in (1, 0):
            spot = pl.ds(pair * 2 * rows, 2 * rows)

            def one(at, _, pair=pair, spot=spot):
                cols = block(at * tile, tile)
                value = matmul(hidden[spot, :], down[:, cols]) + matmul(
                    big[spot, pl.ds(0, wide)], outw[:, cols]
                )
                keep_share(pair, at, value, p_send, p_own)
                return 0

            lax.fori_loop(0, width // tile, one, 0)
            if pair == 1:
                rows_last("p", p_send, p_recv).start()
            else:
                rows_near("p", p_send, p_recv).start()

    pl.run_scoped(
        phase_b,
        pltpu.VMEM(hidden_in.shape, BF16),
        pltpu.VMEM(down_in.shape, BF16),
        pltpu.VMEM(outw_in.shape, BF16),
    )

    def pass_rows(name, send, recv):
        rows_last(name, send, recv).wait_recv()
        send[1] = (send[1].astype(F32) + recv[0].astype(F32)).astype(BF16)
        rows_far(name, send, recv).start()

    pass_rows("p", p_send, p_recv)

    for top in range(tops):
        o_first(top).wait()
    for top in range(tops):
        o_send[top, pl.ds(0, piece)] = (
            o_keep[top, theirs].astype(F32) + o_recv[top, theirs].astype(F32)
        ).astype(BF16)
    o_second().start()

    def q_pass(f):
        q_first(f).wait()
        for top in range(tops):
            q_send[f, top, 0] = (
                q_keep[f, top, 1 - z_at].astype(F32) + q_recv[f, top, 1 - z_at].astype(F32)
            ).astype(BF16)
        q_second(f).start()

    def q_turn(f):
        q_second(f).wait_recv()
        other = 1 - top_at
        q_send[f, 0, 1] = (
            q_keep[f, other, z_at].astype(F32)
            + q_recv[f, other, z_at].astype(F32)
            + q_two[f, other].astype(F32)
        ).astype(BF16)
        q_last(f).start()

    for f in range(groups // 2):
        q_pass(f)
    d_last().start()

    def phase_c(du, wup, wqkv):
        loads = [
            fetch(du_in, du, 0),
            fetch(wup_in, wup, 1),
            fetch(wqkv_in, wqkv, 2),
        ]
        for load in loads:
            load.wait()
        for pair in (1, 0):
            spot = pl.ds(pair * 2 * rows, 2 * rows)

            def one(at, _, pair=pair, spot=spot):
                cols = block(at * tile, tile)
                value = contract_cols(du[spot, :], wup[cols, :]) + contract_cols(
                    big[spot, pl.ds(wide, 3 * wide)], wqkv[cols, :]
                )
                keep_share(pair, at, value, n_send, n_own)
                return 0

            lax.fori_loop(0, width // tile, one, 0)
            if pair == 1:
                rows_last("n", n_send, n_recv).start()
            else:
                rows_near("n", n_send, n_recv).start()
        step = deep // groups

        def column_sums(at, _):
            cols = block(at * step, step)
            value = jnp.sum(du[:, cols].astype(F32), axis=0, keepdims=True)
            for j in range(groups):
                sums[5 + j : 6 + j, cols] = jnp.where(member == j, value, 0.0)
            return 0

        lax.fori_loop(0, groups, column_sums, 0)

    pl.run_scoped(
        phase_c,
        pltpu.VMEM(du_in.shape, BF16),
        pltpu.VMEM(wup_in.shape, BF16),
        pltpu.VMEM(wqkv_in.shape, BF16),
    )
    pass_rows("n", n_send, n_recv)
    for f in range(groups // 2, groups):
        q_pass(f)
    for f in range(groups // 2):
        q_turn(f)
    o_second().wait_recv()
    o_send[0, pl.ds(piece, piece)] = (
        o_keep[1 - top_at, mine].astype(F32)
        + o_recv[1 - top_at, mine].astype(F32)
        + o_two[1 - top_at].astype(F32)
    ).astype(BF16)
    o_last().start()

    def phase_d(x, cot, out, d_own, d_more, d_sum, o_sum, u_more, q_full, u_full):
        loads = [
            fetch(x_in, x, 0),
            fetch(cot_in, cot, 1),
            fetch(u_in.at[:, top_at], u_done, 2),
            fetch(d_in.at[z_at], d_own, 3),
        ]
        for load in loads:
            load.wait()

        for f in range(groups // 2, groups):
            q_turn(f)
        rows_near("n", n_send, n_recv).wait_recv()
        rows_far("n", n_send, n_recv).wait_recv()
        step = 64

        def normal_part(at, _):
            r = block(at * step, step)
            tokens = x[r, :].astype(F32)
            centred = tokens - jnp.mean(tokens, axis=-1, keepdims=True)
            spread = lax.rsqrt(jnp.mean(centred * centred, axis=-1, keepdims=True) + EPS)
            normal = centred * spread
            dn = n_own[r, :] + n_recv[2, r, :].astype(F32) + n_recv[1, r, :].astype(F32)
            sums[0:1, :] = sums[0:1, :] + jnp.sum(dn * normal, axis=0, keepdims=True)
            sums[1:2, :] = sums[1:2, :] + jnp.sum(dn, axis=0, keepdims=True)
            dnorm = dn * gain_ref[...]
            grad = cot[r, :].astype(F32)
            sums[9:10, :] = sums[9:10, :] + jnp.sum(grad, axis=0, keepdims=True)
            change = spread * (
                dnorm
                - jnp.mean(dnorm, axis=-1, keepdims=True)
                - normal * jnp.mean(dnorm * normal, axis=-1, keepdims=True)
            )
            cot[r, :] = (grad + change).astype(BF16)
            return 0

        lax.fori_loop(0, rows // step, normal_part, 0)
        for j in range(1, groups):
            sums_one(j).start()
        own_input = pltpu.make_async_copy(cot, input_out, store_sem.at[1])
        own_input.start()

        rows_near("p", p_send, p_recv).wait_recv()
        rows_far("p", p_send, p_recv).wait_recv()

        def output_part(at, _):
            r = block(at * step, step)
            value = x[r, :].astype(F32) + p_own[r, :] + p_recv[2, r, :].astype(F32)
            value = value + p_recv[1, r, :].astype(F32) + out_bias_ref[...] + down_bias_ref[...]
            out[r, :] = value.astype(BF16)
            return 0

        lax.fori_loop(0, rows // step, output_part, 0)
        own_out = pltpu.make_async_copy(out, result_out, store_sem.at[2])
        own_out.start()

        u_last().wait_recv()
        for f in range(groups):
            u_done[f] = (
                u_done[f].astype(F32) + u_three[f].astype(F32)
            ).astype(BF16)
        for j in range(1, groups):
            u_swap(j).start()
        u_full[:, block(member * deep, deep)] = u_done[member].astype(F32)

        for j in range(1, groups):
            sums_one(j).wait_recv()
        s_all[...] = sums[...] + s_recv[0] + s_recv[1] + s_recv[2]
        for k in range(1, shards):
            sums_two(k).start()
        for f in range(groups):
            q_last(f).wait_recv()
            q_done[f] = (
                q_keep[f, top_at, z_at].astype(F32)
                + q_recv[f, top_at, z_at].astype(F32)
                + q_two[f, top_at].astype(F32)
                + q_three[f].astype(F32)
            ).astype(BF16)
        for j in range(1, groups):
            q_swap(j).start()
        for kind in range(3):
            q_full[:, block(kind * width + member * wide, wide)] = q_done[
                member, :, kind * wide : (kind + 1) * wide
            ].astype(F32)
        o_last().wait_recv()
        o_sum[...] = (
            o_keep[top_at, mine].astype(F32)
            + o_recv[top_at, mine].astype(F32)
            + o_two[top_at].astype(F32)
            + o_three[...].astype(F32)
        )
        own_o = pltpu.make_async_copy(o_sum, o_out, store_sem.at[5])
        own_o.start()
        for k in range(1, shards):
            sums_two(k).wait()
        cols = block(place * span, span)
        value = s_all[:, cols]
        for k in range(1, shards):
            value = value + s_part[k]
        sums_out[:, cols] = value
        for k in range(1, shards):
            sums_three(k).start()

        d_last().wait_recv()
        d_second().wait_recv()
        fetch(d_two, d_more, 4).wait()
        d_sum[...] = d_own[...].astype(F32) + d_more[...].astype(F32) + d_three[...].astype(F32)
        own_down = pltpu.make_async_copy(d_sum, d_out, store_sem.at[3])
        own_down.start()

        for j in range(1, groups):
            u_swap(j).wait_recv()
        for copy in (own_input, own_out):
            copy.wait()
        u_loads = [
            fetch(up_land.at[member ^ j], u_more.at[j], j) for j in range(1, groups)
        ]
        for j in range(1, groups):
            u_loads[j - 1].wait()
            u_full[:, block((member ^ j) * deep, deep)] = u_more[j].astype(F32)
        own_up = pltpu.make_async_copy(u_full, up_out, store_sem.at[0])
        own_up.start()
        for j in range(1, groups):
            q_swap(j).wait_recv()
        q_loads = [
            fetch(qkv_land.at[member ^ j], q_three.at[j], j) for j in range(1, groups)
        ]
        for j in range(1, groups):
            q_loads[j - 1].wait()
            for kind in range(3):
                q_full[:, block(kind * width + (member ^ j) * wide, wide)] = q_three[
                    j, :, kind * wide : (kind + 1) * wide
                ].astype(F32)
        own_q = pltpu.make_async_copy(q_full, qkv_out, store_sem.at[4])
        own_q.start()
        for copy in (own_up, own_down, own_q, own_o):
            copy.wait()

    pl.run_scoped(
        phase_d,
        pltpu.VMEM((rows, width), BF16),
        pltpu.VMEM((rows, width), BF16),
        pltpu.VMEM((rows, width), BF16),
        pltpu.VMEM(d_three.shape, BF16),
        pltpu.VMEM(d_three.shape, BF16),
        pltpu.VMEM(d_three.shape, F32),
        pltpu.VMEM((piece, width), F32),
        pltpu.VMEM(u_done.shape, BF16),
        pltpu.VMEM((piece, 3 * width), F32),
        pltpu.VMEM((piece, groups * deep), F32),
    )
    d_second().wait_send()
    u_last().wait_send()
    d_last().wait_send()
    o_second().wait_send()
    o_last().wait_send()
    for f in range(groups):
        q_second(f).wait_send()
        q_last(f).wait_send()
    for j in range(1, groups):
        q_swap(j).wait_send()
        u_swap(j).wait_send()
        sums_one(j).wait_send()
    for name, send, recv in (("p", p_send, p_recv), ("n", n_send, n_recv)):
        rows_last(name, send, recv).wait_send()
        rows_far(name, send, recv).wait_send()
        rows_near(name, send, recv).wait_send()
    for k in range(1, shards):
        sums_three(k).wait()


def finish(
    back_in, normed, grads, hidden, du, wqkv, wup, outw, down, d_sum, far_sum, u_sum,
    x, cot, gain, out_bias, down_bias, groups, slot_groups,
):
    items, shards = back_in.shape[:2]
    rows, width = x.shape
    wide = width // groups
    deep = hidden.shape[1]
    tops = shards // 4
    piece = wide // shards
    pairs = wide // LANES
    units = deep // shards
    apart = pl.BlockSpec(memory_space=pl.ANY)
    whole = pl.BlockSpec(memory_space=pltpu.VMEM)
    dma = pltpu.SemaphoreType.DMA
    shape = jax.ShapeDtypeStruct
    return pl.pallas_call(
        partial(finish_kernel, items, pairs, slot_groups),
        out_shape=[
            shape((rows, width), BF16),
            shape((rows, width), BF16),
            shape((piece, 3 * width), F32),
            shape((piece, groups * deep), F32),
            shape((piece, width), F32),
            shape((units, width), F32),
            shape((16, width), F32),
            shape((groups, piece, 3 * wide), BF16),
            shape((groups, piece, deep), BF16),
            shape((units, width), BF16),
        ],
        in_specs=[apart] * 14 + [whole] * 3,
        out_specs=[apart] * 6 + [whole] + [apart] * 3,
        scratch_shapes=[
            pltpu.VMEM((rows * groups, 4 * wide), BF16),
            pltpu.VMEM((groups, tops, 2, piece, 3 * wide), BF16),
            pltpu.VMEM((groups, tops, 2, piece, 3 * wide), BF16),
            pltpu.VMEM((groups, tops, 2, piece, 3 * wide), BF16),
            pltpu.VMEM((groups, tops, piece, 3 * wide), BF16),
            pltpu.VMEM((groups, piece, 3 * wide), BF16),
            pltpu.VMEM((groups, piece, 3 * wide), BF16),
            pltpu.VMEM((tops, 2 * piece, width), BF16),
            pltpu.VMEM((tops, 2 * piece, width), BF16),
            pltpu.VMEM((tops, 2 * piece, width), BF16),
            pltpu.VMEM((tops, piece, width), BF16),
            pltpu.VMEM((piece, width), BF16),
            pltpu.VMEM((units, width), BF16),
            pltpu.VMEM((groups, piece, deep), BF16),
            pltpu.VMEM((groups, piece, deep), BF16),
            pltpu.VMEM((3, rows, width), BF16),
            pltpu.VMEM((3, rows, width), BF16),
            pltpu.VMEM((rows, width), F32),
            pltpu.VMEM((3, rows, width), BF16),
            pltpu.VMEM((3, rows, width), BF16),
            pltpu.VMEM((rows, width), F32),
            pltpu.VMEM((16, width), F32),
            pltpu.VMEM((3, 16, width), F32),
            pltpu.VMEM((shards, 16, width // shards), F32),
            pltpu.VMEM((16, width), F32),
            dma((2 + items * shards * 4,)),
            dma((6,)),
            dma((FLIGHTS,)),
            dma((FLIGHTS,)),
        ],
        compiler_params=pltpu.CompilerParams(
            collective_id=2, has_side_effects=True, vmem_limit_bytes=63 * 2**20
        ),
        cost_estimate=pl.CostEstimate(
            flops=2 * rows * groups * width * (2 * deep + 8 * wide),
            bytes_accessed=60 * 2**20,
            transcendentals=0,
        ),
    )(
        back_in, normed, grads, hidden, du, wqkv, wup, outw, down, d_sum, far_sum, u_sum, x, cot,
        gain.reshape(1, width), out_bias.reshape(1, width), down_bias.reshape(1, width),
    )


def scatter_sum(parts, axis_at, place, bits):
    lead, tail = parts.shape[:axis_at], parts.shape[axis_at + 1 :]
    total = len(bits)
    left = list(range(total - 1, -1, -1))
    value = parts.reshape(lead + (2,) * total + tail)
    for bit in bits:
        at = axis_at + left.index(bit)
        left.remove(bit)
        mine = (place >> bit) & 1
        send = lax.dynamic_index_in_dim(value, 1 - mine, at, keepdims=False)
        keep = lax.dynamic_index_in_dim(value, mine, at, keepdims=False)
        got = swap(send.astype(BF16), "ctx", 1 << bit)
        value = keep.astype(F32) + got.astype(F32)
    return value


def scatter_rows(parts):
    last = swap(parts[3].astype(BF16), "fsdp", 1).astype(F32)
    far = swap((parts[2] + last).astype(BF16), "fsdp", 2).astype(F32)
    near = swap(parts[1].astype(BF16), "fsdp", 1).astype(F32)
    return parts[0] + near + far


def total_sum(value):
    for axis in ("fsdp", "ctx"):
        bit = 1
        while bit < lax.axis_size(axis):
            value = value + swap(value, axis, bit)
            bit *= 2
    return value


def on_device(
    inputs,
    norm_gain,
    norm_shift,
    qkv_weight,
    qkv_bias,
    out_weight,
    out_bias,
    up_weight,
    up_bias,
    down_weight,
    down_bias,
    cotangent,
):
    rows = inputs.shape[1]
    width = inputs.shape[2]
    hidden_width = up_weight.shape[1]
    half = rows // 2
    shards = lax.axis_size("ctx")
    groups = lax.axis_size("fsdp")
    place = lax.axis_index("ctx")
    member = lax.axis_index("fsdp")
    wide = width // groups
    deep = hidden_width // groups
    x_first = list(range(shards.bit_length() - 1))
    z_first = x_first[1:2] + x_first[:1] + x_first[2:]

    tokens = inputs[0].astype(F32)
    mean = jnp.mean(tokens, axis=-1, keepdims=True)
    centred = tokens - mean
    inv_scale = lax.rsqrt(jnp.mean(centred * centred, axis=-1, keepdims=True) + EPS)
    normal = centred * inv_scale
    grad_low = cotangent[0]
    grad_full = grad_low.astype(F32)

    pairs = wide // LANES
    heads_in_pair = LANES // HD
    units = pairs * groups
    dup = max(1, shards // units)
    slot_groups = shards // (pairs * dup)
    per_group = groups // slot_groups
    heads = heads_in_pair // dup

    cos_full, sin_full = rotary(shards * rows)
    normed, grads, qkv_own, up_own, hidden, grad_up, qkv_in, grad_in = begin_layer(
        inputs[0],
        norm_gain,
        norm_shift,
        grad_low,
        qkv_weight,
        qkv_bias,
        up_weight,
        up_bias,
        out_weight,
        down_weight,
        cos_full,
        sin_full,
        shards,
        groups,
        pairs,
        slot_groups,
        per_group,
        dup,
    )

    def assembled(back):
        back = back.reshape(pairs, slot_groups, dup, 4, rows, LANES)
        back = jnp.sum(back, axis=2) if dup > 1 else back[:, :, 0]
        return back.transpose(2, 1, 3, 0, 4).reshape(4, slot_groups * rows, wide)

    hw = deep // shards
    if len(x_first) == 3 and dup == 1:
        back_in, down_sum, far_sum, up_sum = middle(
            qkv_in.reshape(per_group, shards, 3, 2, half, LANES),
            grad_in.reshape(shards, per_group, 2, half, LANES),
            hidden,
            normed,
            grads,
            grad_up,
            cos_full,
            sin_full,
            heads,
            groups,
        )
        (
            result,
            input_grad,
            qkv_weight_grad,
            up_weight_grad,
            out_weight_grad,
            down_weight_grad,
            sums,
            *_,
        ) = finish(
            back_in.reshape(per_group, shards, 4, rows, LANES),
            normed,
            grads,
            hidden,
            grad_up,
            qkv_own,
            up_own,
            out_weight,
            down_weight,
            down_sum,
            far_sum,
            up_sum,
            inputs[0],
            grad_low,
            norm_gain,
            out_bias,
            down_bias,
            groups,
            slot_groups,
        )
        return (
            result[None],
            input_grad[None],
            sums[0],
            sums[1],
            qkv_weight_grad,
            sums[2:5].reshape(-1),
            out_weight_grad,
            sums[9],
            up_weight_grad,
            sums[5 : 5 + groups].reshape(-1),
            down_weight_grad,
            sums[9],
        )
    else:
        down_grad = contract_rows(hidden, grads).astype(BF16)
        up_grad = contract_rows(normed, grad_up).astype(BF16)
        down_weight_grad = scatter_sum(
            down_grad.reshape(shards, hw, width), 0, place, x_first
        )
        up_part = scatter_sum(
            up_grad.reshape(groups, shards, wide // shards, deep), 1, place, z_first
        )

        backs = []
        for item in range(per_group):
            back = attend(
                qkv_in.reshape(per_group, shards, 3, 2, half, LANES),
                grad_in.reshape(shards, per_group, 2, half, LANES),
                item,
                cos_full,
                sin_full,
                heads,
                dup,
            )
            back = lax.all_to_all(back, "ctx", 0, 0)
            back = back.reshape(pairs, slot_groups, dup, 4, rows, LANES)
            back = jnp.sum(back, axis=2) if dup > 1 else back[:, :, 0]
            backs.append(back.transpose(2, 1, 3, 0, 4).reshape(4, slot_groups * rows, wide))
        back = jnp.concatenate(backs, axis=1)
        attended = back[0]
        grad_qkv = jnp.concatenate([back[1], back[2], back[3]], axis=1)

        share = matmul(hidden, down_weight) + matmul(attended, out_weight)
        result = tokens + scatter_rows(list(share.reshape(groups, rows, width))) + out_bias + down_bias

        grad_share = contract_cols(grad_up, up_own) + contract_cols(grad_qkv, qkv_own)
        grad_normed = scatter_rows(list(grad_share.reshape(groups, rows, width)))
        grad_full = grad_low.astype(F32)
        grad_normal = grad_normed * norm_gain
        grad_tokens = inv_scale * (
            grad_normal
            - jnp.mean(grad_normal, axis=-1, keepdims=True)
            - normal * jnp.mean(grad_normal * normal, axis=-1, keepdims=True)
        )
        input_grad = (grad_full + grad_tokens).astype(BF16)

        qkv_grad = contract_rows(normed, grad_qkv).astype(BF16)
        out_grad = contract_rows(attended, grads).astype(BF16)
        ow = wide // shards
        out_weight_grad = scatter_sum(out_grad.reshape(shards, ow, width), 0, place, z_first)
        qkv_part = scatter_sum(
            qkv_grad.reshape(groups, shards, ow, 3 * wide), 1, place, x_first
        )

        def relative(value):
            return [
                lax.dynamic_index_in_dim(value, member ^ j, 0, keepdims=False) for j in range(groups)
            ]

        def exchange(part):
            sent = relative(part.astype(BF16))
            got = [sent[0]] + [swap(sent[j], "fsdp", j) for j in range(1, groups)]
            return relative(jnp.stack(got))

        up_weight_grad = jnp.concatenate(exchange(up_part), axis=1).astype(F32)
        qkv_weight_grad = jnp.concatenate(
            [item.reshape(ow, 3, 1, wide) for item in exchange(qkv_part)], axis=2
        ).reshape(ow, 3 * width).astype(F32)

        qkv_bias_cols = jnp.sum(grad_qkv.astype(F32), axis=0).reshape(3, 1, wide)
        backs = []
        for item in range(per_group):
            back = attend(
                qkv_in.reshape(per_group, shards, 3, 2, half, LANES),
                grad_in.reshape(shards, per_group, 2, half, LANES),
                item,
                cos_full,
                sin_full,
                heads,
                dup,
            )
            back = lax.all_to_all(back, "ctx", 0, 0)
            backs.append(assembled(back))
    back = jnp.concatenate(backs, axis=1)
    attended = back[0]
    grad_qkv = jnp.concatenate([back[1], back[2], back[3]], axis=1)

    share = matmul(hidden, down_weight) + matmul(attended, out_weight)
    result = tokens + scatter_rows(list(share.reshape(groups, rows, width))) + out_bias + down_bias

    grad_share = contract_cols(grad_up, up_own) + contract_cols(grad_qkv, qkv_own)
    grad_normed = scatter_rows(list(grad_share.reshape(groups, rows, width)))
    grad_full = grad_low.astype(F32)
    grad_normal = grad_normed * norm_gain
    grad_tokens = inv_scale * (
        grad_normal
        - jnp.mean(grad_normal, axis=-1, keepdims=True)
        - normal * jnp.mean(grad_normal * normal, axis=-1, keepdims=True)
    )
    input_grad = (grad_full + grad_tokens).astype(BF16)

    qkv_grad = contract_rows(normed, grad_qkv).astype(BF16)
    out_grad = contract_rows(attended, grads).astype(BF16)
    ow = wide // shards
    out_weight_grad = scatter_sum(out_grad.reshape(shards, ow, width), 0, place, z_first)
    qkv_part = scatter_sum(
        qkv_grad.reshape(groups, shards, ow, 3 * wide), 1, place, x_first
    )

    def relative(value):
        return [
            lax.dynamic_index_in_dim(value, member ^ j, 0, keepdims=False) for j in range(groups)
        ]

    def exchange(part):
        sent = relative(part.astype(BF16))
        got = [sent[0]] + [swap(sent[j], "fsdp", j) for j in range(1, groups)]
        return relative(jnp.stack(got))

    up_weight_grad = jnp.concatenate(exchange(up_part), axis=1).astype(F32)
    qkv_weight_grad = jnp.concatenate(
        [item.reshape(ow, 3, 1, wide) for item in exchange(qkv_part)], axis=2
    ).reshape(ow, 3 * width).astype(F32)

    qkv_bias_cols = jnp.sum(grad_qkv.astype(F32), axis=0).reshape(3, 1, wide)
    up_bias_cols = jnp.sum(grad_up.astype(F32), axis=0).reshape(1, deep)
    qkv_bias_all = lax.dynamic_update_slice(
        jnp.zeros((3, groups, wide), F32), qkv_bias_cols, (0, member, 0)
    ).reshape(-1)
    up_bias_all = lax.dynamic_update_slice(
        jnp.zeros((groups, deep), F32), up_bias_cols, (member, 0)
    ).reshape(-1)
    early = total_sum(jnp.concatenate([jnp.sum(grad_full, axis=0), up_bias_all]))
    late = total_sum(
        jnp.concatenate(
            [jnp.sum(grad_normed * normal, axis=0), jnp.sum(grad_normed, axis=0), qkv_bias_all]
        )
    )
    out_bias_grad, up_bias_grad = early[:width], early[width:]
    gain_grad, shift_grad, qkv_bias_grad = late[:width], late[width : 2 * width], late[2 * width :]
    return (
        result.astype(BF16)[None],
        input_grad[None],
        gain_grad,
        shift_grad,
        qkv_weight_grad,
        qkv_bias_grad,
        out_weight_grad,
        out_bias_grad,
        up_weight_grad,
        up_bias_grad,
        down_weight_grad,
        out_bias_grad,
    )


def solution(mesh):
    in_specs = (
        P("fsdp", "ctx", None),
        P(),
        P(),
        P("fsdp", None),
        P(),
        P("fsdp", None),
        P(),
        P("fsdp", None),
        P(),
        P("fsdp", None),
        P(),
        P("fsdp", "ctx", None),
    )
    out_specs = (
        P("fsdp", "ctx", None),
        P("fsdp", "ctx", None),
        P(),
        P(),
        P(("fsdp", "ctx"), None),
        P(),
        P(("fsdp", "ctx"), None),
        P(),
        P(("fsdp", "ctx"), None),
        P(),
        P(("fsdp", "ctx"), None),
        P(),
    )
    return jax.shard_map(
        on_device, mesh=mesh, in_specs=in_specs, out_specs=out_specs, check_vma=False
    )
```

```python
from functools import partial

import jax
import jax.numpy as jnp
import numpy as np
from jax import lax
from jax.experimental import pallas as pl
from jax.experimental.pallas import tpu as pltpu
from jax.sharding import PartitionSpec as P

HD = 64
ROT = 32
LANES = 128

EPS = 1e-05
ROOT = 0.7978845608028654
CUBIC = 0.044715
F32 = jnp.float32
BF16 = jnp.bfloat16


def gelu_value(value):
    return 0.5 * value * (1.0 + jnp.tanh(ROOT * (value + CUBIC * value * value * value)))


def gelu_slope(value):
    tangent = jnp.tanh(ROOT * (value + CUBIC * value * value * value))
    return 0.5 * (1.0 + tangent) + 0.5 * value * (1.0 - tangent * tangent) * ROOT * (
        1.0 + 3.0 * CUBIC * value * value
    )


def contract_rows(left, right):
    return lax.dot_general(left, right, (((0,), (0,)), ((), ())), preferred_element_type=F32)


def contract_cols(left, right):
    return lax.dot_general(left, right, (((1,), (1,)), ((), ())), preferred_element_type=F32)


def matmul(left, right):
    return jnp.dot(left, right, preferred_element_type=F32)


def swap(value, axis, bit):
    size = lax.axis_size(axis)
    return lax.ppermute(value, axis, [(i, i ^ bit) for i in range(size)])


def after(value, *events):
    return lax.optimization_barrier((value,) + events)[0]


def rotary(length):
    quarter = ROT // 2
    inverse = np.float32(10000.0) ** (-np.arange(quarter, dtype=np.float32) * 2.0 / ROT)
    angle = np.arange(length, dtype=np.float32)[:, None] * inverse.astype(np.float32)[None, :]
    cosine, sine = np.cos(angle), np.sin(angle)
    one = np.concatenate([cosine, cosine, np.ones((length, HD - ROT))], axis=1)
    two = np.concatenate([-sine, sine, np.zeros((length, HD - ROT))], axis=1)
    copies = (1, LANES // HD)
    return (
        jnp.asarray(np.tile(one, copies), F32),
        jnp.asarray(np.tile(two, copies), F32),
    )


def turn(rows, cosine, sine):
    lane = lax.broadcasted_iota(jnp.int32, rows.shape, 1) % HD
    quarter = ROT // 2
    other = jnp.where(
        lane < quarter,
        pltpu.roll(rows, LANES - quarter, 1),
        pltpu.roll(rows, quarter, 1),
    )
    return rows * cosine + other * sine


def remote(src, dst, sends, recvs, at, target):
    return pltpu.make_async_remote_copy(
        src_ref=src,
        dst_ref=dst,
        send_sem=sends.at[at],
        recv_sem=recvs.at[at],
        device_id=target,
        device_id_type=pl.DeviceIdType.MESH,
    )


def start_kernel(
    shards,
    groups,
    pairs,
    slot_groups,
    items,
    dup,
    x_ref,
    gain_ref,
    shift_ref,
    cot_ref,
    qkv_ref,
    qkv_bias_ref,
    up_ref,
    up_bias_ref,
    out_ref,
    down_ref,
    cos_ref,
    sin_ref,
    normed_out,
    grads_out,
    wqkv_out,
    wup_out,
    hidden_out,
    du_out,
    qkv_in,
    do_in,
    normed,
    grads,
    wqkv,
    wup,
    down,
    outw,
    cosine,
    sine,
    stage,
    dstage,
    dh,
    hidden,
    du,
    local_sem,
    store_sem,
    qs,
    qr,
    us,
    ur,
    rs,
    rr,
    as_,
    ar,
    ds_,
    dr,
):
    place = lax.axis_index("ctx")
    member = lax.axis_index("fsdp")
    side = place % 2
    rows, width = x_ref.shape
    half = rows // 2
    wide = width // groups
    deep = up_ref.shape[1] // groups
    part = wide // 2

    barrier = pltpu.get_barrier_semaphore()
    for j in range(1, groups):
        pl.semaphore_signal(
            barrier, inc=1, device_id={"fsdp": member ^ j}, device_id_type=pl.DeviceIdType.MESH
        )
    for k in range(1, shards):
        pl.semaphore_signal(
            barrier, inc=1, device_id={"ctx": place ^ k}, device_id_type=pl.DeviceIdType.MESH
        )

    def local(src, dst, at):
        copy = pltpu.make_async_copy(src, dst, local_sem.at[at])
        copy.start()
        return copy

    def block(at, size):
        return pl.ds(pl.multiple_of(at, size), size)

    own_rows = block(member * wide, wide)
    loads = [
        local(
            qkv_ref.at[:, block(p * width + member * wide, wide)],
            wqkv.at[own_rows, pl.ds(p * wide, wide)],
            p,
        )
        for p in range(3)
    ]
    loads.append(local(up_ref.at[:, block(member * deep, deep)], wup.at[own_rows, :], 3))
    loads.append(local(cot_ref, grads.at[pl.ds(0, rows)], 4))
    loads.append(local(out_ref, outw, 5))
    loads.append(local(down_ref, down, 6))
    upper = 2 * shards - 1 - place
    for at, (table, held) in enumerate(((cos_ref, cosine), (sin_ref, sine))):
        loads.append(
            local(table.at[block(place * half, half)], held.at[pl.ds(0, half)], 7 + 2 * at)
        )
        loads.append(
            local(table.at[block(upper * half, half)], held.at[pl.ds(half, half)], 8 + 2 * at)
        )
    pl.semaphore_wait(barrier, groups - 1 + shards - 1)

    half_rows = block(member * wide + side * part, part)
    quarter = part // 2
    level = (place // 2) % 2
    own_quarter = (side * 2 + level) * quarter
    next_quarter = ((1 - side) * 2 + level) * quarter
    started = []

    def begin(copy):
        copy.start()
        started.append(copy)
        return copy

    q_far = {}
    for j in (2, 3):
        for p in range(3):
            q_far[j, p] = begin(
                remote(
                    qkv_ref.at[
                        block(own_quarter, quarter), block(p * width + (member ^ j) * wide, wide)
                    ],
                    wqkv.at[block(member * wide + own_quarter, quarter), pl.ds(p * wide, wide)],
                    qs,
                    qr,
                    (j - 2) * 3 + p,
                    {"fsdp": member ^ j},
                )
            )

    tokens = x_ref[...].astype(F32)
    centred = tokens - jnp.mean(tokens, axis=-1, keepdims=True)
    spread = lax.rsqrt(jnp.mean(centred * centred, axis=-1, keepdims=True) + EPS)
    normed[0:rows, :] = (centred * spread * gain_ref[...] + shift_ref[...]).astype(BF16)
    n_near = begin(
        remote(normed.at[pl.ds(0, rows)], normed.at[pl.ds(rows, rows)], rs, rr, 1, {"fsdp": member ^ 1})
    )
    q_near = [
        begin(
            remote(
                qkv_ref.at[:, block(p * width + (member ^ 1) * wide, wide)],
                wqkv.at[own_rows, pl.ds(p * wide, wide)],
                qs,
                qr,
                6 + p,
                {"fsdp": member ^ 1},
            )
        )
        for p in range(3)
    ]

    q_side = {}
    q_over = []
    for j in (2, 3):
        for p in range(3):
            at = (j - 2) * 3 + p
            q_far[j, p].wait_recv()
            spot = wqkv.at[
                block((member ^ j) * wide + own_quarter, quarter), pl.ds(p * wide, wide)
            ]
            q_side[j, p] = begin(remote(spot, spot, qs, qr, 9 + at, {"ctx": place ^ 1}))
            q_over.append(begin(remote(spot, spot, qs, qr, 15 + at, {"ctx": place ^ 2})))
    n_far = begin(
        remote(
            normed.at[pl.ds(0, rows)], normed.at[pl.ds(2 * rows, rows)], rs, rr, 0, {"fsdp": member ^ 2}
        )
    )
    for j in (2, 3):
        for p in range(3):
            q_side[j, p].wait_recv()
            spot = wqkv.at[
                block((member ^ j) * wide + next_quarter, quarter), pl.ds(p * wide, wide)
            ]
            q_over.append(
                begin(remote(spot, spot, qs, qr, 21 + (j - 2) * 3 + p, {"ctx": place ^ 2}))
            )

    for at in (0, 1, 2, 7, 8, 9, 10):
        loads[at].wait()
    for copy in q_near + q_over:
        copy.wait_recv()
    n_near.wait_recv()
    arrivals = []
    stores = []

    def keep(src, dst):
        copy = pltpu.make_async_copy(src, dst, store_sem.at[len(stores)])
        copy.start()
        stores.append(copy)

    def owner(target):
        return target // (slot_groups * dup), (target // dup) % slot_groups

    for item in range(items):
        if item == items - 1:
            n_far.wait_recv()
            n_last = begin(
                remote(
                    normed.at[pl.ds(2 * rows, rows)],
                    normed.at[pl.ds(3 * rows, rows)],
                    rs,
                    rr,
                    2,
                    {"fsdp": member ^ 1},
                )
            )
            loads[4].wait()
            g_far = begin(
                remote(
                    grads.at[pl.ds(0, rows)],
                    grads.at[pl.ds(2 * rows, rows)],
                    rs,
                    rr,
                    3,
                    {"fsdp": member ^ 2},
                )
            )
            g_near = begin(
                remote(
                    grads.at[pl.ds(0, rows)],
                    grads.at[pl.ds(rows, rows)],
                    rs,
                    rr,
                    4,
                    {"fsdp": member ^ 1},
                )
            )
            u_near = begin(
                remote(
                    up_ref.at[:, block((member ^ 1) * deep, deep)],
                    wup.at[own_rows, :],
                    us,
                    ur,
                    0,
                    {"fsdp": member ^ 1},
                )
            )
            n_last.wait_recv()

        def project(p, _, item=item):
            for g in range(slot_groups):
                slot = item * slot_groups + g
                acc = qkv_bias_ref[p * groups + member] + jnp.dot(
                    normed[slot * rows : (slot + 1) * rows, :],
                    wqkv[:, block(p * wide, wide)],
                    preferred_element_type=F32,
                )
                for h in range(pairs):
                    cols = acc[:, h * LANES : (h + 1) * LANES]
                    turned = turn(cols, cosine[...], sine[...])
                    stage[item, h, g, p] = jnp.where(p < 2, turned, cols).astype(BF16)
            return 0

        lax.fori_loop(0, 3, project, 0)
        for k in range(1, shards):
            pair, group = owner(place ^ k)
            arrivals.append(
                begin(
                    remote(
                        stage.at[item, pair, group],
                        qkv_in.at[item, place],
                        as_,
                        ar,
                        item * shards + k,
                        {"ctx": place ^ k},
                    )
                )
            )
        pair, group = owner(place)
        keep(stage.at[item, pair, group], qkv_in.at[item, place])

    g_far.wait_recv()
    g_last = begin(
        remote(
            grads.at[pl.ds(2 * rows, rows)],
            grads.at[pl.ds(3 * rows, rows)],
            rs,
            rr,
            5,
            {"fsdp": member ^ 1},
        )
    )
    tile = 512
    tiles = deep // tile
    u_far = {}
    for c in range(tiles):
        for j in (2, 3):
            u_far[c, j] = begin(
                remote(
                    up_ref.at[block(side * part, part), block((member ^ j) * deep + c * tile, tile)],
                    wup.at[half_rows, pl.ds(c * tile, tile)],
                    us,
                    ur,
                    1 + c * 2 + j - 2,
                    {"fsdp": member ^ j},
                )
            )
    g_near.wait_recv()
    loads[5].wait()
    g_last.wait_recv()
    for slot in range(groups):
        item, g = slot // slot_groups, slot % slot_groups
        att = contract_cols(grads[slot * rows : (slot + 1) * rows, :], outw[...]).astype(BF16)
        for h in range(pairs):
            dstage[h, g, item] = att[:, h * LANES : (h + 1) * LANES]
    for k in range(1, shards):
        pair, group = owner(place ^ k)
        arrivals.append(
            begin(
                remote(
                    dstage.at[pair, group],
                    do_in.at[place],
                    ds_,
                    dr,
                    k,
                    {"ctx": place ^ k},
                )
            )
        )
    pair, group = owner(place)
    keep(dstage.at[pair, group], do_in.at[place])
    keep(normed, normed_out)
    keep(grads, grads_out)
    keep(wqkv, wqkv_out)

    loads[6].wait()
    high = 2 * rows

    def back(at, _):
        r, c = block((at % 2) * high, high), block((at // 2) * tile, tile)
        dh[r, c] = contract_cols(grads[r, :], down[c, :])
        return 0

    def forward(c):
        cols = pl.ds(c * tile, tile)

        def one(at, _):
            r = block(at * high, high)
            value = matmul(normed[r, :], wup[:, cols]) + up_bias_ref[member, :, cols]
            hidden[r, cols] = gelu_value(value).astype(BF16)
            du[r, cols] = (dh[r, cols] * gelu_slope(value)).astype(BF16)
            return 0

        lax.fori_loop(0, 2, one, 0)

    lax.fori_loop(0, 2 * tiles, back, 0)
    loads[3].wait()
    u_near.wait_recv()
    u_side = []
    for c in range(tiles + 1):
        if c < tiles:
            for j in (2, 3):
                u_far[c, j].wait_recv()
                spot = wup.at[
                    block((member ^ j) * wide + side * part, part), pl.ds(c * tile, tile)
                ]
                u_side.append(
                    begin(
                        remote(spot, spot, us, ur, 1 + 2 * (tiles + c) + j - 2, {"ctx": place ^ 1})
                    )
                )
        if c > 0:
            u_side[2 * c - 2].wait_recv()
            u_side[2 * c - 1].wait_recv()
            forward(c - 1)
    keep(wup, wup_out)
    keep(hidden, hidden_out)
    keep(du, du_out)
    for copy in arrivals:
        copy.wait_recv()
    for copy in started:
        copy.wait_send()
    for copy in stores:
        copy.wait()


def begin_layer(
    x, gain, shift, cot, qkv_w, qkv_b, up_w, up_b, out_w, down_w, cosine, sine,
    shards, groups, pairs, slot_groups, items, dup,
):
    rows, width = x.shape
    wide = width // groups
    deep = up_w.shape[1] // groups
    total = rows * groups
    whole = pl.BlockSpec(memory_space=pltpu.VMEM)
    apart = pl.BlockSpec(memory_space=pl.ANY)
    dma = pltpu.SemaphoreType.DMA
    shape = jax.ShapeDtypeStruct
    stores = items + 1 + 6
    return pl.pallas_call(
        partial(start_kernel, shards, groups, pairs, slot_groups, items, dup),
        out_shape=[
            shape((total, width), BF16),
            shape((total, width), BF16),
            shape((width, 3 * wide), BF16),
            shape((width, deep), BF16),
            shape((total, deep), BF16),
            shape((total, deep), BF16),
            shape((items, shards, 3, rows, LANES), BF16),
            shape((shards, items, rows, LANES), BF16),
        ],
        in_specs=[whole, whole, whole, apart, apart, whole, apart, whole, apart, apart, apart, apart],
        out_specs=[apart] * 8,
        scratch_shapes=[
            pltpu.VMEM((total, width), BF16),
            pltpu.VMEM((total, width), BF16),
            pltpu.VMEM((width, 3 * wide), BF16),
            pltpu.VMEM((width, deep), BF16),
            pltpu.VMEM((deep, width), BF16),
            pltpu.VMEM((wide, width), BF16),
            pltpu.VMEM((rows, LANES), F32),
            pltpu.VMEM((rows, LANES), F32),
            pltpu.VMEM((items, pairs, slot_groups, 3, rows, LANES), BF16),
            pltpu.VMEM((pairs, slot_groups, items, rows, LANES), BF16),
            pltpu.VMEM((total, deep), F32),
            pltpu.VMEM((total, deep), BF16),
            pltpu.VMEM((total, deep), BF16),
            dma((11,)),
            dma((stores,)),
            dma((27,)),
            dma((27,)),
            dma((1 + 4 * (deep // 512),)),
            dma((1 + 4 * (deep // 512),)),
            dma((6,)),
            dma((6,)),
            dma((items * shards,)),
            dma((items * shards,)),
            dma((shards,)),
            dma((shards,)),
        ],
        compiler_params=pltpu.CompilerParams(
            collective_id=0, has_side_effects=True, vmem_limit_bytes=62 * 2**20
        ),
        cost_estimate=pl.CostEstimate(
            flops=2 * total * width * (3 * wide + wide + 2 * deep),
            bytes_accessed=60 * 2**20,
            transcendentals=total * deep,
        ),
    )(
        x,
        gain.reshape(1, width),
        shift.reshape(1, width),
        cot,
        qkv_w,
        qkv_b.reshape(3 * groups, 1, wide),
        up_w,
        up_b.reshape(groups, 1, deep),
        out_w,
        down_w,
        cosine,
        sine,
    )


def attend_kernel(
    shards, heads, dup, qkv_ref, do_ref, cos_ref, sin_ref, out_ref, s_buf, dp_buf, dk_buf, dv_buf
):
    half = qkv_ref.shape[-2]
    block = 2 * half
    count = shards
    base = lax.axis_index("ctx") % dup
    lane = lax.broadcasted_iota(jnp.int32, (block, LANES), 1) // HD
    own = [lane == (base + h) for h in range(heads)]
    scale = HD**-0.5

    def where_is(item):
        low = item < count // 2
        first = jnp.where(low, 2 * item, 2 * count - 1 - 2 * item)
        second = jnp.where(low, 2 * item + 1, 2 * count - 2 - 2 * item)
        return first, second, jnp.where(low, 0, 1)

    def load(part, item):
        first, second, side = where_is(item)
        return jnp.concatenate(
            [qkv_ref[0, first, part, side], qkv_ref[0, second, part, side]], axis=0
        )

    def load_do(item):
        first, second, side = where_is(item)
        return jnp.concatenate([do_ref[first, 0, side], do_ref[second, 0, side]], axis=0)

    def store(part, item, value):
        first, second, side = where_is(item)
        out_ref[first, 0, part, side] = value[:half].astype(out_ref.dtype)
        out_ref[second, 0, part, side] = value[half:].astype(out_ref.dtype)

    dk_buf[...] = jnp.zeros_like(dk_buf)
    dv_buf[...] = jnp.zeros_like(dv_buf)
    nothing = jnp.zeros((block, LANES), BF16)
    key_at = lax.broadcasted_iota(jnp.int32, (block, block), 0)
    query_at = lax.broadcasted_iota(jnp.int32, (block, block), 1)

    def per_query(item, _):
        query = load(0, item) * jnp.asarray(scale, BF16)
        grad = load_do(item)
        queries = [jnp.where(own[h], query, nothing) for h in range(heads)]
        grads = [jnp.where(own[h], grad, nothing) for h in range(heads)]

        def measure(key_item, state, diagonal):
            keys, values = load(1, key_item), load(2, key_item)
            new = []
            for h in range(heads):
                top, total, dot = state[h]
                s = contract_cols(keys, queries[h])
                if diagonal:
                    s = jnp.where(key_at <= query_at, s, -1e30)
                dp = contract_cols(values, grads[h])
                s_buf[h, key_item] = s
                dp_buf[h, key_item] = dp
                new_top = jnp.maximum(top, jnp.max(s, axis=0, keepdims=True))
                e = jnp.exp(s - new_top)
                fade = jnp.exp(top - new_top)
                new.append(
                    (
                        new_top,
                        total * fade + jnp.sum(e, axis=0, keepdims=True),
                        dot * fade + jnp.sum(e * dp, axis=0, keepdims=True),
                    )
                )
            return tuple(new)

        zero = jnp.zeros((1, block), F32)
        start = tuple((zero - 1e30, zero, zero) for _ in range(heads))
        state = lax.fori_loop(0, item, lambda k, st: measure(k, st, False), start)
        state = measure(item, state, True)
        logs = [top + jnp.log(total) for top, total, _ in state]
        deltas = [dot / total for _, total, dot in state]

        def apply(key_item, state):
            keys, values = load(1, key_item), load(2, key_item)
            out, dq = state
            dk, dv = dk_buf[key_item], dv_buf[key_item]
            for h in range(heads):
                p = jnp.exp(s_buf[h, key_item] - logs[h])
                ds = (p * (dp_buf[h, key_item] - deltas[h])).astype(BF16)
                p = p.astype(BF16)
                dv = dv + matmul(p, grads[h])
                dk = dk + matmul(ds, queries[h])
                out = out + jnp.where(own[h], contract_rows(p, values), 0.0)
                dq = dq + jnp.where(own[h], contract_rows(ds, keys), 0.0)
            dk_buf[key_item] = dk
            dv_buf[key_item] = dv
            return out, dq

        empty = jnp.zeros((block, LANES), F32)
        out, dq = lax.fori_loop(0, item + 1, apply, (empty, empty))
        store(0, item, out)
        rows = pl.ds(pl.multiple_of(item * block, block), block)
        store(1, item, turn(dq * scale, cos_ref[rows, :], -sin_ref[rows, :]))
        return 0

    lax.fori_loop(0, count, per_query, 0)

    def finish(item, _):
        rows = pl.ds(pl.multiple_of(item * block, block), block)
        store(2, item, turn(dk_buf[item], cos_ref[rows, :], -sin_ref[rows, :]))
        store(3, item, dv_buf[item])
        return 0

    lax.fori_loop(0, count, finish, 0)


def attend(qkv, grads, item, cosine, sine, heads, dup):
    shards, items = qkv.shape[1], 1
    half = qkv.shape[-2]
    tokens = shards * 2 * half
    block = 2 * half
    once = pl.Buffered(1)
    pairs = shards * (shards + 1) // 2 * items * heads
    return pl.pallas_call(
        partial(attend_kernel, shards, heads, dup),
        grid=(items,),
        out_shape=jax.ShapeDtypeStruct((shards, items, 4, 2, half, LANES), BF16),
        in_specs=[
            pl.BlockSpec(
                (1, shards, 3, 2, half, LANES), lambda i: (item, 0, 0, 0, 0, 0), pipeline_mode=once
            ),
            pl.BlockSpec(
                (shards, 1, 2, half, LANES), lambda i: (0, item, 0, 0, 0), pipeline_mode=once
            ),
            pl.BlockSpec((tokens, LANES), lambda i: (0, 0), pipeline_mode=once),
            pl.BlockSpec((tokens, LANES), lambda i: (0, 0), pipeline_mode=once),
        ],
        out_specs=pl.BlockSpec(
            (shards, 1, 4, 2, half, LANES), lambda i: (0, i, 0, 0, 0, 0), pipeline_mode=once
        ),
        scratch_shapes=[
            pltpu.VMEM((heads, shards, block, block), F32),
            pltpu.VMEM((heads, shards, block, block), F32),
            pltpu.VMEM((shards, block, LANES), F32),
            pltpu.VMEM((shards, block, LANES), F32),
        ],
        compiler_params=pltpu.CompilerParams(vmem_limit_bytes=58 * 2**20),
        cost_estimate=pl.CostEstimate(
            flops=pairs * 5 * 2 * block * block * 256,
            bytes_accessed=16 * 2**20,
            transcendentals=2 * pairs * block * block,
        ),
    )(qkv, grads, cosine, sine)


def middle_kernel(
    items,
    heads,
    qkv_in,
    do_in,
    hidden_in,
    normed_in,
    grads_in,
    du_in,
    cos_in,
    sin_in,
    back_in,
    down_out,
    far_out,
    up_out,
    d_send,
    d_keep,
    d_recv,
    d_last,
    u_send,
    u_keep,
    u_recv,
    u_last,
    out,
    local_sem,
    store_sem,
    own_sem,
    ds_,
    dr,
    us,
    ur,
    bs,
    br,
):
    place = lax.axis_index("ctx")
    shards = out.shape[1]
    x_at, z_at = place % 2, (place // 2) % 2
    top_at = place // 4
    near, over = {"ctx": place ^ 1}, {"ctx": place ^ 2}
    barrier = pltpu.get_barrier_semaphore()
    for k in range(1, shards):
        pl.semaphore_signal(
            barrier, inc=1, device_id={"ctx": place ^ k}, device_id_type=pl.DeviceIdType.MESH
        )

    def fetch(src, dst, at):
        copy = pltpu.make_async_copy(src, dst, local_sem.at[at])
        copy.start()
        return copy

    def block(at, size):
        return pl.ds(pl.multiple_of(at, size), size)

    members, tops, lanes, width = u_send.shape
    wide = lanes * 2 * tops
    units = d_send.shape[2]

    def down_one(top):
        spot = (1 - top_at) if top == 0 else top_at
        return remote(d_send.at[spot], d_recv.at[spot], ds_, dr, top, near)

    def down_two():
        return remote(d_send.at[1 - top_at, 0], d_last, ds_, dr, tops, over)

    def up_one(member):
        return remote(u_send.at[member], u_recv.at[member], us, ur, member, over)

    piece = lanes // 2

    def up_two(member):
        return remote(
            u_send.at[member, :, pl.ds(0, piece)], u_last.at[member], us, ur, members + member, near
        )

    def back_one(item, part, k):
        return remote(
            out.at[item, place ^ k, :, part],
            back_in.at[item, place, :, part],
            bs,
            br,
            (item * 2 + part) * shards + k,
            {"ctx": place ^ k},
        )

    def back_own(item, part):
        return pltpu.make_async_copy(
            out.at[item, place, :, part],
            back_in.at[item, place, :, part],
            own_sem.at[item * 2 + part],
        )

    def sums(hidden, normed, grads, du):
        loads = [
            fetch(src, dst, at)
            for at, (src, dst) in enumerate(
                ((hidden_in, hidden), (grads_in, grads), (normed_in, normed), (du_in, du))
            )
        ]
        loads[0].wait()
        loads[1].wait()
        pl.semaphore_wait(barrier, shards - 1)

        def down(which, into, top):
            def one(low, _):
                at = ((top * 2 + low) * 2 + which) * units
                into[top, low] = contract_rows(hidden[:, block(at, units)], grads[...]).astype(BF16)
                return 0

            lax.fori_loop(0, 2, one, 0)

        for top in range(tops):
            down(1 - x_at, d_send, (1 - top_at) if top == 0 else top_at)
            down_one(top).start()
        loads[2].wait()
        loads[3].wait()

        def up(which, into, member):
            def one(top, _):
                at = member * wide + (top * 2 + which) * lanes
                into[member, top] = contract_rows(normed[:, block(at, lanes)], du[...]).astype(BF16)
                return 0

            lax.fori_loop(0, tops, one, 0)

        for member in range(members):
            up(1 - z_at, u_send, member)
            up_one(member).start()
        for top in range(tops):
            down(x_at, d_keep, top)
        for member in range(members):
            up(z_at, u_keep, member)

    tokens = hidden_in.shape[0]
    pl.run_scoped(
        sums,
        pltpu.VMEM(hidden_in.shape, BF16),
        pltpu.VMEM((tokens, width), BF16),
        pltpu.VMEM((tokens, width), BF16),
        pltpu.VMEM(du_in.shape, BF16),
    )

    half = out.shape[-2]
    size = 2 * half

    def attention(qkv, do, cosine, sine, s_buf, dp_buf, dk_buf, dv_buf):
        loads = []
        for item in range(items):
            loads.append(fetch(qkv_in.at[item], qkv.at[item], 2 * item))
            loads.append(fetch(do_in.at[:, item], do.at[item], 2 * item + 1))
        loads.append(fetch(cos_in, cosine, 2 * items))
        loads.append(fetch(sin_in, sine, 2 * items + 1))
        for load in loads:
            load.wait()
        lane = lax.broadcasted_iota(jnp.int32, (size, LANES), 1) // HD
        own = [lane == h for h in range(heads)]
        key_at = lax.broadcasted_iota(jnp.int32, (size, size), 0)
        query_at = lax.broadcasted_iota(jnp.int32, (size, size), 1)
        nothing = jnp.zeros((size, LANES), BF16)
        scale = HD**-0.5

        for item in range(items):
            dk_buf[...] = jnp.zeros_like(dk_buf)
            dv_buf[...] = jnp.zeros_like(dv_buf)
            for part in (1, 0):

                def where_is(at, part=part):
                    if part:
                        return 2 * shards - 1 - 2 * at, 2 * shards - 2 - 2 * at
                    return 2 * at, 2 * at + 1

                def shard_of(at):
                    low = at < shards // 2
                    first = jnp.where(low, 2 * at, 2 * shards - 1 - 2 * at)
                    second = jnp.where(low, 2 * at + 1, 2 * shards - 2 - 2 * at)
                    return first, second, jnp.where(low, 0, 1)

                def load(which, at, item=item):
                    first, second, side = shard_of(at)
                    return jnp.concatenate(
                        [qkv[item, first, which, side], qkv[item, second, which, side]], axis=0
                    )

                def store(which, at, value, item=item, part=part, where_is=where_is):
                    first, second = where_is(at)
                    out[item, first, which, part] = value[:half].astype(BF16)
                    out[item, second, which, part] = value[half:].astype(BF16)

                def per_query(at, _, item=item, load=load, store=store, shard_of=shard_of):
                    query = load(0, at) * jnp.asarray(scale, BF16)
                    first, second, where = shard_of(at)
                    grad = jnp.concatenate([do[item, first, where], do[item, second, where]], axis=0)
                    queries = [jnp.where(own[h], query, nothing) for h in range(heads)]
                    grads = [jnp.where(own[h], grad, nothing) for h in range(heads)]

                    def measure(key, state, diagonal):
                        keys, values = load(1, key), load(2, key)
                        new = []
                        for h in range(heads):
                            top, total, dot = state[h]
                            s = contract_cols(keys, queries[h])
                            if diagonal:
                                s = jnp.where(key_at <= query_at, s, -1e30)
                            dp = contract_cols(values, grads[h])
                            s_buf[h, key] = s
                            dp_buf[h, key] = dp
                            new_top = jnp.maximum(top, jnp.max(s, axis=0, keepdims=True))
                            e = jnp.exp(s - new_top)
                            fade = jnp.exp(top - new_top)
                            new.append(
                                (
                                    new_top,
                                    total * fade + jnp.sum(e, axis=0, keepdims=True),
                                    dot * fade + jnp.sum(e * dp, axis=0, keepdims=True),
                                )
                            )
                        return tuple(new)

                    zero = jnp.zeros((1, size), F32)
                    start = tuple((zero - 1e30, zero, zero) for _ in range(heads))
                    state = lax.fori_loop(0, at, lambda k, st: measure(k, st, False), start)
                    state = measure(at, state, True)
                    logs = [top + jnp.log(total) for top, total, _ in state]
                    deltas = [dot / total for _, total, dot in state]

                    def apply(key, state):
                        keys, values = load(1, key), load(2, key)
                        attended, dq = state
                        dk, dv = dk_buf[key], dv_buf[key]
                        for h in range(heads):
                            p = jnp.exp(s_buf[h, key] - logs[h])
                            ds = (p * (dp_buf[h, key] - deltas[h])).astype(BF16)
                            p = p.astype(BF16)
                            dv = dv + matmul(p, grads[h])
                            dk = dk + matmul(ds, queries[h])
                            attended = attended + jnp.where(own[h], contract_rows(p, values), 0.0)
                            dq = dq + jnp.where(own[h], contract_rows(ds, keys), 0.0)
                        dk_buf[key] = dk
                        dv_buf[key] = dv
                        return attended, dq

                    empty = jnp.zeros((size, LANES), F32)
                    attended, dq = lax.fori_loop(0, at + 1, apply, (empty, empty))
                    store(0, at, attended)
                    rows = block(at * size, size)
                    store(1, at, turn(dq * scale, cosine[rows, :], -sine[rows, :]))
                    return 0

                low = part * (shards // 2)
                lax.fori_loop(low, low + shards // 2, per_query, 0)

                def finish(at, _, store=store):
                    rows = block(at * size, size)
                    store(2, at, turn(dk_buf[at], cosine[rows, :], -sine[rows, :]))
                    store(3, at, dv_buf[at])
                    return 0

                lax.fori_loop(low, low + shards // 2, finish, 0)
                for k in range(1, shards):
                    back_one(item, part, k).start()
                back_own(item, part).start()

    pl.run_scoped(
        attention,
        pltpu.VMEM((items,) + qkv_in.shape[1:], BF16),
        pltpu.VMEM((items, shards) + do_in.shape[2:], BF16),
        pltpu.VMEM(cos_in.shape, F32),
        pltpu.VMEM(sin_in.shape, F32),
        pltpu.VMEM((heads, shards, size, size), F32),
        pltpu.VMEM((heads, shards, size, size), F32),
        pltpu.VMEM((shards, size, LANES), F32),
        pltpu.VMEM((shards, size, LANES), F32),
    )

    stores = []

    def keep(src, dst):
        copy = pltpu.make_async_copy(src, dst, store_sem.at[len(stores)])
        copy.start()
        stores.append(copy)

    theirs = block((1 - x_at) * piece, piece)
    mine = block(x_at * piece, piece)
    down_one(0).wait()
    d_send[1 - top_at, 0] = (
        d_keep[1 - top_at, 1 - z_at].astype(F32) + d_recv[1 - top_at, 1 - z_at].astype(F32)
    ).astype(BF16)
    down_two().start()
    for member in range(members):
        up_one(member).wait()

        def pass_up(top, _, member=member):
            u_send[member, top, pl.ds(0, piece)] = (
                u_keep[member, top, theirs].astype(F32) + u_recv[member, top, theirs].astype(F32)
            ).astype(BF16)
            return 0

        lax.fori_loop(0, tops, pass_up, 0)
        up_two(member).start()
    down_one(1).wait()

    def add_down(low, _):
        d_keep[top_at, low] = (
            d_keep[top_at, low].astype(F32) + d_recv[top_at, low].astype(F32)
        ).astype(BF16)
        return 0

    lax.fori_loop(0, 2, add_down, 0)
    keep(d_keep.at[top_at], down_out)
    down_two().wait_recv()
    d_last[...] = (
        d_keep[1 - top_at, z_at].astype(F32)
        + d_recv[1 - top_at, z_at].astype(F32)
        + d_last[...].astype(F32)
    ).astype(BF16)
    keep(d_last, far_out)
    for member in range(members):
        up_two(member).wait_recv()

        def add_up(top, _, member=member):
            u_last[member, top] = (
                u_keep[member, top, mine].astype(F32)
                + u_recv[member, top, mine].astype(F32)
                + u_last[member, top].astype(F32)
            ).astype(BF16)
            return 0

        lax.fori_loop(0, tops, add_up, 0)
        keep(u_last.at[member], up_out.at[member])
    for item in range(items):
        for part in (1, 0):
            for k in range(1, shards):
                back_one(item, part, k).wait()
            back_own(item, part).wait()
    down_two().wait_send()
    for member in range(members):
        up_two(member).wait_send()
    for copy in stores:
        copy.wait()


def middle(qkv_in, do_in, hidden, normed, grads, du, cosine, sine, heads, groups):
    items, shards = qkv_in.shape[:2]
    half = qkv_in.shape[-2]
    width = normed.shape[1]
    deep = hidden.shape[1]
    units = deep // shards
    tops = shards // 4
    lanes = width // groups // tops // 2
    apart = pl.BlockSpec(memory_space=pl.ANY)
    dma = pltpu.SemaphoreType.DMA
    shape = jax.ShapeDtypeStruct
    pairs = shards * (shards + 1) // 2 * items * heads
    return pl.pallas_call(
        partial(middle_kernel, items, heads),
        out_shape=[
            shape((items, shards, 4, 2, half, LANES), BF16),
            shape((2, units, width), BF16),
            shape((units, width), BF16),
            shape((groups, tops, lanes // 2, deep), BF16),
        ],
        in_specs=[apart] * 8,
        out_specs=[apart] * 4,
        scratch_shapes=[
            pltpu.VMEM((tops, 2, units, width), BF16),
            pltpu.VMEM((tops, 2, units, width), BF16),
            pltpu.VMEM((tops, 2, units, width), BF16),
            pltpu.VMEM((units, width), BF16),
            pltpu.VMEM((groups, tops, lanes, deep), BF16),
            pltpu.VMEM((groups, tops, lanes, deep), BF16),
            pltpu.VMEM((groups, tops, lanes, deep), BF16),
            pltpu.VMEM((groups, tops, lanes // 2, deep), BF16),
            pltpu.VMEM((items, shards, 4, 2, half, LANES), BF16),
            dma((max(4, 2 * items + 2),)),
            dma((tops + groups,)),
            dma((2 * items,)),
            dma((tops + 1,)),
            dma((tops + 1,)),
            dma((2 * groups,)),
            dma((2 * groups,)),
            dma((2 * items * shards,)),
            dma((2 * items * shards,)),
        ],
        compiler_params=pltpu.CompilerParams(
            collective_id=1, has_side_effects=True, vmem_limit_bytes=63 * 2**20
        ),
        cost_estimate=pl.CostEstimate(
            flops=pairs * 10 * (2 * half) ** 2 * 256 + 8 * width * deep * hidden.shape[0],
            bytes_accessed=40 * 2**20,
            transcendentals=2 * pairs * (2 * half) ** 2,
        ),
    )(qkv_in, do_in, hidden, normed, grads, du, cosine, sine)


FLIGHTS = 64


def finish_kernel(
    items,
    pairs,
    slot_groups,
    back_in,
    normed_in,
    grads_in,
    hidden_in,
    du_in,
    wqkv_in,
    wup_in,
    outw_in,
    down_in,
    d_in,
    far_in,
    u_in,
    x_in,
    cot_in,
    gain_ref,
    out_bias_ref,
    down_bias_ref,
    result_out,
    input_out,
    qkv_out,
    up_out,
    o_out,
    d_out,
    sums_out,
    qkv_land,
    up_land,
    d_two,
    big,
    q_send,
    q_keep,
    q_recv,
    q_two,
    q_three,
    q_done,
    o_send,
    o_keep,
    o_recv,
    o_two,
    o_three,
    d_three,
    u_three,
    u_done,
    p_send,
    p_recv,
    p_own,
    n_send,
    n_recv,
    n_own,
    sums,
    s_recv,
    s_part,
    s_all,
    local_sem,
    store_sem,
    sends,
    recvs,
):
    place = lax.axis_index("ctx")
    member = lax.axis_index("fsdp")
    shards = back_in.shape[1]
    groups, tops, _, piece, qcols = q_send.shape
    rows, width = p_own.shape
    wide = width // groups
    deep = hidden_in.shape[1]
    x_at, z_at, top_at = place % 2, (place // 2) % 2, place // 4
    near, over, far = {"ctx": place ^ 1}, {"ctx": place ^ 2}, {"ctx": place ^ 4}

    barrier = pltpu.get_barrier_semaphore()
    for j in range(1, groups):
        pl.semaphore_signal(
            barrier, inc=1, device_id={"fsdp": member ^ j}, device_id_type=pl.DeviceIdType.MESH
        )
    for k in range(1, shards):
        pl.semaphore_signal(
            barrier, inc=1, device_id={"ctx": place ^ k}, device_id_type=pl.DeviceIdType.MESH
        )

    def block(at, size):
        return pl.ds(pl.multiple_of(at, size), size)

    names = {}

    def flight(name, src, dst, target):
        at = names.setdefault(name, len(names))
        return remote(src, dst, sends, recvs, at, target)

    def fetch(src, dst, at):
        copy = pltpu.make_async_copy(src, dst, local_sem.at[at])
        copy.start()
        return copy

    def core(j):
        return {"fsdp": member ^ j}

    theirs = block((1 - x_at) * piece, piece)
    mine = block(x_at * piece, piece)

    def d_second():
        return flight("d2", d_in.at[1 - z_at], d_two, over)

    def d_last():
        return flight("d", far_in, d_three, far)

    def u_last():
        return flight("u", u_in.at[:, 1 - top_at], u_three, far)

    def o_first(top):
        return flight(("o1", top), o_send.at[top], o_recv.at[top], over)

    def o_second():
        return flight("o2", o_send.at[:, pl.ds(0, piece)], o_two, near)

    def o_last():
        return flight("o3", o_send.at[0, pl.ds(piece, piece)], o_three, far)

    def q_first(f):
        return flight(("q1", f), q_send.at[f], q_recv.at[f], near)

    def q_second(f):
        return flight(("q2", f), q_send.at[f, :, 0], q_two.at[f], over)

    def q_last(f):
        return flight(("q3", f), q_send.at[f, 0, 1], q_three.at[f], far)

    def q_swap(j):
        return flight(("q4", j), q_done.at[member ^ j], qkv_land.at[member], core(j))

    def u_swap(j):
        return flight(("u4", j), u_done.at[member ^ j], up_land.at[member], core(j))

    def rows_last(name, send, recv):
        return flight((name, 3), send.at[0], recv.at[0], core(1))

    def rows_far(name, send, recv):
        return flight((name, 2), send.at[1], recv.at[1], core(2))

    def rows_near(name, send, recv):
        return flight((name, 1), send.at[2], recv.at[2], core(1))

    def sums_one(j):
        return flight(("s1", j), sums, s_recv.at[j - 1], core(j))

    span = width // shards

    def sums_two(k):
        return flight(
            ("s2", k), s_all.at[:, block((place ^ k) * span, span)], s_part.at[k], {"ctx": place ^ k}
        )

    def sums_three(k):
        mine = block(place * span, span)
        return flight(("s3", k), sums_out.at[:, mine], sums_out.at[:, mine], {"ctx": place ^ k})

    pl.semaphore_wait(barrier, groups - 1 + shards - 1)
    u_last().start()
    d_second().start()

    def phase_a(normed, grads):
        loads = [fetch(normed_in, normed, 0), fetch(grads_in, grads, 1)]
        for item in range(items):
            for owner in range(shards):
                pair, g = owner // slot_groups, owner % slot_groups
                spot = pl.ds((item * slot_groups + g) * rows, rows)
                for kind in range(4):
                    loads.append(
                        fetch(
                            back_in.at[item, owner, kind],
                            big.at[spot, pl.ds(kind * wide + pair * LANES, LANES)],
                            2 + (item * shards + owner) * 4 + kind,
                        )
                    )
        sums[...] = jnp.zeros_like(sums)
        for load in loads:
            load.wait()

        def out_grad(top, low, into):
            at = (top * 2 + low) * LANES
            into[top] = contract_rows(big[:, block(at, LANES)], grads[...]).astype(BF16)

        for top in range(tops):
            out_grad(top, 1 - z_at, o_send)
            o_first(top).start()

        for f in range(groups):

            def one(at, _, f=f):
                top, low = at // 2, at % 2
                value = contract_rows(
                    normed[:, block(f * wide + at * LANES, LANES)], big[:, wide:]
                )
                first, second = value[:piece], value[piece:]
                q_send[f, top, low] = jnp.where(x_at == 0, second, first).astype(BF16)
                q_keep[f, top, low] = jnp.where(x_at == 0, first, second).astype(BF16)
                return 0

            lax.fori_loop(0, 2 * tops, one, 0)
            q_first(f).start()
        for top in range(tops):
            out_grad(top, z_at, o_keep)
        for kind in range(3):
            cols = big[:, (kind + 1) * wide : (kind + 2) * wide].astype(F32)
            sums[2 + kind : 3 + kind, block(member * wide, wide)] = jnp.sum(
                cols, axis=0, keepdims=True
            )

    total = rows * groups
    pl.run_scoped(
        phase_a, pltpu.VMEM((total, width), BF16), pltpu.VMEM((total, width), BF16)
    )

    tile = 256

    def keep_share(pair, at, value, send, own):
        cols = block(at * tile, tile)
        if pair == 1:
            send[1, :, cols] = value[:rows].astype(BF16)
            send[0, :, cols] = value[rows:].astype(BF16)
        else:
            own[:, cols] = value[:rows]
            send[2, :, cols] = value[rows:].astype(BF16)

    def phase_b(hidden, down, outw):
        loads = [
            fetch(hidden_in, hidden, 0),
            fetch(down_in, down, 1),
            fetch(outw_in, outw, 2),
        ]
        for load in loads:
            load.wait()
        for pair in (1, 0):
            spot = pl.ds(pair * 2 * rows, 2 * rows)

            def one(at, _, pair=pair, spot=spot):
                cols = block(at * tile, tile)
                value = matmul(hidden[spot, :], down[:, cols]) + matmul(
                    big[spot, pl.ds(0, wide)], outw[:, cols]
                )
                keep_share(pair, at, value, p_send, p_own)
                return 0

            lax.fori_loop(0, width // tile, one, 0)
            if pair == 1:
                rows_last("p", p_send, p_recv).start()
            else:
                rows_near("p", p_send, p_recv).start()

    pl.run_scoped(
        phase_b,
        pltpu.VMEM(hidden_in.shape, BF16),
        pltpu.VMEM(down_in.shape, BF16),
        pltpu.VMEM(outw_in.shape, BF16),
    )

    def pass_rows(name, send, recv):
        rows_last(name, send, recv).wait_recv()
        send[1] = (send[1].astype(F32) + recv[0].astype(F32)).astype(BF16)
        rows_far(name, send, recv).start()

    pass_rows("p", p_send, p_recv)

    for top in range(tops):
        o_first(top).wait()
    for top in range(tops):
        o_send[top, pl.ds(0, piece)] = (
            o_keep[top, theirs].astype(F32) + o_recv[top, theirs].astype(F32)
        ).astype(BF16)
    o_second().start()

    def q_pass(f):
        q_first(f).wait()
        for top in range(tops):
            q_send[f, top, 0] = (
                q_keep[f, top, 1 - z_at].astype(F32) + q_recv[f, top, 1 - z_at].astype(F32)
            ).astype(BF16)
        q_second(f).start()

    def q_turn(f):
        q_second(f).wait_recv()
        other = 1 - top_at
        q_send[f, 0, 1] = (
            q_keep[f, other, z_at].astype(F32)
            + q_recv[f, other, z_at].astype(F32)
            + q_two[f, other].astype(F32)
        ).astype(BF16)
        q_last(f).start()

    for f in range(groups // 2):
        q_pass(f)
    d_last().start()

    def phase_c(du, wup, wqkv):
        loads = [
            fetch(du_in, du, 0),
            fetch(wup_in, wup, 1),
            fetch(wqkv_in, wqkv, 2),
        ]
        for load in loads:
            load.wait()
        for pair in (1, 0):
            spot = pl.ds(pair * 2 * rows, 2 * rows)

            def one(at, _, pair=pair, spot=spot):
                cols = block(at * tile, tile)
                value = contract_cols(du[spot, :], wup[cols, :]) + contract_cols(
                    big[spot, pl.ds(wide, 3 * wide)], wqkv[cols, :]
                )
                keep_share(pair, at, value, n_send, n_own)
                return 0

            lax.fori_loop(0, width // tile, one, 0)
            if pair == 1:
                rows_last("n", n_send, n_recv).start()
            else:
                rows_near("n", n_send, n_recv).start()
        step = deep // groups

        def column_sums(at, _):
            cols = block(at * step, step)
            value = jnp.sum(du[:, cols].astype(F32), axis=0, keepdims=True)
            for j in range(groups):
                sums[5 + j : 6 + j, cols] = jnp.where(member == j, value, 0.0)
            return 0

        lax.fori_loop(0, groups, column_sums, 0)

    pl.run_scoped(
        phase_c,
        pltpu.VMEM(du_in.shape, BF16),
        pltpu.VMEM(wup_in.shape, BF16),
        pltpu.VMEM(wqkv_in.shape, BF16),
    )
    pass_rows("n", n_send, n_recv)
    for f in range(groups // 2, groups):
        q_pass(f)
    for f in range(groups // 2):
        q_turn(f)
    o_second().wait_recv()
    o_send[0, pl.ds(piece, piece)] = (
        o_keep[1 - top_at, mine].astype(F32)
        + o_recv[1 - top_at, mine].astype(F32)
        + o_two[1 - top_at].astype(F32)
    ).astype(BF16)
    o_last().start()

    def phase_d(x, cot, out, d_own, d_more, d_sum, o_sum, u_more, q_full, u_full):
        loads = [
            fetch(x_in, x, 0),
            fetch(cot_in, cot, 1),
            fetch(u_in.at[:, top_at], u_done, 2),
            fetch(d_in.at[z_at], d_own, 3),
        ]
        for load in loads:
            load.wait()

        for f in range(groups // 2, groups):
            q_turn(f)
        rows_near("n", n_send, n_recv).wait_recv()
        rows_far("n", n_send, n_recv).wait_recv()
        step = 64

        def normal_part(at, _):
            r = block(at * step, step)
            tokens = x[r, :].astype(F32)
            centred = tokens - jnp.mean(tokens, axis=-1, keepdims=True)
            spread = lax.rsqrt(jnp.mean(centred * centred, axis=-1, keepdims=True) + EPS)
            normal = centred * spread
            dn = n_own[r, :] + n_recv[2, r, :].astype(F32) + n_recv[1, r, :].astype(F32)
            sums[0:1, :] = sums[0:1, :] + jnp.sum(dn * normal, axis=0, keepdims=True)
            sums[1:2, :] = sums[1:2, :] + jnp.sum(dn, axis=0, keepdims=True)
            dnorm = dn * gain_ref[...]
            grad = cot[r, :].astype(F32)
            sums[9:10, :] = sums[9:10, :] + jnp.sum(grad, axis=0, keepdims=True)
            change = spread * (
                dnorm
                - jnp.mean(dnorm, axis=-1, keepdims=True)
                - normal * jnp.mean(dnorm * normal, axis=-1, keepdims=True)
            )
            cot[r, :] = (grad + change).astype(BF16)
            return 0

        lax.fori_loop(0, rows // step, normal_part, 0)
        for j in range(1, groups):
            sums_one(j).start()
        own_input = pltpu.make_async_copy(cot, input_out, store_sem.at[1])
        own_input.start()

        rows_near("p", p_send, p_recv).wait_recv()
        rows_far("p", p_send, p_recv).wait_recv()

        def output_part(at, _):
            r = block(at * step, step)
            value = x[r, :].astype(F32) + p_own[r, :] + p_recv[2, r, :].astype(F32)
            value = value + p_recv[1, r, :].astype(F32) + out_bias_ref[...] + down_bias_ref[...]
            out[r, :] = value.astype(BF16)
            return 0

        lax.fori_loop(0, rows // step, output_part, 0)
        own_out = pltpu.make_async_copy(out, result_out, store_sem.at[2])
        own_out.start()

        u_last().wait_recv()
        for f in range(groups):
            u_done[f] = (
                u_done[f].astype(F32) + u_three[f].astype(F32)
            ).astype(BF16)
        for j in range(1, groups):
            u_swap(j).start()
        u_full[:, block(member * deep, deep)] = u_done[member].astype(F32)

        for j in range(1, groups):
            sums_one(j).wait_recv()
        s_all[...] = sums[...] + s_recv[0] + s_recv[1] + s_recv[2]
        for k in range(1, shards):
            sums_two(k).start()
        for f in range(groups):
            q_last(f).wait_recv()
            q_done[f] = (
                q_keep[f, top_at, z_at].astype(F32)
                + q_recv[f, top_at, z_at].astype(F32)
                + q_two[f, top_at].astype(F32)
                + q_three[f].astype(F32)
            ).astype(BF16)
        for j in range(1, groups):
            q_swap(j).start()
        for kind in range(3):
            q_full[:, block(kind * width + member * wide, wide)] = q_done[
                member, :, kind * wide : (kind + 1) * wide
            ].astype(F32)
        o_last().wait_recv()
        o_sum[...] = (
            o_keep[top_at, mine].astype(F32)
            + o_recv[top_at, mine].astype(F32)
            + o_two[top_at].astype(F32)
            + o_three[...].astype(F32)
        )
        own_o = pltpu.make_async_copy(o_sum, o_out, store_sem.at[5])
        own_o.start()
        for k in range(1, shards):
            sums_two(k).wait()
        cols = block(place * span, span)
        value = s_all[:, cols]
        for k in range(1, shards):
            value = value + s_part[k]
        sums_out[:, cols] = value
        for k in range(1, shards):
            sums_three(k).start()

        d_last().wait_recv()
        d_second().wait_recv()
        fetch(d_two, d_more, 4).wait()
        d_sum[...] = d_own[...].astype(F32) + d_more[...].astype(F32) + d_three[...].astype(F32)
        own_down = pltpu.make_async_copy(d_sum, d_out, store_sem.at[3])
        own_down.start()

        for j in range(1, groups):
            u_swap(j).wait_recv()
        for copy in (own_input, own_out):
            copy.wait()
        u_loads = [
            fetch(up_land.at[member ^ j], u_more.at[j], j) for j in range(1, groups)
        ]
        for j in range(1, groups):
            u_loads[j - 1].wait()
            u_full[:, block((member ^ j) * deep, deep)] = u_more[j].astype(F32)
        own_up = pltpu.make_async_copy(u_full, up_out, store_sem.at[0])
        own_up.start()
        for j in range(1, groups):
            q_swap(j).wait_recv()
        q_loads = [
            fetch(qkv_land.at[member ^ j], q_three.at[j], j) for j in range(1, groups)
        ]
        for j in range(1, groups):
            q_loads[j - 1].wait()
            for kind in range(3):
                q_full[:, block(kind * width + (member ^ j) * wide, wide)] = q_three[
                    j, :, kind * wide : (kind + 1) * wide
                ].astype(F32)
        own_q = pltpu.make_async_copy(q_full, qkv_out, store_sem.at[4])
        own_q.start()
        for copy in (own_up, own_down, own_q, own_o):
            copy.wait()

    pl.run_scoped(
        phase_d,
        pltpu.VMEM((rows, width), BF16),
        pltpu.VMEM((rows, width), BF16),
        pltpu.VMEM((rows, width), BF16),
        pltpu.VMEM(d_three.shape, BF16),
        pltpu.VMEM(d_three.shape, BF16),
        pltpu.VMEM(d_three.shape, F32),
        pltpu.VMEM((piece, width), F32),
        pltpu.VMEM(u_done.shape, BF16),
        pltpu.VMEM((piece, 3 * width), F32),
        pltpu.VMEM((piece, groups * deep), F32),
    )
    d_second().wait_send()
    u_last().wait_send()
    d_last().wait_send()
    o_second().wait_send()
    o_last().wait_send()
    for f in range(groups):
        q_second(f).wait_send()
        q_last(f).wait_send()
    for j in range(1, groups):
        q_swap(j).wait_send()
        u_swap(j).wait_send()
        sums_one(j).wait_send()
    for name, send, recv in (("p", p_send, p_recv), ("n", n_send, n_recv)):
        rows_last(name, send, recv).wait_send()
        rows_far(name, send, recv).wait_send()
        rows_near(name, send, recv).wait_send()
    for k in range(1, shards):
        sums_three(k).wait()


def finish(
    back_in, normed, grads, hidden, du, wqkv, wup, outw, down, d_sum, far_sum, u_sum,
    x, cot, gain, out_bias, down_bias, groups, slot_groups,
):
    items, shards = back_in.shape[:2]
    rows, width = x.shape
    wide = width // groups
    deep = hidden.shape[1]
    tops = shards // 4
    piece = wide // shards
    pairs = wide // LANES
    units = deep // shards
    apart = pl.BlockSpec(memory_space=pl.ANY)
    whole = pl.BlockSpec(memory_space=pltpu.VMEM)
    dma = pltpu.SemaphoreType.DMA
    shape = jax.ShapeDtypeStruct
    return pl.pallas_call(
        partial(finish_kernel, items, pairs, slot_groups),
        out_shape=[
            shape((rows, width), BF16),
            shape((rows, width), BF16),
            shape((piece, 3 * width), F32),
            shape((piece, groups * deep), F32),
            shape((piece, width), F32),
            shape((units, width), F32),
            shape((16, width), F32),
            shape((groups, piece, 3 * wide), BF16),
            shape((groups, piece, deep), BF16),
            shape((units, width), BF16),
        ],
        in_specs=[apart] * 14 + [whole] * 3,
        out_specs=[apart] * 6 + [whole] + [apart] * 3,
        scratch_shapes=[
            pltpu.VMEM((rows * groups, 4 * wide), BF16),
            pltpu.VMEM((groups, tops, 2, piece, 3 * wide), BF16),
            pltpu.VMEM((groups, tops, 2, piece, 3 * wide), BF16),
            pltpu.VMEM((groups, tops, 2, piece, 3 * wide), BF16),
            pltpu.VMEM((groups, tops, piece, 3 * wide), BF16),
            pltpu.VMEM((groups, piece, 3 * wide), BF16),
            pltpu.VMEM((groups, piece, 3 * wide), BF16),
            pltpu.VMEM((tops, 2 * piece, width), BF16),
            pltpu.VMEM((tops, 2 * piece, width), BF16),
            pltpu.VMEM((tops, 2 * piece, width), BF16),
            pltpu.VMEM((tops, piece, width), BF16),
            pltpu.VMEM((piece, width), BF16),
            pltpu.VMEM((units, width), BF16),
            pltpu.VMEM((groups, piece, deep), BF16),
            pltpu.VMEM((groups, piece, deep), BF16),
            pltpu.VMEM((3, rows, width), BF16),
            pltpu.VMEM((3, rows, width), BF16),
            pltpu.VMEM((rows, width), F32),
            pltpu.VMEM((3, rows, width), BF16),
            pltpu.VMEM((3, rows, width), BF16),
            pltpu.VMEM((rows, width), F32),
            pltpu.VMEM((16, width), F32),
            pltpu.VMEM((3, 16, width), F32),
            pltpu.VMEM((shards, 16, width // shards), F32),
            pltpu.VMEM((16, width), F32),
            dma((2 + items * shards * 4,)),
            dma((6,)),
            dma((FLIGHTS,)),
            dma((FLIGHTS,)),
        ],
        compiler_params=pltpu.CompilerParams(
            collective_id=2, has_side_effects=True, vmem_limit_bytes=63 * 2**20
        ),
        cost_estimate=pl.CostEstimate(
            flops=2 * rows * groups * width * (2 * deep + 8 * wide),
            bytes_accessed=60 * 2**20,
            transcendentals=0,
        ),
    )(
        back_in, normed, grads, hidden, du, wqkv, wup, outw, down, d_sum, far_sum, u_sum, x, cot,
        gain.reshape(1, width), out_bias.reshape(1, width), down_bias.reshape(1, width),
    )


def deliver_kernel(count, groups, *refs):
    arrays, sums = refs[:count], refs[count]
    outs = refs[count + 1 : 2 * count + 1]
    gain, shift, qkv_bias, out_bias, up_bias, down_bias = refs[2 * count + 1 : 2 * count + 7]
    held = refs[2 * count + 7 : 3 * count + 7]
    sem = refs[-1]
    loads = [
        pltpu.make_async_copy(src, dst, sem.at[at]) for at, (src, dst) in enumerate(zip(arrays, held))
    ]
    copies = [
        pltpu.make_async_copy(src, dst, sem.at[count + at])
        for at, (src, dst) in enumerate(zip(held, outs))
    ]
    for load in loads:
        load.start()
    for load, copy in zip(loads, copies):
        load.wait()
        copy.start()
    width = sums.shape[1]
    gain[...] = sums[0, :]
    shift[...] = sums[1, :]
    out_bias[...] = sums[9, :]
    down_bias[...] = sums[9, :]
    for row in range(3):
        qkv_bias[row * width : (row + 1) * width] = sums[2 + row, :]
    for row in range(groups):
        up_bias[row * width : (row + 1) * width] = sums[5 + row, :]
    for copy in copies:
        copy.wait()


def deliver(arrays, sums, groups):
    width = sums.shape[1]
    apart = pl.BlockSpec(memory_space=pl.ANY)
    whole = pl.BlockSpec(memory_space=pltpu.VMEM)
    flat = [width, width, 3 * width, width, groups * width, width]
    return pl.pallas_call(
        partial(deliver_kernel, len(arrays), groups),
        out_shape=[jax.ShapeDtypeStruct(item.shape, item.dtype) for item in arrays]
        + [jax.ShapeDtypeStruct((size,), F32) for size in flat],
        in_specs=[apart] * len(arrays) + [whole],
        out_specs=[apart] * len(arrays) + [whole] * 6,
        scratch_shapes=[pltpu.VMEM(item.shape, item.dtype) for item in arrays]
        + [pltpu.SemaphoreType.DMA((2 * len(arrays),))],
        compiler_params=pltpu.CompilerParams(vmem_limit_bytes=60 * 2**20),
        cost_estimate=pl.CostEstimate(flops=0, bytes_accessed=20 * 2**20, transcendentals=0),
    )(*arrays, sums)


def scatter_sum(parts, axis_at, place, bits):
    lead, tail = parts.shape[:axis_at], parts.shape[axis_at + 1 :]
    total = len(bits)
    left = list(range(total - 1, -1, -1))
    value = parts.reshape(lead + (2,) * total + tail)
    for bit in bits:
        at = axis_at + left.index(bit)
        left.remove(bit)
        mine = (place >> bit) & 1
        send = lax.dynamic_index_in_dim(value, 1 - mine, at, keepdims=False)
        keep = lax.dynamic_index_in_dim(value, mine, at, keepdims=False)
        got = swap(send.astype(BF16), "ctx", 1 << bit)
        value = keep.astype(F32) + got.astype(F32)
    return value


def scatter_rows(parts):
    last = swap(parts[3].astype(BF16), "fsdp", 1).astype(F32)
    far = swap((parts[2] + last).astype(BF16), "fsdp", 2).astype(F32)
    near = swap(parts[1].astype(BF16), "fsdp", 1).astype(F32)
    return parts[0] + near + far


def total_sum(value):
    for axis in ("fsdp", "ctx"):
        bit = 1
        while bit < lax.axis_size(axis):
            value = value + swap(value, axis, bit)
            bit *= 2
    return value


def on_device(
    inputs,
    norm_gain,
    norm_shift,
    qkv_weight,
    qkv_bias,
    out_weight,
    out_bias,
    up_weight,
    up_bias,
    down_weight,
    down_bias,
    cotangent,
):
    rows = inputs.shape[1]
    width = inputs.shape[2]
    hidden_width = up_weight.shape[1]
    half = rows // 2
    shards = lax.axis_size("ctx")
    groups = lax.axis_size("fsdp")
    place = lax.axis_index("ctx")
    member = lax.axis_index("fsdp")
    wide = width // groups
    deep = hidden_width // groups
    x_first = list(range(shards.bit_length() - 1))
    z_first = x_first[1:2] + x_first[:1] + x_first[2:]

    tokens = inputs[0].astype(F32)
    mean = jnp.mean(tokens, axis=-1, keepdims=True)
    centred = tokens - mean
    inv_scale = lax.rsqrt(jnp.mean(centred * centred, axis=-1, keepdims=True) + EPS)
    normal = centred * inv_scale
    grad_low = cotangent[0]
    grad_full = grad_low.astype(F32)

    pairs = wide // LANES
    heads_in_pair = LANES // HD
    units = pairs * groups
    dup = max(1, shards // units)
    slot_groups = shards // (pairs * dup)
    per_group = groups // slot_groups
    heads = heads_in_pair // dup

    cos_full, sin_full = rotary(shards * rows)
    normed, grads, qkv_own, up_own, hidden, grad_up, qkv_in, grad_in = begin_layer(
        inputs[0],
        norm_gain,
        norm_shift,
        grad_low,
        qkv_weight,
        qkv_bias,
        up_weight,
        up_bias,
        out_weight,
        down_weight,
        cos_full,
        sin_full,
        shards,
        groups,
        pairs,
        slot_groups,
        per_group,
        dup,
    )

    def assembled(back):
        back = back.reshape(pairs, slot_groups, dup, 4, rows, LANES)
        back = jnp.sum(back, axis=2) if dup > 1 else back[:, :, 0]
        return back.transpose(2, 1, 3, 0, 4).reshape(4, slot_groups * rows, wide)

    hw = deep // shards
    if len(x_first) == 3 and dup == 1:
        back_in, down_sum, far_sum, up_sum = middle(
            qkv_in.reshape(per_group, shards, 3, 2, half, LANES),
            grad_in.reshape(shards, per_group, 2, half, LANES),
            hidden,
            normed,
            grads,
            grad_up,
            cos_full,
            sin_full,
            heads,
            groups,
        )
        (
            result,
            input_grad,
            qkv_weight_grad,
            up_weight_grad,
            out_weight_grad,
            down_weight_grad,
            sums,
            *_,
        ) = finish(
            back_in.reshape(per_group, shards, 4, rows, LANES),
            normed,
            grads,
            hidden,
            grad_up,
            qkv_own,
            up_own,
            out_weight,
            down_weight,
            down_sum,
            far_sum,
            up_sum,
            inputs[0],
            grad_low,
            norm_gain,
            out_bias,
            down_bias,
            groups,
            slot_groups,
        )
        (
            result,
            input_grad,
            qkv_weight_grad,
            up_weight_grad,
            out_weight_grad,
            down_weight_grad,
            gain_grad,
            shift_grad,
            qkv_bias_grad,
            out_bias_grad,
            up_bias_grad,
            down_bias_grad,
        ) = deliver(
            (
                result,
                input_grad,
                qkv_weight_grad,
                up_weight_grad,
                out_weight_grad,
                down_weight_grad,
            ),
            sums,
            groups,
        )
        return (
            result[None],
            input_grad[None],
            gain_grad,
            shift_grad,
            qkv_weight_grad,
            qkv_bias_grad,
            out_weight_grad,
            out_bias_grad,
            up_weight_grad,
            up_bias_grad,
            down_weight_grad,
            down_bias_grad,
        )
    else:
        down_grad = contract_rows(hidden, grads).astype(BF16)
        up_grad = contract_rows(normed, grad_up).astype(BF16)
        down_weight_grad = scatter_sum(
            down_grad.reshape(shards, hw, width), 0, place, x_first
        )
        up_part = scatter_sum(
            up_grad.reshape(groups, shards, wide // shards, deep), 1, place, z_first
        )

        backs = []
        for item in range(per_group):
            back = attend(
                qkv_in.reshape(per_group, shards, 3, 2, half, LANES),
                grad_in.reshape(shards, per_group, 2, half, LANES),
                item,
                cos_full,
                sin_full,
                heads,
                dup,
            )
            back = lax.all_to_all(back, "ctx", 0, 0)
            back = back.reshape(pairs, slot_groups, dup, 4, rows, LANES)
            back = jnp.sum(back, axis=2) if dup > 1 else back[:, :, 0]
            backs.append(back.transpose(2, 1, 3, 0, 4).reshape(4, slot_groups * rows, wide))
        back = jnp.concatenate(backs, axis=1)
        attended = back[0]
        grad_qkv = jnp.concatenate([back[1], back[2], back[3]], axis=1)

        share = matmul(hidden, down_weight) + matmul(attended, out_weight)
        result = tokens + scatter_rows(list(share.reshape(groups, rows, width))) + out_bias + down_bias

        grad_share = contract_cols(grad_up, up_own) + contract_cols(grad_qkv, qkv_own)
        grad_normed = scatter_rows(list(grad_share.reshape(groups, rows, width)))
        grad_full = grad_low.astype(F32)
        grad_normal = grad_normed * norm_gain
        grad_tokens = inv_scale * (
            grad_normal
            - jnp.mean(grad_normal, axis=-1, keepdims=True)
            - normal * jnp.mean(grad_normal * normal, axis=-1, keepdims=True)
        )
        input_grad = (grad_full + grad_tokens).astype(BF16)

        qkv_grad = contract_rows(normed, grad_qkv).astype(BF16)
        out_grad = contract_rows(attended, grads).astype(BF16)
        ow = wide // shards
        out_weight_grad = scatter_sum(out_grad.reshape(shards, ow, width), 0, place, z_first)
        qkv_part = scatter_sum(
            qkv_grad.reshape(groups, shards, ow, 3 * wide), 1, place, x_first
        )

        def relative(value):
            return [
                lax.dynamic_index_in_dim(value, member ^ j, 0, keepdims=False) for j in range(groups)
            ]

        def exchange(part):
            sent = relative(part.astype(BF16))
            got = [sent[0]] + [swap(sent[j], "fsdp", j) for j in range(1, groups)]
            return relative(jnp.stack(got))

        up_weight_grad = jnp.concatenate(exchange(up_part), axis=1).astype(F32)
        qkv_weight_grad = jnp.concatenate(
            [item.reshape(ow, 3, 1, wide) for item in exchange(qkv_part)], axis=2
        ).reshape(ow, 3 * width).astype(F32)

        qkv_bias_cols = jnp.sum(grad_qkv.astype(F32), axis=0).reshape(3, 1, wide)
        backs = []
        for item in range(per_group):
            back = attend(
                qkv_in.reshape(per_group, shards, 3, 2, half, LANES),
                grad_in.reshape(shards, per_group, 2, half, LANES),
                item,
                cos_full,
                sin_full,
                heads,
                dup,
            )
            back = lax.all_to_all(back, "ctx", 0, 0)
            backs.append(assembled(back))
    back = jnp.concatenate(backs, axis=1)
    attended = back[0]
    grad_qkv = jnp.concatenate([back[1], back[2], back[3]], axis=1)

    share = matmul(hidden, down_weight) + matmul(attended, out_weight)
    result = tokens + scatter_rows(list(share.reshape(groups, rows, width))) + out_bias + down_bias

    grad_share = contract_cols(grad_up, up_own) + contract_cols(grad_qkv, qkv_own)
    grad_normed = scatter_rows(list(grad_share.reshape(groups, rows, width)))
    grad_full = grad_low.astype(F32)
    grad_normal = grad_normed * norm_gain
    grad_tokens = inv_scale * (
        grad_normal
        - jnp.mean(grad_normal, axis=-1, keepdims=True)
        - normal * jnp.mean(grad_normal * normal, axis=-1, keepdims=True)
    )
    input_grad = (grad_full + grad_tokens).astype(BF16)

    qkv_grad = contract_rows(normed, grad_qkv).astype(BF16)
    out_grad = contract_rows(attended, grads).astype(BF16)
    ow = wide // shards
    out_weight_grad = scatter_sum(out_grad.reshape(shards, ow, width), 0, place, z_first)
    qkv_part = scatter_sum(
        qkv_grad.reshape(groups, shards, ow, 3 * wide), 1, place, x_first
    )

    def relative(value):
        return [
            lax.dynamic_index_in_dim(value, member ^ j, 0, keepdims=False) for j in range(groups)
        ]

    def exchange(part):
        sent = relative(part.astype(BF16))
        got = [sent[0]] + [swap(sent[j], "fsdp", j) for j in range(1, groups)]
        return relative(jnp.stack(got))

    up_weight_grad = jnp.concatenate(exchange(up_part), axis=1).astype(F32)
    qkv_weight_grad = jnp.concatenate(
        [item.reshape(ow, 3, 1, wide) for item in exchange(qkv_part)], axis=2
    ).reshape(ow, 3 * width).astype(F32)

    qkv_bias_cols = jnp.sum(grad_qkv.astype(F32), axis=0).reshape(3, 1, wide)
    up_bias_cols = jnp.sum(grad_up.astype(F32), axis=0).reshape(1, deep)
    qkv_bias_all = lax.dynamic_update_slice(
        jnp.zeros((3, groups, wide), F32), qkv_bias_cols, (0, member, 0)
    ).reshape(-1)
    up_bias_all = lax.dynamic_update_slice(
        jnp.zeros((groups, deep), F32), up_bias_cols, (member, 0)
    ).reshape(-1)
    early = total_sum(jnp.concatenate([jnp.sum(grad_full, axis=0), up_bias_all]))
    late = total_sum(
        jnp.concatenate(
            [jnp.sum(grad_normed * normal, axis=0), jnp.sum(grad_normed, axis=0), qkv_bias_all]
        )
    )
    out_bias_grad, up_bias_grad = early[:width], early[width:]
    gain_grad, shift_grad, qkv_bias_grad = late[:width], late[width : 2 * width], late[2 * width :]
    return (
        result.astype(BF16)[None],
        input_grad[None],
        gain_grad,
        shift_grad,
        qkv_weight_grad,
        qkv_bias_grad,
        out_weight_grad,
        out_bias_grad,
        up_weight_grad,
        up_bias_grad,
        down_weight_grad,
        out_bias_grad,
    )


def solution(mesh):
    in_specs = (
        P("fsdp", "ctx", None),
        P(),
        P(),
        P("fsdp", None),
        P(),
        P("fsdp", None),
        P(),
        P("fsdp", None),
        P(),
        P("fsdp", None),
        P(),
        P("fsdp", "ctx", None),
    )
    out_specs = (
        P("fsdp", "ctx", None),
        P("fsdp", "ctx", None),
        P(),
        P(),
        P(("fsdp", "ctx"), None),
        P(),
        P(("fsdp", "ctx"), None),
        P(),
        P(("fsdp", "ctx"), None),
        P(),
        P(("fsdp", "ctx"), None),
        P(),
    )
    return jax.shard_map(
        on_device, mesh=mesh, in_specs=in_specs, out_specs=out_specs, check_vma=False
    )
```
